32 devices in a mesh: dp: 16 (over z, y, x), mp: 2 (over core).
Axes of the slice: x: 2, y: 2, z: 4, core: 2. Of those that a mesh axis runs over, the one named last changes fastest.
Arguments:
- lang: bfloat16 [512, 20, 768], P(('dp', 'mp')), may hold values from -6 to 6
- vis: bfloat16 [512, 36, 768], P(('dp', 'mp')), may hold values from -6 to 6
- word_mask: int32 [512, 20], P(('dp', 'mp')), may hold values from 0 to 1, as said below
- region_count: int32 [512], P(('dp', 'mp')), may hold values from 10 to 36, as said below
- cot_lang: bfloat16 [512, 20, 768], P(('dp', 'mp')), may hold values from -6 to 6
- cot_vis: bfloat16 [512, 36, 768], P(('dp', 'mp')), may hold values from -6 to 6
- attn_w: float32 [3, 4, 768, 768], P(None, None, 'dp', 'mp'), may hold values from -0.4330127 to 0.4330127
- attn_m: float32 [3, 4, 768, 768], P(None, None, 'dp', 'mp'), may hold values from -0.0010301495 to 0.0010301495
- attn_v: float32 [3, 4, 768, 768], P(None, None, 'dp', 'mp'), may hold values from 0 to 6.75028755e-07
- attn_ema: float32 [3, 4, 768, 768], P(None, None, 'dp', 'mp'), may hold values from -0.4330127 to 0.4330127
- ffn_w: float32 [2, 2, 768, 3072], P(None, None, 'dp', 'mp'), may hold values from -0.14433757 to 0.14433757
- ffn_m: float32 [2, 2, 768, 3072], P(None, None, 'dp', 'mp'), may hold values from -0.00040017346 to 0.00040017346
- ffn_v: float32 [2, 2, 768, 3072], P(None, None, 'dp', 'mp'), may hold values from 0 to 1.09888402e-07
- ffn_ema: float32 [2, 2, 768, 3072], P(None, None, 'dp', 'mp'), may hold values from -0.14433757 to 0.14433757
- gains: float32 [5, 768], P(None, 'dp'), may hold values from 0.35 to 1.9
- gains_m: float32 [5, 768], P(None, 'dp'), may hold values from -0.0048828125 to 0.0048828125
- gains_v: float32 [5, 768], P(None, 'dp'), may hold values from 7.535205e-08 to 3.02978e-07
- gains_ema: float32 [5, 768], P(None, 'dp'), may hold values from 0.5 to 1.5
- biases: float32 [16, 768], P(None, 'dp'), may hold values from -3 to 3
- biases_m: float32 [16, 768], P(None, 'dp'), may hold values from -0.0048828125 to 0.0048828125
- biases_v: float32 [16, 768], P(None, 'dp'), may hold values from 7.535205e-08 to 3.02978e-07
- biases_ema: float32 [16, 768], P(None, 'dp'), may hold values from -3 to 3
- bias_up: float32 [2, 3072], P(None, 'dp'), may hold values from -3 to 3
- bias_up_m: float32 [2, 3072], P(None, 'dp'), may hold values from -0.0014648438 to 0.0014648438
- bias_up_v: float32 [2, 3072], P(None, 'dp'), may hold values from 7.0642545e-09 to 2.8257018e-08
- bias_up_ema: float32 [2, 3072], P(None, 'dp'), may hold values from -3 to 3
Outputs:
- out_lang: float32 [512, 20, 768], P(('dp', 'mp'))
- out_vis: float32 [512, 36, 768], P(('dp', 'mp'))
- grad_lang: float32 [512, 20, 768], P(('dp', 'mp'))
- grad_vis: float32 [512, 36, 768], P(('dp', 'mp'))
- grad_norm: float32 [], replicated
- attn_w_new: float32 [3, 4, 768, 768], P(None, None, 'dp', 'mp')
- attn_m_new: float32 [3, 4, 768, 768], P(None, None, 'dp', 'mp')
- attn_v_new: float32 [3, 4, 768, 768], P(None, None, 'dp', 'mp')
- attn_ema_new: float32 [3, 4, 768, 768], P(None, None, 'dp', 'mp')
- ffn_w_new: float32 [2, 2, 768, 3072], P(None, None, 'dp', 'mp')
- ffn_m_new: float32 [2, 2, 768, 3072], P(None, None, 'dp', 'mp')
- ffn_v_new: float32 [2, 2, 768, 3072], P(None, None, 'dp', 'mp')
- ffn_ema_new: float32 [2, 2, 768, 3072], P(None, None, 'dp', 'mp')
- gains_new: float32 [5, 768], P(None, 'dp')
- gains_m_new: float32 [5, 768], P(None, 'dp')
- gains_v_new: float32 [5, 768], P(None, 'dp')
- gains_ema_new: float32 [5, 768], P(None, 'dp')
- biases_new: float32 [16, 768], P(None, 'dp')
- biases_m_new: float32 [16, 768], P(None, 'dp')
- biases_v_new: float32 [16, 768], P(None, 'dp')
- biases_ema_new: float32 [16, 768], P(None, 'dp')
- bias_up_new: float32 [2, 3072], P(None, 'dp')
- bias_up_m_new: float32 [2, 3072], P(None, 'dp')
- bias_up_v_new: float32 [2, 3072], P(None, 'dp')
- bias_up_ema_new: float32 [2, 3072], P(None, 'dp')
The draws below stay inside these ranges and needn't reach their ends.
Inputs may be any that keep to these rules, and one draw needn't show every extreme that they name: `word_mask`: each row is 1 on its first l positions and 0 after them, with l from 6 to 20; some row has l = 20 and some l = 6. `region_count`: some item has 36 regions and some 10.
All inputs are finite; a program needn't handle non-finite values.
Results may differ from the reference program's by a relative error of at most 0.019.
The reference program's roundings to bfloat16 on the way count: a program that leaves them out, or rounds other values in their place, can miss the bound.
Values may be sent and summed in bfloat16 or wider, within the bound.
No kernel may reach another device: no remote copies, remote signals or barrier semaphores. Data moves between devices by JAX's collectives and lax.ppermute only.
A program may use at most 256 MiB of HBM per device.

```python
import math
import jax
import jax.numpy as jnp
from jax import lax

D = 768
HEADS = 12
FF = 3072
HEAD_DIM = 64
WORDS = 20
REGIONS = 36
STEP = 7
ITEMS = 512


def rough_normal(key, shape):
    return jnp.clip(jax.random.normal(key, shape, jnp.float32), -4.0, 4.0)


def grad_scale():
    return 1.0 / math.sqrt(8.0 * D * D + 0.7 * D * FF)


def attn_spread():
    return jnp.array([1.4, 1.4, 1.0, 3.0], jnp.float32)[None, :, None, None] / math.sqrt(D)


def ffn_spread():
    return jnp.array([1.0 / math.sqrt(D), 1.0 / math.sqrt(FF)], jnp.float32)[None, :, None, None]


def attn_magnitude():
    per_kind = jnp.array([0.85, 0.85, 0.9, 0.3], jnp.float32)[None, :, None, None]
    per_layer = jnp.array([1.4, 1.0, 1.0], jnp.float32)[:, None, None, None]
    return per_kind * per_layer * grad_scale()


def ffn_magnitude():
    return jnp.array([0.26, 0.5], jnp.float32)[None, :, None, None] * grad_scale()


def signed_moment(key, magnitude, shape):
    sign_key, size_key = jax.random.split(key)
    sign_values = jnp.where(jax.random.bernoulli(sign_key, 0.5, shape), 1.0, -1.0)
    spread = jnp.exp(jax.random.uniform(size_key, shape, jnp.float32, math.log(0.5), math.log(2.0)))
    return sign_values * spread * magnitude


def square_moment(key, magnitude, shape):
    spread = jnp.exp(jax.random.uniform(key, shape, jnp.float32, 0.0, math.log(4.0)))
    return spread * (0.4 / 0.6) * magnitude * magnitude


def draw_attn_w(key, part):
    return rough_normal(key, (3, 4, D, D)) * attn_spread()


def draw_attn_ema(key, part):
    return rough_normal(jax.random.fold_in(key, 7101), (3, 4, D, D)) * attn_spread()


def draw_attn_m(key, part):
    return signed_moment(key, attn_magnitude(), (3, 4, D, D))


def draw_attn_v(key, part):
    return square_moment(key, attn_magnitude(), (3, 4, D, D))


def draw_ffn_w(key, part):
    return rough_normal(key, (2, 2, D, FF)) * ffn_spread()


def draw_ffn_ema(key, part):
    return rough_normal(jax.random.fold_in(key, 7102), (2, 2, D, FF)) * ffn_spread()


def draw_ffn_m(key, part):
    return signed_moment(key, ffn_magnitude(), (2, 2, D, FF))


def draw_ffn_v(key, part):
    return square_moment(key, ffn_magnitude(), (2, 2, D, FF))


def draw_gains(key, part):
    position = jnp.arange(D).astype(jnp.float32) / (D - 1)
    ramp = 0.5 + position
    factor = jnp.exp(jax.random.uniform(key, (5, D), jnp.float32, math.log(0.85), math.log(1.15)))
    return factor * ramp[None, :]


def draw_word_mask(key, part):
    length = jax.random.randint(key, (ITEMS,), 6, WORDS + 1)
    length = length.at[0].set(WORDS).at[1].set(6)
    return (jnp.arange(WORDS)[None, :] < length[:, None]).astype(jnp.int32)


def draw_region_count(key, part):
    former, latter = jax.random.split(key)
    base_one = jax.random.randint(former, (ITEMS,), 0, REGIONS - 9)
    base_two = jax.random.randint(latter, (ITEMS,), 8, REGIONS - 9)
    counts = 10 + base_one * base_two // (REGIONS - 10)
    return counts.at[0].set(REGIONS).at[1].set(10).astype(jnp.int32)


def block_levels(stream_key, shape, pieces, low, high):
    def one(dim, shards_of):
        steps = jax.random.uniform(jax.random.fold_in(jax.random.fold_in(stream_key, 6), dim), (shards_of,), jnp.float32, low / len(pieces), high / len(pieces))
        return jnp.repeat(jnp.exp(steps), shape[dim] // shards_of).reshape((-1,) + (1,) * (len(shape) - dim - 1))

    level = one(*pieces[0])
    for cut in pieces[1:]:
        level = level * one(*cut)
    return level


def gaussian(own_key, shape, deviation, bound, shards=(), kind=jnp.bfloat16):
    result = jax.random.normal(own_key, shape, jnp.float32) * deviation
    if len(shards) > 0:
        result = block_levels(own_key, shape, shards, -0.22, 0.18) * result
    return jnp.clip(result, min=-bound, max=bound).astype(kind)


def setup_inputs(seed: int = 0) -> dict:
    arg_keys = jax.random.split(jax.random.key(seed), 27)
    lang = gaussian(arg_keys[0], (ITEMS, WORDS, D), 1.0, 6.0, ((0, 32),))
    vis = gaussian(arg_keys[1], (ITEMS, REGIONS, D), 1.0, 6.0, ((0, 32),))
    word_mask = draw_word_mask(jax.random.fold_in(arg_keys[26], 71), 0)
    region_count = draw_region_count(jax.random.fold_in(arg_keys[26], 71), 0)
    cot_lang = gaussian(arg_keys[4], (ITEMS, WORDS, D), 1.0, 6.0, ((0, 32),))
    cot_vis = gaussian(arg_keys[5], (ITEMS, REGIONS, D), 1.0, 6.0, ((0, 32),))
    attn_w = draw_attn_w(jax.random.fold_in(arg_keys[26], 71), 0)
    attn_m = draw_attn_m(jax.random.fold_in(arg_keys[26], 71), 0)
    attn_v = draw_attn_v(jax.random.fold_in(arg_keys[26], 71), 0)
    attn_ema = draw_attn_ema(jax.random.fold_in(arg_keys[26], 71), 0)
    ffn_w = draw_ffn_w(jax.random.fold_in(arg_keys[26], 71), 0)
    ffn_m = draw_ffn_m(jax.random.fold_in(arg_keys[26], 71), 0)
    ffn_v = draw_ffn_v(jax.random.fold_in(arg_keys[26], 71), 0)
    ffn_ema = draw_ffn_ema(jax.random.fold_in(arg_keys[26], 71), 0)
    gains = draw_gains(jax.random.fold_in(arg_keys[26], 71), 0)
    gains_m = gaussian(arg_keys[15], (5, D), (0.85 / (8 * D * D + 7 * D * FF // 10) ** 0.5), 0.0048828125, ((1, 16),), jnp.float32)
    gains_v = jnp.clip(jnp.exp(math.log(3.029780089036649e-07) - 1.3914891 * jax.random.uniform(arg_keys[16], (5, D), jnp.float32) ** block_levels(arg_keys[16], (5, D), ((1, 16),), -0.2, 0.2)), 7.535204815667385e-08, 3.029780089036649e-07)
    gains_ema = jnp.clip(1.0 + 0.1 * jax.random.normal(arg_keys[17], (5, D), jnp.float32), 0.5, 1.5)
    biases = gaussian(arg_keys[18], (16, D), 0.2, 3.0, ((1, 16),), jnp.float32)
    biases_m = gaussian(arg_keys[19], (16, D), (0.85 / (8 * D * D + 7 * D * FF // 10) ** 0.5), 0.0048828125, ((1, 16),), jnp.float32)
    biases_v = jnp.clip(jnp.exp(math.log(3.029780089036649e-07) - 1.3914891 * jax.random.uniform(arg_keys[20], (16, D), jnp.float32) ** block_levels(arg_keys[20], (16, D), ((1, 16),), -0.2, 0.2)), 7.535204815667385e-08, 3.029780089036649e-07)
    biases_ema = gaussian(arg_keys[21], (16, D), 0.2, 3.0, ((1, 16),), jnp.float32)
    bias_up = gaussian(arg_keys[22], (2, FF), 0.2, 3.0, ((1, 16),), jnp.float32)
    bias_up_m = gaussian(arg_keys[23], (2, FF), (0.26 / (8 * D * D + 7 * D * FF // 10) ** 0.5), 0.0014648438, ((1, 16),), jnp.float32)
    bias_up_v = jnp.clip(jnp.exp(math.log(2.8257018058752692e-08) - 1.3862944 * jax.random.uniform(arg_keys[24], (2, FF), jnp.float32) ** block_levels(arg_keys[24], (2, FF), ((1, 16),), -0.2, 0.2)), 7.064254514688173e-09, 2.8257018058752692e-08)
    bias_up_ema = gaussian(arg_keys[25], (2, FF), 0.2, 3.0, ((1, 16),), jnp.float32)
    return {"lang": lang, "vis": vis, "word_mask": word_mask, "region_count": region_count, "cot_lang": cot_lang, "cot_vis": cot_vis, "attn_w": attn_w, "attn_m": attn_m, "attn_v": attn_v, "attn_ema": attn_ema, "ffn_w": ffn_w, "ffn_m": ffn_m, "ffn_v": ffn_v, "ffn_ema": ffn_ema, "gains": gains, "gains_m": gains_m, "gains_v": gains_v, "gains_ema": gains_ema, "biases": biases, "biases_m": biases_m, "biases_v": biases_v, "biases_ema": biases_ema, "bias_up": bias_up, "bias_up_m": bias_up_m, "bias_up_v": bias_up_v, "bias_up_ema": bias_up_ema}


@jax.custom_vjp
def low(v):
    return lax.optimization_barrier(v.astype(jnp.bfloat16)).astype(jnp.float32)

@jax.custom_vjp
def low_back(v):
    return v

def low_keep(v):
    return (low(v), None)

def low_pass(kept, grad):
    return (grad,)

def back_keep(v):
    return (v, None)

def back_low(kept, grad):
    return (low(grad),)
low.defvjp(low_keep, low_pass)
low_back.defvjp(back_keep, back_low)
highest = lax.Precision.HIGHEST
norm_eps = 1e-12
mask_fill = -1000000000.0
beta_one = 0.5
beta_two = 0.6
ema_decay = 0.5
adam_eps = 1e-08
weight_decay = 0.01
rate_mats = 0.02
rate_small = 0.2
clip_norm = 1.0

def layer_norm(summed, gain, shift):
    average = lax.optimization_barrier(jnp.mean(summed, axis=-1, keepdims=True))
    centered = summed - average
    inverse = lax.rsqrt(lax.optimization_barrier(jnp.mean(centered * centered, axis=-1, keepdims=True)) + norm_eps)
    return centered * inverse * gain + shift

def split_heads(values):
    return values.reshape(values.shape[0], values.shape[1], HEADS, HEAD_DIM)

def attend(query_in, context_in, key_live, matrices, bias_query, bias_value, bias_out):
    queries = low_back(low(jnp.einsum('bnd,dk->bnk', query_in, matrices[0], precision=highest) + bias_query))
    keys = low_back(low(jnp.einsum('bnd,dk->bnk', context_in, matrices[1], precision=highest)))
    values = low_back(low(jnp.einsum('bnd,dk->bnk', context_in, matrices[2], precision=highest) + bias_value))
    scores = jnp.einsum('bnhe,bmhe->bhnm', split_heads(queries), split_heads(keys), precision=highest) * HEAD_DIM ** (-0.5)
    scores = low_back(scores + mask_fill * (1.0 - key_live)[:, None, None, :])
    weights = low(jax.nn.softmax(scores, axis=-1))
    context = jnp.einsum('bhnm,bmhe->bnhe', weights, split_heads(values), precision=highest)
    context = low_back(low(context.reshape(queries.shape)))
    return low_back(jnp.einsum('bnk,dk->bnd', context, matrices[3], precision=highest) + bias_out)

def feed(rows_in, matrices, bias_hidden, bias_out):
    hidden = low_back(jnp.einsum('bnd,df->bnf', rows_in, matrices[0], precision=highest) + bias_hidden)
    active = low(jax.nn.gelu(hidden, approximate=False))
    return low_back(jnp.einsum('bnf,df->bnd', active, matrices[1], precision=highest) + bias_out)

def forward(params, lang, vis, word_live, region_live):
    attn_w, ffn_w, gains, biases, bias_up = params
    matrices = low(attn_w)
    ffn_mats = low(ffn_w)
    inputs = [lang, vis]
    live_masks = [word_live, region_live]
    lowered = [low(lang), low(vis)]
    first = []
    for stream in range(2):
        branch = attend(lowered[stream], lowered[1 - stream], live_masks[1 - stream], matrices[0], biases[0], biases[1], biases[2])
        first.append(layer_norm(inputs[stream] + branch, gains[0], biases[11]))
    second = []
    for stream in range(2):
        rows_low = low(first[stream])
        branch = attend(rows_low, rows_low, live_masks[stream], matrices[1 + stream], biases[3 + 3 * stream], biases[4 + 3 * stream], biases[5 + 3 * stream])
        second.append(layer_norm(first[stream] + branch, gains[1 + stream], biases[12 + stream]))
    outputs = []
    for stream in range(2):
        branch = feed(low(second[stream]), ffn_mats[stream], bias_up[stream], biases[9 + stream])
        normed = layer_norm(second[stream] + branch, gains[3 + stream], biases[14 + stream])
        outputs.append(normed * live_masks[stream][..., None])
    return (outputs[0], outputs[1])

def adam_update(weight, moment_one, moment_two, average, grad, clip, rate):
    clipped = grad * clip
    new_one = beta_one * moment_one + (1.0 - beta_one) * clipped
    new_two = beta_two * moment_two + (1.0 - beta_two) * clipped * clipped
    direction = new_one / (1.0 - beta_one ** STEP) / (jnp.sqrt(new_two / (1.0 - beta_two ** STEP)) + adam_eps)
    new_weight = weight - rate * (direction + weight_decay * weight)
    new_average = ema_decay * average + (1.0 - ema_decay) * new_weight
    return (new_weight, new_one, new_two, new_average)

def reference(lang, vis, word_mask, region_count, cot_lang, cot_vis, attn_w, attn_m, attn_v, attn_ema, ffn_w, ffn_m, ffn_v, ffn_ema, gains, gains_m, gains_v, gains_ema, biases, biases_m, biases_v, biases_ema, bias_up, bias_up_m, bias_up_v, bias_up_ema):
    word_live = word_mask.astype(jnp.float32)
    region_live = (jnp.arange(REGIONS)[None, :] < region_count[:, None]).astype(jnp.float32)
    params = (attn_w, ffn_w, gains, biases, bias_up)
    blocks = ITEMS // 32

    def split(array):
        return array.astype(jnp.float32).reshape((blocks, 32) + array.shape[1:])
    stacked = (split(lang), split(vis), split(word_live), split(region_live), split(cot_lang), split(cot_vis))
    zeros = jax.tree.map(jnp.zeros_like, params)

    def one_block(totals, block):
        lang_block, vis_block, word_block, region_block, cot_words, cot_regions = block

        def run(weights, lang_rows, vis_rows):
            return forward(weights, lang_rows, vis_rows, word_block, region_block)
        outputs, pullback = jax.vjp(run, params, lang_block, vis_block)
        grad_params, grad_words, grad_regions = pullback((cot_words, cot_regions))
        totals = jax.tree.map(lambda left, right: left + right, totals, grad_params)
        return (totals, (outputs[0], outputs[1], grad_words, grad_regions))
    grads, results = lax.scan(one_block, zeros, stacked)
    out_lang = results[0].reshape(ITEMS, WORDS, D)
    out_vis = results[1].reshape(ITEMS, REGIONS, D)
    grad_lang = results[2].reshape(ITEMS, WORDS, D)
    grad_vis = results[3].reshape(ITEMS, REGIONS, D)
    squares = jnp.float32(0.0)
    for grad in grads:
        squares = squares + jnp.sum(grad * grad)
    grad_norm = jnp.sqrt(squares)
    clip = jnp.minimum(1.0, clip_norm / (grad_norm + 1e-06))
    attn_new = adam_update(attn_w, attn_m, attn_v, attn_ema, grads[0], clip, rate_mats)
    ffn_new = adam_update(ffn_w, ffn_m, ffn_v, ffn_ema, grads[1], clip, rate_mats)
    gains_new = adam_update(gains, gains_m, gains_v, gains_ema, grads[2], clip, rate_small)
    biases_new = adam_update(biases, biases_m, biases_v, biases_ema, grads[3], clip, rate_small)
    up_new = adam_update(bias_up, bias_up_m, bias_up_v, bias_up_ema, grads[4], clip, rate_small)
    return (out_lang, out_vis, grad_lang, grad_vis, grad_norm, attn_new[0], attn_new[1], attn_new[2], attn_new[3], ffn_new[0], ffn_new[1], ffn_new[2], ffn_new[3], gains_new[0], gains_new[1], gains_new[2], gains_new[3], biases_new[0], biases_new[1], biases_new[2], biases_new[3], up_new[0], up_new[1], up_new[2], up_new[3])
```

```python
import functools
import math
import jax
import jax.numpy as jnp
from jax import lax
from jax.experimental import pallas as pl
from jax.experimental.pallas import tpu as pltpu
from jax.sharding import PartitionSpec as P

HEAD_DIM = 64
STEP = 7


norm_eps = 1e-12
mask_fill = -1000000000.0
beta_one = 0.5
beta_two = 0.6
ema_decay = 0.5
adam_eps = 1e-08
weight_decay = 0.01
rate_mats = 0.02
rate_small = 0.2
clip_norm = 1.0

GROUP = 4
low = jnp.bfloat16
LINE = 4
CHIPS = 16
PAIR = 2 * HEAD_DIM
TILE = 256
CHUNK = 32
FEED = 512
FEED_ROWS = 64
SQRT_HALF = 0.5**0.5
BELL = (2.0 * math.pi) ** -0.5


def moves(target):
    pairs = []
    for z in range(LINE):
        for y in range(2):
            for x in range(2):
                there = target(z, y, x)
                pairs.append((z * 4 + y * 2 + x, there[0] * 4 + there[1] * 2 + there[2]))
    return pairs


routes = {
    1: moves(lambda z, y, x: (z, y, 1 - x)),
    2: moves(lambda z, y, x: (z, 1 - y, x)),
    4: moves(lambda z, y, x: (z ^ 1, y, x)),
    8: moves(lambda z, y, x: (z ^ 2, y, x)),
}


def send(values, bit):
    return lax.ppermute(values, "dp", routes[bit])


def swap_cores(values):
    return lax.ppermute(values, "mp", [(0, 1), (1, 0)])


def widen(values):
    return values.astype(jnp.float32)


def pick(values, axis, index):
    return lax.dynamic_index_in_dim(values, index, axis, keepdims=False)


def bit_of(bit):
    return (lax.axis_index("dp") // bit) % 2


def after(values, *others):
    return lax.optimization_barrier((values,) + others)[0]


def assemble_kernel(places, spans, place_ref, *refs):
    pieces, wholes, sem = refs[: len(places)], refs[len(places) : -1], refs[-1]
    chip, core = place_ref[0], place_ref[1]
    rows, columns = pieces[0].shape[2], pieces[0].shape[3]
    copies = []
    for piece, (offsets, other) in zip(pieces, places):
        for number, offset in enumerate(offsets):
            row = pl.ds(pl.multiple_of((chip ^ offset) * rows, 16), rows)
            column = pl.ds(pl.multiple_of((core ^ other) * columns, 128), columns)
            for whole, (start, count) in zip(wholes, spans):
                copies.append(
                    pltpu.make_async_copy(
                        piece.at[number, pl.ds(start, count)], whole.at[:, row, column], sem
                    )
                )
    for copy in copies:
        copy.start()
    for copy in copies:
        copy.wait()


def assemble(pieces, places, spans):
    _, _, rows, columns = pieces[0].shape
    place = jnp.stack([lax.axis_index("dp"), lax.axis_index("mp")]).astype(jnp.int32)
    return pl.pallas_call(
        functools.partial(assemble_kernel, places, spans),
        out_shape=[shape_of((count, rows * CHIPS, columns * 2), low) for _, count in spans],
        in_specs=[pl.BlockSpec(memory_space=pltpu.SMEM)]
        + [pl.BlockSpec(memory_space=pl.ANY)] * len(pieces),
        out_specs=vmem(len(spans)),
        scratch_shapes=[pltpu.SemaphoreType.DMA],
        compiler_params=params_of(24),
        cost_estimate=cost_of(3),
        name="assemble",
    )(place, *pieces)


def gather_mats(own, order, spans):
    if lax.axis_size("dp") != CHIPS:
        whole = lax.all_gather(own, "dp", axis=1, tiled=True)
        whole = lax.all_gather(whole, "mp", axis=2, tiled=True)
        return [whole[start : start + count] for start, count in spans]
    values, offsets = own[None], [0]
    for bit in order[:-1]:
        values = jnp.concatenate([values, send(values, bit)])
        offsets = offsets + [offset ^ bit for offset in offsets]
    last = send(values, order[-1])
    far = [offset ^ order[-1] for offset in offsets]
    pieces = [values, swap_cores(values), last, swap_cores(last)]
    places = [(offsets, 0), (offsets, 1), (far, 0), (far, 1)]
    return assemble(pieces, places, spans)


class Scatter:
    def __init__(self, mine, other, order):
        self.staged = lax.axis_size("dp") == CHIPS
        self.parts = widen(mine) + widen(swap_cores(other))
        self.order = list(order)
        self.left = [8, 4, 2, 1]
        if self.staged:
            count, width, columns = self.parts.shape
            self.parts = self.parts.astype(low)
            self.parts = self.parts.reshape(count, 2, 2, 2, 2, width // CHIPS, columns)

    def step(self, times=1):
        for _ in range(times if self.staged else 0):
            bit = self.order.pop(0)
            axis = 1 + self.left.index(bit)
            self.left.remove(bit)
            kept = pick(self.parts, axis, bit_of(bit))
            arrived = send(pick(self.parts, axis, 1 - bit_of(bit)), bit)
            self.parts = widen(kept) + widen(arrived)
            if self.left:
                self.parts = self.parts.astype(low)
        return self.parts

    def finish(self):
        if self.staged:
            return self.step(len(self.order))
        return lax.psum_scatter(self.parts, "dp", scatter_dimension=1, tiled=True)


def gather_small(values):
    if lax.axis_size("dp") != CHIPS:
        return lax.all_gather(values, "dp", axis=0, tiled=False)
    values = values[None]
    for bit in (1, 2, 4, 8):
        there = send(values, bit)
        at_zero = bit_of(bit) == 0
        values = jnp.concatenate(
            [jnp.where(at_zero, values, there), jnp.where(at_zero, there, values)]
        )
    return values


def scatter_small(values):
    values = values + swap_cores(values)
    if lax.axis_size("dp") != CHIPS:
        return lax.psum_scatter(values, "dp", scatter_dimension=0, tiled=True)[0]
    for bit in (8, 4, 2, 1):
        half = values.shape[0] // 2
        at_zero = bit_of(bit) == 0
        kept = jnp.where(at_zero, values[:half], values[half:])
        sent = jnp.where(at_zero, values[half:], values[:half])
        values = kept + send(sent, bit)
    return values[0]


def sum_all(value):
    if lax.axis_size("dp") != CHIPS:
        return lax.psum(value, ("dp", "mp"))
    value = value.reshape(1, 1)
    value = value + swap_cores(value)
    for bit in (1, 2, 4, 8):
        value = value + send(value, bit)
    return value[0, 0]


def dot_nn(left, right):
    return lax.dot_general(left, right, (((1,), (0,)), ((), ())), preferred_element_type=jnp.float32)


def dot_nt(left, right):
    return lax.dot_general(left, right, (((1,), (1,)), ((), ())), preferred_element_type=jnp.float32)


def dot_tn(left, right):
    return lax.dot_general(left, right, (((0,), (0,)), ((), ())), preferred_element_type=jnp.float32)


def fold_rows(values):
    return jnp.sum(values.reshape(values.shape[0] // 8, 8, values.shape[1]), axis=0)


def close_rows(values):
    return jnp.sum(values, axis=0, keepdims=True)


def norm_rows(summed, gain, shift):
    average = jnp.mean(summed, axis=-1, keepdims=True)
    centered = summed - average
    inverse = lax.rsqrt(jnp.mean(centered * centered, axis=-1, keepdims=True) + norm_eps)
    normed = centered * inverse
    return normed * gain + shift, normed, inverse


def norm_rows_back(grad_out, normed, inverse, gain):
    scaled = grad_out * gain
    return inverse * (
        scaled
        - jnp.mean(scaled, axis=-1, keepdims=True)
        - normed * jnp.mean(scaled * normed, axis=-1, keepdims=True)
    )


def stack_heads(block):
    first = lax.broadcasted_iota(jnp.int32, block.shape, 1) < HEAD_DIM
    nothing = jnp.zeros_like(block)
    return jnp.concatenate(
        [jnp.where(first, block, nothing), jnp.where(first, nothing, block)], axis=0
    )


def merge_heads(double):
    rows = double.shape[0] // 2
    first = lax.broadcasted_iota(jnp.int32, (rows, double.shape[1]), 1) < HEAD_DIM
    return jnp.where(first, double[:rows], double[rows:])


def pair_forward(queries, keys, values, bias):
    count = keys.shape[0]
    scores = dot_nt(stack_heads(keys), queries) * HEAD_DIM ** (-0.5)
    weights, totals = [], []
    for part in (scores[:count] + bias, scores[count:] + bias):
        top = jnp.max(part, axis=0, keepdims=True)
        powers = jnp.exp(part - top)
        total = jnp.sum(powers, axis=0, keepdims=True)
        weights.append((powers * (1.0 / total)).astype(low))
        totals.append(top + jnp.log(total))
    context = dot_tn(jnp.concatenate(weights, axis=0), stack_heads(values))
    return context.astype(low), totals


def pair_backward(queries, keys, values, grad, bias, totals):
    count = keys.shape[0]
    both_keys = stack_heads(keys)
    scores = dot_nt(both_keys, queries) * HEAD_DIM ** (-0.5)
    sensed = dot_nt(stack_heads(values), grad)
    weights, slopes = [], []
    for part, sense, total in (
        (scores[:count], sensed[:count], totals[0]),
        (scores[count:], sensed[count:], totals[1]),
    ):
        weight = jnp.exp(part + bias - total)
        inner = jnp.sum(sense * weight, axis=0, keepdims=True)
        weights.append(weight.astype(low))
        slopes.append((weight * (sense - inner)).astype(low))
    weights = jnp.concatenate(weights, axis=0)
    slopes = jnp.concatenate(slopes, axis=0)
    grad_queries = (dot_tn(slopes, both_keys) * HEAD_DIM ** (-0.5)).astype(low)
    grad_keys = (merge_heads(dot_nn(slopes, queries)) * HEAD_DIM ** (-0.5)).astype(low)
    grad_values = merge_heads(dot_nn(weights, grad)).astype(low)
    return grad_queries, grad_keys, grad_values


def tiles_of(width):
    return [(at, min(TILE, width - at)) for at in range(0, width, TILE)]


def row_block(start, size, step):
    return pl.ds(pl.multiple_of(start + step * size, 16), size)


def attend_front(plan, *refs):
    streams, relations, cross = plan["streams"], plan["relations"], plan["cross"]
    refs = list(refs)

    def take(count):
        taken = refs[:count]
        del refs[:count]
        return taken

    (x_ref,) = take(1)
    before = [] if cross else take(1)
    mats = take(plan["mats"])
    gain_ref, bias_ref, key_ref = take(3)
    same = take(len(relations))
    q_ref, k_ref, v_ref, ctx_ref = take(4)
    logs = take(len(relations))
    normed = take(len(streams))
    inverse = take(len(streams))
    lowered = take(len(streams))
    (acc_ref,) = take(1)
    width = x_ref.shape[1]
    weights = [mats[i // (4 // len(mats))].at[i % (4 // len(mats))] for i in range(4)]
    rows = x_ref[...]
    for target, weight, row in ((q_ref, 0, 0), (k_ref, 1, None), (v_ref, 2, 1)):
        for at, size in tiles_of(width):
            part = dot_nn(rows, weights[weight][:, at : at + size])
            if row is not None:
                line = plan["rows"][row]
                part = part + bias_ref[line : line + 1, at : at + size]
            target[:, at : at + size] = part.astype(low)
    pairs = width // PAIR
    groups = plan["groups"]

    def one_group(group, carry):
        for which, (asking, asked) in enumerate(relations):
            ask = row_block(*streams[asking], group)
            key = row_block(*streams[asked], group)
            bias = same[which][...] + key_ref[key, :]
            for pair in range(pairs):
                lanes = slice(pair * PAIR, (pair + 1) * PAIR)
                context, totals = pair_forward(
                    q_ref[ask, lanes], k_ref[key, lanes], v_ref[key, lanes], bias
                )
                ctx_ref[ask, lanes] = context
                for side in range(2):
                    logs[which][group * (2 * pairs) + 2 * pair + side] = totals[side]
        return carry

    lax.fori_loop(0, groups, one_group, 0)
    context = ctx_ref[...]
    for at, size in tiles_of(width):
        acc_ref[:, at : at + size] = dot_nt(context, weights[3][at : at + size, :])
    gain = gain_ref[plan["gain"] : plan["gain"] + 1, :]
    shift = bias_ref[plan["shift"] : plan["shift"] + 1, :]
    out_bias = bias_ref[plan["rows"][2] : plan["rows"][2] + 1, :]
    for index, (start, size) in enumerate(streams):

        def one_chunk(step, carry, start=start, index=index):
            here = row_block(start, CHUNK, step)
            there = row_block(0, CHUNK, step)
            if cross:
                base = widen(x_ref[here, :])
            else:
                last_gain, last_shift = plan["before"]
                base = (
                    before[0][here, :] * gain_ref[last_gain : last_gain + 1, :]
                    + bias_ref[last_shift : last_shift + 1, :]
                )
            value, unit, scale = norm_rows(base + acc_ref[here, :] + out_bias, gain, shift)
            normed[index][there, :] = unit
            inverse[index][there, :] = scale
            lowered[index][there, :] = value.astype(low)
            return carry

        lax.fori_loop(0, size * groups // CHUNK, one_chunk, 0)


def attend_back(plan, *refs):
    streams, relations = plan["streams"], plan["relations"]
    refs = list(refs)

    def take(count):
        taken = refs[:count]
        del refs[:count]
        return taken

    (core_ref,) = take(1)
    carried = [take(plan["carried"]) for _ in streams]
    normed = take(len(streams))
    inverse = take(len(streams))
    (x_ref,) = take(1)
    mats = take(plan["mats"])
    gain_ref, key_ref = take(2)
    same = take(len(relations))
    q_ref, k_ref, v_ref, ctx_ref = take(4)
    logs = take(len(relations))
    grad_in = take(len(streams))
    mine = take(plan["mats"])
    other = take(plan["mats"])
    (small_ref,) = take(1)
    do_ref, dctx_ref, dq_ref, dk_ref, dv_ref = take(5)
    width = x_ref.shape[1]
    half = width // 2
    each = 4 // plan["mats"]
    weights = [mats[i // each].at[i % each] for i in range(4)]
    gain = gain_ref[plan["gain"] : plan["gain"] + 1, :]
    groups = plan["groups"]
    nothing = jnp.zeros((8, width), jnp.float32)
    sums = (nothing, nothing, nothing)
    for index, (start, size) in enumerate(streams):

        def one_chunk(step, sums, start=start, index=index):
            here = row_block(start, CHUNK, step)
            there = row_block(0, CHUNK, step)
            grad = carried[index][0][there, :]
            for more in carried[index][1:]:
                grad = grad + more[there, :]
            unit = normed[index][there, :]
            down = norm_rows_back(grad, unit, inverse[index][there, :], gain)
            sent = down.astype(low)
            grad_in[index][there, :] = down
            do_ref[here, :] = sent
            return (
                sums[0] + fold_rows(grad * unit),
                sums[1] + fold_rows(grad),
                sums[2] + fold_rows(widen(sent)),
            )

        sums = lax.fori_loop(0, size * groups // CHUNK, one_chunk, sums)
    sent = do_ref[...]
    for at, size in tiles_of(width):
        dctx_ref[:, at : at + size] = dot_nn(sent, weights[3][:, at : at + size]).astype(low)
    pairs = width // PAIR

    def one_group(group, carry):
        for which, (asking, asked) in enumerate(relations):
            ask = row_block(*streams[asking], group)
            key = row_block(*streams[asked], group)
            bias = same[which][...] + key_ref[key, :]
            for pair in range(pairs):
                lanes = slice(pair * PAIR, (pair + 1) * PAIR)
                base = group * (2 * pairs) + 2 * pair
                grads = pair_backward(
                    q_ref[ask, lanes],
                    k_ref[key, lanes],
                    v_ref[key, lanes],
                    dctx_ref[ask, lanes],
                    bias,
                    [logs[which][base], logs[which][base + 1]],
                )
                dq_ref[ask, lanes], dk_ref[key, lanes], dv_ref[key, lanes] = grads
        return carry

    lax.fori_loop(0, groups, one_group, 0)
    at_zero = core_ref[0] == 0
    rows = x_ref[...]
    context = ctx_ref[...]
    for number, (left, right) in enumerate(
        ((rows, dq_ref), (rows, dk_ref), (rows, dv_ref), (sent, ctx_ref))
    ):
        wide = right[...]
        for at, size in tiles_of(width):
            whole = dot_tn(left[:, at : at + size], wide).astype(low)
            former, latter = whole[:, :half], whole[:, half:]
            mine[number // each][number % each, at : at + size, :] = jnp.where(
                at_zero, former, latter
            )
            other[number // each][number % each, at : at + size, :] = jnp.where(
                at_zero, latter, former
            )
    for index, (start, size) in enumerate(streams):
        span = slice(start, start + size * groups)
        for at, wide in tiles_of(width):
            grad_in[index][:, at : at + wide] += (
                dot_nt(dq_ref[span, :], weights[0][at : at + wide, :])
                + dot_nt(dk_ref[span, :], weights[1][at : at + wide, :])
                + dot_nt(dv_ref[span, :], weights[2][at : at + wide, :])
            )

    def add_chunk(step, sums):
        here = row_block(0, CHUNK, step)
        return (
            sums[0] + fold_rows(widen(dq_ref[here, :])),
            sums[1] + fold_rows(widen(dv_ref[here, :])),
        )

    more = lax.fori_loop(0, x_ref.shape[0] // CHUNK, add_chunk, (nothing, nothing))
    small_ref[...] = jnp.concatenate(
        [close_rows(part) for part in sums + more] + [jnp.zeros((3, width), jnp.float32)], axis=0
    )


def vmem(count):
    return [pl.BlockSpec(memory_space=pltpu.VMEM)] * count


def shape_of(shape, kind):
    return jax.ShapeDtypeStruct(tuple(shape), kind)


def cost_of(micros):
    return pl.CostEstimate(flops=int(micros * 1.15e9), bytes_accessed=1 << 20, transcendentals=0)


def params_of(mib):
    return pltpu.CompilerParams(vmem_limit_bytes=mib << 20)


def layer_plan(layer, sizes, groups, mats):
    if layer == 0:
        starts = (0, sizes[0] * groups)
        streams = [(starts[i], sizes[i]) for i in range(2)]
        relations, gain, shift = [(0, 1), (1, 0)], 0, 11
    else:
        streams, relations = [(0, sizes[0])], [(0, 0)]
        gain, shift = layer, 11 + layer
    return {
        "streams": streams,
        "relations": relations,
        "cross": layer == 0,
        "mats": mats,
        "groups": groups,
        "gain": gain,
        "shift": shift,
        "rows": [3 * layer, 3 * layer + 1, 3 * layer + 2],
        "before": (0, 11),
        "carried": 1 if layer == 0 else 2,
    }


def run_front(plan, x, before, mats, gains, biases, key_bias, same):
    rows, width = x.shape
    groups = plan["groups"]
    outs = [shape_of((rows, width), low)] * 4
    for asking, _ in plan["relations"]:
        outs.append(
            shape_of((groups * width // HEAD_DIM, 1, plan["streams"][asking][1]), jnp.float32)
        )
    counts = [size * groups for _, size in plan["streams"]]
    outs += [shape_of((count, width), jnp.float32) for count in counts]
    outs += [shape_of((count, 1), jnp.float32) for count in counts]
    outs += [shape_of((count, width), low) for count in counts]
    args = [x] + ([] if before is None else [before]) + list(mats) + [gains, biases, key_bias]
    args += list(same)
    results = pl.pallas_call(
        functools.partial(attend_front, plan),
        out_shape=outs,
        in_specs=vmem(len(args)),
        out_specs=vmem(len(outs)),
        scratch_shapes=[pltpu.VMEM((rows, width), jnp.float32)],
        compiler_params=params_of(48),
        cost_estimate=cost_of(0.028 * rows),
        name="attend_front",
    )(*args)
    related, many = len(plan["relations"]), len(counts)
    kept = results[: 4 + related]
    rest = results[4 + related :]
    return kept, rest[:many], rest[many : 2 * many], rest[2 * many :]


def run_back(plan, core, carried, normed, inverse, x, mats, gains, key_bias, same, kept):
    rows, width = x.shape
    counts = [size * plan["groups"] for _, size in plan["streams"]]
    grads = [shape_of(mat.shape[:2] + (width // 2,), low) for mat in mats]
    outs = [shape_of((count, width), jnp.float32) for count in counts] + grads + grads
    outs.append(shape_of((8, width), jnp.float32))
    args = [part for parts in carried for part in parts] + list(normed) + list(inverse) + [x]
    args += list(mats) + [gains, key_bias] + list(same) + list(kept)
    results = pl.pallas_call(
        functools.partial(attend_back, plan),
        out_shape=outs,
        in_specs=[pl.BlockSpec(memory_space=pltpu.SMEM)] + vmem(len(args)),
        out_specs=vmem(len(outs)),
        scratch_shapes=[pltpu.VMEM((rows, width), low)] * 5,
        compiler_params=params_of(56),
        name="attend_back",
    )(core, *args)
    many, count = len(counts), len(mats)
    return (
        results[:many],
        results[many : many + count],
        results[many + count : many + 2 * count],
        results[-1],
    )


def feed_up(line, x_ref, mat_ref, bias_ref, h_ref, slope_ref):
    bias = bias_ref[line : line + 1, :]
    weight = mat_ref[0]
    rows = x_ref.shape[0]
    block = min(FEED_ROWS, rows)

    def one_chunk(step, carry):
        here = row_block(0, block, step)
        hidden = dot_nn(x_ref[here, :], weight) + bias
        share = 0.5 + 0.5 * lax.erf(hidden * SQRT_HALF)
        h_ref[here, :] = (hidden * share).astype(low)
        slope_ref[here, :] = (share + hidden * (jnp.exp(hidden * hidden * -0.5) * BELL)).astype(low)
        return carry

    lax.fori_loop(0, rows // block, one_chunk, 0)


def feed_down(plan, h_ref, mat_ref, gain_ref, bias_ref, unit_ref, cot_ref, live_ref, *refs):
    out_ref, du_ref, do_ref, small_ref, acc_ref = refs
    step = pl.program_id(0)
    width = out_ref.shape[1]

    @pl.when(step == 0)
    def _():
        acc_ref[...] = jnp.zeros_like(acc_ref)

    rows = h_ref[...]
    for at, size in tiles_of(width):
        acc_ref[:, at : at + size] += dot_nt(rows, mat_ref[0, at : at + size, :])

    @pl.when(step == pl.num_programs(0) - 1)
    def _():
        def line(ref, row):
            return ref[row : row + 1, :]

        stream = plan
        last_gain, last_shift = line(gain_ref, 1 + stream), line(bias_ref, 12 + stream)
        gain, shift = line(gain_ref, 3 + stream), line(bias_ref, 14 + stream)
        out_bias = line(bias_ref, 9 + stream)
        nothing = jnp.zeros((8, width), jnp.float32)

        def one_chunk(chunk, sums):
            here = row_block(0, CHUNK, chunk)
            live = live_ref[here, :]
            base = unit_ref[here, :] * last_gain + last_shift
            value, unit, scale = norm_rows(base + acc_ref[here, :] + out_bias, gain, shift)
            out_ref[here, :] = value * live
            grad = widen(cot_ref[here, :]) * live
            down = norm_rows_back(grad, unit, scale, gain)
            sent = down.astype(low)
            du_ref[here, :] = down
            do_ref[here, :] = sent
            return (
                sums[0] + fold_rows(grad * unit),
                sums[1] + fold_rows(grad),
                sums[2] + fold_rows(widen(sent)),
            )

        sums = lax.fori_loop(0, out_ref.shape[0] // CHUNK, one_chunk, (nothing,) * 3)
        small_ref[...] = jnp.concatenate(
            [close_rows(part) for part in sums] + [jnp.zeros((5, width), jnp.float32)], axis=0
        )


def feed_back(core_ref, do_ref, x_ref, h_ref, slope_ref, up_ref, down_ref, *refs):
    dx_ref, mine, other, line_ref = refs
    step = pl.program_id(0)
    sent = do_ref[...]
    rows = x_ref[...]
    slope = (dot_nn(sent, down_ref[0]) * widen(slope_ref[...])).astype(low)
    line_ref[...] = jnp.broadcast_to(
        close_rows(fold_rows(widen(slope))), line_ref.shape
    )
    grad_up = dot_tn(rows, slope).astype(low)
    grad_down = dot_tn(sent, h_ref[...]).astype(low)
    part = dot_nt(slope, up_ref[0])

    @pl.when(step == 0)
    def _():
        dx_ref[...] = part

    @pl.when(step > 0)
    def _():
        dx_ref[...] += part

    @pl.when(step < pl.num_programs(0) // 2)
    def _():
        other[0] = grad_up
        other[1] = grad_down

    @pl.when(step >= pl.num_programs(0) // 2)
    def _():
        mine[0] = grad_up
        mine[1] = grad_down


def run_up(stream, x, mat, biases):
    rows, width = x.shape
    hidden = mat.shape[2]
    wide = lambda step: (0, step)
    return pl.pallas_call(
        functools.partial(feed_up, stream),
        grid=(hidden // FEED,),
        out_shape=[shape_of((rows, hidden), low)] * 2,
        in_specs=[
            pl.BlockSpec((rows, width), lambda step: (0, 0)),
            pl.BlockSpec((1, width, FEED), lambda step: (0, 0, step)),
            pl.BlockSpec((2, FEED), wide),
        ],
        out_specs=[pl.BlockSpec((rows, FEED), wide)] * 2,
        compiler_params=params_of(32),
        cost_estimate=cost_of(0.033 * rows),
        name="feed_up",
    )(x, mat, biases)


def run_down(stream, h, mat, gains, biases, unit, cot, live):
    rows, hidden = h.shape
    width = unit.shape[1]
    fixed = lambda step: (0, 0)

    def whole(array):
        return pl.BlockSpec(array.shape, fixed)

    outs = [
        shape_of((rows, width), jnp.float32),
        shape_of((rows, width), jnp.float32),
        shape_of((rows, width), low),
        shape_of((8, width), jnp.float32),
    ]
    return pl.pallas_call(
        functools.partial(feed_down, stream),
        grid=(hidden // FEED,),
        out_shape=outs,
        in_specs=[
            pl.BlockSpec((rows, FEED), lambda step: (0, step)),
            pl.BlockSpec((1, width, FEED), lambda step: (0, 0, step)),
            whole(gains),
            whole(biases),
            whole(unit),
            whole(cot),
            whole(live),
        ],
        out_specs=[whole(out) for out in outs],
        scratch_shapes=[pltpu.VMEM((rows, width), jnp.float32)],
        compiler_params=params_of(40),
        cost_estimate=cost_of(0.022 * rows),
        name="feed_down",
    )(h, mat, gains, biases, unit, cot, live)


def run_feed_back(core, sent, x, h, slope, up, down):
    rows, hidden = h.shape
    width = x.shape[1]
    steps = hidden // FEED
    half = steps // 2

    def chunk(step, core_ref):
        return (step + half * (1 - core_ref[0])) % steps

    def wide(step, core_ref):
        return (0, chunk(step, core_ref))

    def deep(step, core_ref):
        return (0, 0, chunk(step, core_ref))

    fixed = lambda step, core_ref: (0, 0)
    late = pl.BlockSpec((2, width, FEED), lambda step, core_ref: (0, 0, jnp.maximum(step - half, 0)))
    early = pl.BlockSpec((2, width, FEED), lambda step, core_ref: (0, 0, jnp.minimum(step, half - 1)))
    part = shape_of((2, width, hidden // 2), low)
    return pl.pallas_call(
        feed_back,
        grid_spec=pltpu.PrefetchScalarGridSpec(
            num_scalar_prefetch=1,
            grid=(steps,),
            in_specs=[
                pl.BlockSpec((rows, width), fixed),
                pl.BlockSpec((rows, width), fixed),
                pl.BlockSpec((rows, FEED), wide),
                pl.BlockSpec((rows, FEED), wide),
                pl.BlockSpec((1, width, FEED), deep),
                pl.BlockSpec((1, width, FEED), deep),
            ],
            out_specs=[
                pl.BlockSpec((rows, width), fixed),
                late,
                early,
                pl.BlockSpec((8, FEED), wide),
            ],
        ),
        out_shape=[
            shape_of((rows, width), jnp.float32),
            part,
            part,
            shape_of((8, hidden), jnp.float32),
        ],
        compiler_params=params_of(40),
        cost_estimate=cost_of(0.04 * rows),
        name="feed_back",
    )(core, sent, x, h, slope, up, down)


def adam_update(weight, moment_one, moment_two, average, grad, clip, rate):
    clipped = grad * clip
    new_one = beta_one * moment_one + (1.0 - beta_one) * clipped
    new_two = beta_two * moment_two + (1.0 - beta_two) * clipped * clipped
    direction = (
        new_one / (1.0 - beta_one**STEP) / (jnp.sqrt(new_two / (1.0 - beta_two**STEP)) + adam_eps)
    )
    new_weight = weight - rate * (direction + weight_decay * weight)
    new_average = ema_decay * average + (1.0 - ema_decay) * new_weight
    return (new_weight, new_one, new_two, new_average)


def local(
    lang,
    vis,
    word_mask,
    region_count,
    cot_lang,
    cot_vis,
    attn_w,
    attn_m,
    attn_v,
    attn_ema,
    ffn_w,
    ffn_m,
    ffn_v,
    ffn_ema,
    gains,
    gains_m,
    gains_v,
    gains_ema,
    biases,
    biases_m,
    biases_v,
    biases_ema,
    bias_up,
    bias_up_m,
    bias_up_v,
    bias_up_ema,
):
    core_index = lax.axis_index("mp")
    items, words, regions = lang.shape[0], lang.shape[1], vis.shape[1]
    width = lang.shape[2]
    model_share = gains.shape[1]
    hidden_share = bias_up.shape[1]
    small_own = jnp.concatenate([gains.reshape(-1), biases.reshape(-1), bias_up.reshape(-1)])
    small_size = small_own.shape[0]
    padded = -(-small_size // 1024) * 1024
    small_all = gather_small(jnp.pad(small_own, (0, padded - small_size)).reshape(-1, 128))
    small_all = small_all.reshape(small_all.shape[0], padded)
    cuts = (5 * model_share, 21 * model_share)

    def spread(columns, count):
        parts = columns.reshape(columns.shape[0], count, -1)
        return parts.transpose(1, 0, 2).reshape(count, -1)

    gain_all = spread(small_all[:, : cuts[0]], 5)
    bias_all = spread(small_all[:, cuts[0] : cuts[1]], 16)
    up_all = spread(small_all[:, cuts[1] : small_size], 2)
    attn_low = attn_w.astype(low)
    ffn_low = ffn_w.astype(low)
    forth, back = (4, 8, 1, 2), (4, 8, 2, 1)
    cross_mats = gather_mats(attn_low[0], forth, [(0, 4)])
    self_mats = gather_mats(attn_low[1:].reshape((-1,) + attn_low.shape[2:]), back, [(0, 4), (4, 4)])
    word_mats = gather_mats(ffn_low[0], forth, [(0, 1), (1, 1)])
    region_mats = gather_mats(ffn_low[1], back, [(0, 1), (1, 1)])
    up_mats, down_mats = zip(word_mats, region_mats)

    core = core_index.astype(jnp.int32).reshape(1)
    slots = (words, regions)
    groups = items // GROUP
    sizes = (words * GROUP, regions * GROUP)
    counts = (words * items, regions * items)
    word_live = word_mask.astype(jnp.float32)
    region_live = (jnp.arange(regions)[None, :] < region_count[:, None]).astype(jnp.float32)
    live = [word_live.reshape(-1, 1), region_live.reshape(-1, 1)]
    key_bias = [(part - 1.0) * -mask_fill for part in live]
    key_all = jnp.concatenate(key_bias)
    x_all = jnp.concatenate([lang.reshape(-1, width), vis.reshape(-1, width)])
    cots = [cot_lang.reshape(-1, width), cot_vis.reshape(-1, width)]

    def same_item(asked, asking):
        rows = jnp.arange(sizes[asked])[:, None] // slots[asked]
        columns = jnp.arange(sizes[asking])[None, :] // slots[asking]
        return jnp.where(rows == columns, 0.0, mask_fill).astype(jnp.float32)

    cross_plan = layer_plan(0, sizes, groups, 1)
    cross_same = [same_item(1, 0), same_item(0, 1)]
    cross_kept, unit_one, scale_one, low_one = run_front(
        cross_plan, x_all, None, cross_mats, gain_all, bias_all, key_all, cross_same
    )
    self_plans = [layer_plan(1 + stream, (sizes[stream],), groups, 1) for stream in range(2)]
    self_same = [[same_item(stream, stream)] for stream in range(2)]
    yx, xy = (2, 1, 8, 4), (1, 2, 8, 4)

    def go_up(stream):
        kept, unit, scale, lowered = run_front(
            self_plans[stream],
            low_one[stream],
            unit_one[stream],
            [self_mats[stream]],
            gain_all,
            bias_all,
            key_bias[stream],
            self_same[stream],
        )
        return kept, unit[0], scale[0], lowered[0]

    def go_feed(stream, made, gate):
        return run_up(stream, made[3], up_mats[stream], after(up_all, *gate))

    def go_down(stream, made, up):
        out, grad, sent, small = run_down(
            stream,
            up[0],
            down_mats[stream],
            gain_all,
            bias_all,
            made[1],
            cots[stream],
            live[stream],
        )
        return out.reshape(items, slots[stream], width), grad, sent, small

    def go_feed_back(stream, made, up, down):
        return run_feed_back(
            core, down[2], made[3], *up, up_mats[stream], down_mats[stream]
        )

    def go_back(stream, made, down, feed, gate):
        return run_back(
            self_plans[stream],
            after(core, *gate),
            [[down[1], feed[0]]],
            [made[1]],
            [made[2]],
            low_one[stream],
            [self_mats[stream]],
            gain_all,
            key_bias[stream],
            self_same[stream],
            made[0],
        )

    word_made = go_up(0)
    word_up = go_feed(0, word_made, ())
    word_down = go_down(0, word_made, word_up)
    word_feed = go_feed_back(0, word_made, word_up, word_down)
    word_ring = Scatter(word_feed[1], word_feed[2], yx)
    word_back = go_back(0, word_made, word_down, word_feed, ())
    word_self_ring = Scatter(word_back[1][0], word_back[2][0], xy)
    region_made = go_up(1)
    region_up = go_feed(1, region_made, (word_ring.parts,))
    word_ring.step()
    region_down = go_down(1, region_made, region_up)
    region_feed = go_feed_back(1, region_made, region_up, region_down)
    region_back = go_back(
        1, region_made, region_down, region_feed, (word_ring.parts, word_self_ring.parts)
    )
    region_rings = [
        Scatter(region_feed[1][part : part + 1], region_feed[2][part : part + 1], order)
        for part, order in enumerate((xy, yx))
    ]
    word_ring.step()
    word_self_ring.step()
    region_self_ring = Scatter(region_back[1][0], region_back[2][0], yx)
    grads_in, mine, other, cross_small = run_back(
        cross_plan,
        after(
            core, word_ring.parts, word_self_ring.parts, *[ring.parts for ring in region_rings]
        ),
        [[word_back[0][0]], [region_back[0][0]]],
        unit_one,
        scale_one,
        x_all,
        cross_mats,
        gain_all,
        key_all,
        cross_same,
        cross_kept,
    )
    outputs = [word_down[0], region_down[0]]
    downs = [word_down[1:], region_down[1:]]
    feeds = [word_feed, region_feed]
    self_small = [word_back[3], region_back[3]]
    grad_lang = grads_in[0].reshape(lang.shape)
    grad_vis = grads_in[1].reshape(vis.shape)
    cross_rings = [
        Scatter(mine[0][part : part + 2], other[0][part : part + 2], order)
        for part, order in ((0, xy), (2, yx))
    ]
    region_shard = jnp.concatenate([ring.finish() for ring in region_rings])
    cross_shard = jnp.concatenate([ring.finish() for ring in cross_rings])
    attn_shard = jnp.stack([cross_shard, word_self_ring.finish(), region_self_ring.finish()])
    ffn_shard = jnp.stack([word_ring.finish(), region_shard])

    layers = [cross_small, self_small[0], self_small[1]]
    gain_rows = [part[0:1] for part in layers] + [part[2][0:1] for part in downs]
    bias_rows = []
    for part in layers:
        bias_rows += [part[3:5], part[2:3]]
    bias_rows += [part[2][2:3] for part in downs]
    bias_rows += [part[1:2] for part in layers] + [part[2][1:2] for part in downs]
    up_rows = [part[3][0:1] for part in feeds]

    def split(rows, share):
        rows = jnp.concatenate(rows)
        count = rows.shape[0]
        return rows.reshape(count, -1, share).transpose(1, 0, 2).reshape(-1, count * share)

    small_grad = jnp.concatenate(
        [split(gain_rows, model_share), split(bias_rows, model_share), split(up_rows, hidden_share)],
        axis=1,
    )
    small_grad = jnp.pad(small_grad, ((0, 0), (0, padded - small_size)))
    small_sum = scatter_small(small_grad.reshape(small_grad.shape[0], -1, 128)).reshape(-1)
    gains_shard = small_sum[: cuts[0]].reshape(5, model_share)
    biases_shard = small_sum[cuts[0] : cuts[1]].reshape(16, model_share)
    up_shard = small_sum[cuts[1] : small_size].reshape(2, hidden_share)
    squares = jnp.sum(attn_shard * attn_shard) + jnp.sum(ffn_shard * ffn_shard)
    squares = squares + jnp.where(core_index == 0, jnp.sum(small_sum * small_sum), 0.0)
    grad_norm = jnp.sqrt(sum_all(squares))
    clip = jnp.minimum(1.0, clip_norm / (grad_norm + 1e-06))
    attn_new = adam_update(attn_w, attn_m, attn_v, attn_ema, attn_shard, clip, rate_mats)
    ffn_new = adam_update(ffn_w, ffn_m, ffn_v, ffn_ema, ffn_shard, clip, rate_mats)
    gains_new = adam_update(gains, gains_m, gains_v, gains_ema, gains_shard, clip, rate_small)
    biases_new = adam_update(biases, biases_m, biases_v, biases_ema, biases_shard, clip, rate_small)
    up_new = adam_update(bias_up, bias_up_m, bias_up_v, bias_up_ema, up_shard, clip, rate_small)
    return (
        outputs[0],
        outputs[1],
        grad_lang,
        grad_vis,
        grad_norm,
        attn_new[0],
        attn_new[1],
        attn_new[2],
        attn_new[3],
        ffn_new[0],
        ffn_new[1],
        ffn_new[2],
        ffn_new[3],
        gains_new[0],
        gains_new[1],
        gains_new[2],
        gains_new[3],
        biases_new[0],
        biases_new[1],
        biases_new[2],
        biases_new[3],
        up_new[0],
        up_new[1],
        up_new[2],
        up_new[3],
    )


def solution(mesh):
    return jax.shard_map(
        local,
        mesh=mesh,
        in_specs=(
            P(("dp", "mp"), None, None),
            P(("dp", "mp"), None, None),
            P(("dp", "mp"), None),
            P(("dp", "mp")),
            P(("dp", "mp"), None, None),
            P(("dp", "mp"), None, None),
            P(None, None, "dp", "mp"),
            P(None, None, "dp", "mp"),
            P(None, None, "dp", "mp"),
            P(None, None, "dp", "mp"),
            P(None, None, "dp", "mp"),
            P(None, None, "dp", "mp"),
            P(None, None, "dp", "mp"),
            P(None, None, "dp", "mp"),
            P(None, "dp"),
            P(None, "dp"),
            P(None, "dp"),
            P(None, "dp"),
            P(None, "dp"),
            P(None, "dp"),
            P(None, "dp"),
            P(None, "dp"),
            P(None, "dp"),
            P(None, "dp"),
            P(None, "dp"),
            P(None, "dp"),
        ),
        out_specs=(
            P(("dp", "mp"), None, None),
            P(("dp", "mp"), None, None),
            P(("dp", "mp"), None, None),
            P(("dp", "mp"), None, None),
            P(),
            P(None, None, "dp", "mp"),
            P(None, None, "dp", "mp"),
            P(None, None, "dp", "mp"),
            P(None, None, "dp", "mp"),
            P(None, None, "dp", "mp"),
            P(None, None, "dp", "mp"),
            P(None, None, "dp", "mp"),
            P(None, None, "dp", "mp"),
            P(None, "dp"),
            P(None, "dp"),
            P(None, "dp"),
            P(None, "dp"),
            P(None, "dp"),
            P(None, "dp"),
            P(None, "dp"),
            P(None, "dp"),
            P(None, "dp"),
            P(None, "dp"),
            P(None, "dp"),
            P(None, "dp"),
        ),
        check_vma=False,
    )
```

```python
import functools
import math
import jax
import jax.numpy as jnp
from jax import lax
from jax.experimental import pallas as pl
from jax.experimental.pallas import tpu as pltpu
from jax.sharding import PartitionSpec as P

HEAD_DIM = 64
STEP = 7


norm_eps = 1e-12
mask_fill = -1000000000.0
beta_one = 0.5
beta_two = 0.6
ema_decay = 0.5
adam_eps = 1e-08
weight_decay = 0.01
rate_mats = 0.02
rate_small = 0.2
clip_norm = 1.0

GROUP = 4
low = jnp.bfloat16
LINE = 4
CHIPS = 16
PAIR = 2 * HEAD_DIM
TILE = 256
CHUNK = 32
FEED = 1536
FEED_ROWS = 64
BELL = (2.0 * math.pi) ** -0.5
COST_SCALE = 0.05
HEAD_SCALE = HEAD_DIM ** (-0.5)
SQRT_HALF = 0.5**0.5


def moves(target):
    pairs = []
    for z in range(LINE):
        for y in range(2):
            for x in range(2):
                there = target(z, y, x)
                if there is not None:
                    pairs.append((z * 4 + y * 2 + x, there[0] * 4 + there[1] * 2 + there[2]))
    return pairs


routes = {
    1: moves(lambda z, y, x: (z, y, 1 - x)),
    2: moves(lambda z, y, x: (z, 1 - y, x)),
    4: moves(lambda z, y, x: (z ^ 1, y, x)),
    8: moves(lambda z, y, x: (z ^ 2, y, x)),
}
middle = moves(lambda z, y, x: (3 - z, y, x) if z in (1, 2) else None)
inwards = moves(lambda z, y, x: (z ^ 1, y, x) if z in (0, 3) else None)
outwards = moves(lambda z, y, x: (z ^ 1, y, x) if z in (1, 2) else None)


def send(values, bit):
    return lax.ppermute(values, "dp", routes[bit])


def swap_cores(values):
    return lax.ppermute(values, "mp", [(0, 1), (1, 0)])


def widen(values):
    return values.astype(jnp.float32)


def pick(values, axis, index):
    return lax.dynamic_index_in_dim(values, index, axis, keepdims=False)


def bit_of(bit):
    return (lax.axis_index("dp") // bit) % 2


def after(values, *others):
    return lax.optimization_barrier((values,) + others)[0]


def assemble_kernel(places, spans, rows, place_ref, *refs):
    pieces, wholes, sem = refs[: len(places)], refs[len(places) : -1], refs[-1]
    columns = pieces[0].shape[3]
    below = wholes[len(spans)] if len(wholes) > len(spans) else None
    copies = []
    for piece, (first, other) in zip(pieces, places):
        for number in range(piece.shape[0]):
            row = pl.ds(pl.multiple_of(place_ref[first + number] * rows, 16), rows)
            column = pl.ds(pl.multiple_of((place_ref[CHIPS] ^ other) * columns, 128), columns)
            for whole, (start, count) in zip(wholes, spans):
                if piece.shape[2] == rows:
                    pairs = [(piece.at[number, pl.ds(start, count)], whole.at[:, row, column])]
                else:
                    pairs = [
                        (piece.at[number, 0, pl.ds(at * rows, rows)], whole.at[at, row, column])
                        for at in range(start, start + count)
                    ]
                copies += [pltpu.make_async_copy(here, there, sem) for here, there in pairs]
            if below is not None and not other:
                rest = pl.ds(piece.shape[2] - below.shape[1], below.shape[1])
                copies.append(
                    pltpu.make_async_copy(
                        piece.at[number, 0, rest], below.at[place_ref[first + number]], sem
                    )
                )
    for copy in copies:
        copy.start()
    for copy in copies:
        copy.wait()


def assemble(pieces, places, spans, rows, place):
    columns = pieces[0].shape[3]
    outs = [shape_of((count, rows * CHIPS, columns * 2), low) for _, count in spans]
    below = pieces[0].shape[2] - rows * sum(count for _, count in spans)
    if pieces[0].shape[2] != rows:
        outs.append(shape_of((CHIPS, below, columns), low))
    return pl.pallas_call(
        functools.partial(assemble_kernel, places, spans, rows),
        out_shape=outs,
        in_specs=[pl.BlockSpec(memory_space=pltpu.SMEM)]
        + [pl.BlockSpec(memory_space=pl.ANY)] * len(pieces),
        out_specs=vmem(len(outs)),
        scratch_shapes=[pltpu.SemaphoreType.DMA],
        compiler_params=params_of(24),
        cost_estimate=cost_of(3),
        name="assemble",
    )(place, *pieces)


class Gather:
    def __init__(self, own):
        self.staged = lax.axis_size("dp") == CHIPS
        self.own = own[None]
        self.last = self.pair = self.mid = self.four = self.own

    def near(self, *gate):
        if self.staged:
            own = after(self.own, *gate) if gate else self.own
            self.pair = self.last = jnp.concatenate([self.own, send(own, 4)])

    def inner(self, *gate):
        if self.staged:
            self.mid = self.last = lax.ppermute(after(self.pair, *gate), "dp", middle)

    def outer(self, *gate):
        if self.staged:
            out = lax.ppermute(after(self.mid, *gate), "dp", outwards)
            self.four = self.last = jnp.concatenate([self.pair, self.mid + out])

    def sides(self, *gate):
        if self.staged:
            four = after(self.four, *gate)
            self.by_x, self.by_y = send(four, 1), send(four, 2)
            self.last = (self.by_x, self.by_y)

    def corner(self, *gate):
        if self.staged:
            by_x, by_y = after((self.by_x[:2], self.by_y[2:]), *gate)
            self.corners = send(by_x, 2), send(by_y, 1)
            self.last = self.corners

    def most(self, *gate):
        if self.staged:
            parts = jnp.concatenate([self.four, self.by_x, self.by_y])
            self.major = (parts, swap_cores(after(parts, *gate)))
            self.last = self.major[1]

    def rest(self, *gate):
        if self.staged:
            parts = jnp.concatenate(self.corners)
            self.minor = (parts, swap_cores(after(parts, *gate)))
            self.last = self.minor[1]

    def place(self):
        chip = lax.axis_index("dp")
        z = chip // 4
        far = jnp.where((z == 1) | (z == 2), 12, 8)
        four = jnp.stack([chip, chip ^ 4, chip ^ far, chip ^ far ^ 4])
        return jnp.concatenate(
            [four, four ^ 1, four ^ 2, four ^ 3, lax.axis_index("mp").reshape(1)]
        ).astype(jnp.int32)

    def finish(self, spans, rows):
        if not self.staged:
            whole = lax.all_gather(self.own[0], "dp", axis=1, tiled=True)
            whole = lax.all_gather(whole, "mp", axis=2, tiled=True)
            return [whole[start : start + count] for start, count in spans]
        pieces, places = [], []
        for pair, first in zip((self.major, self.minor), (0, 12)):
            pieces += pair
            places += [(first, 0), (first, 1)]
        made = assemble(pieces, places, spans, rows, self.place())
        self.below = made[-1]
        return made[: len(spans)]


class Scatter:
    def __init__(self, other, gate=()):
        self.staged = lax.axis_size("dp") == CHIPS
        self.raw = []
        self.arrived = self.last = swap_cores(after(other, *gate))

    def add(self, mine, split):
        self.total = widen(mine) + widen(self.arrived)
        if self.staged:
            total = self.total.astype(low)
            total = total.reshape((-1, 4, 2, 2, total.shape[1] // CHIPS, total.shape[2]))
            count = total.shape[0]
            self.parts = [total[: count // 2], total[count // 2 :]] if split else [total]
            self.last = self.parts

    def side(self, bit, *gate):
        if not self.staged:
            return
        parts, self.raw = [], []
        for part, way in zip(self.parts, (bit, 3 - bit)):
            axis = 2 if way == 2 or part.ndim == 5 else 3
            kept = pick(part, axis, bit_of(way))
            arrived = send(after(pick(part, axis, 1 - bit_of(way)), *gate), way)
            self.raw.append(arrived)
            parts.append((widen(kept) + widen(arrived)).astype(low))
        if parts[0].ndim == 4:
            whole = parts[0] if len(parts) == 1 else jnp.concatenate(parts)
            whole = whole.reshape((whole.shape[0], 2, 2) + whole.shape[2:])
            self.own = pick(whole, 1, bit_of(8))
            self.far = pick(whole, 1, 1 - bit_of(8))
            self.last = (self.own, self.far)
        else:
            self.parts = self.last = parts

    def join(self, narrow):
        if self.staged:
            columns = narrow.own.shape[-1]

            def cut(values):
                return [values[..., at : at + columns] for at in range(0, values.shape[-1], columns)]

            self.own = jnp.concatenate(cut(self.own) + [narrow.own])
            self.far = jnp.concatenate(cut(self.far) + [narrow.far])
            self.last = (self.own, self.far)

    def outer(self, *gate):
        if self.staged:
            arrived = lax.ppermute(after(self.far, *gate), "dp", inwards)
            self.far = self.last = (widen(self.far) + widen(arrived)).astype(low)

    def inner(self, *gate):
        if self.staged:
            arrived = lax.ppermute(after(self.far, *gate), "dp", middle)
            self.own = self.last = (widen(self.own) + widen(arrived)).astype(low)

    def near(self, *gate):
        if not self.staged:
            return lax.psum_scatter(self.total, "dp", scatter_dimension=1, tiled=True)
        arrived = send(after(pick(self.own, 1, 1 - bit_of(4)), *gate), 4)
        return widen(pick(self.own, 1, bit_of(4))) + widen(arrived)


def three_terms(values):
    terms = []
    for _ in range(3):
        terms.append(values.astype(low))
        values = values - lax.reduce_precision(values, 8, 7)
    return jnp.stack(terms)


def scatter_small(values):
    values = values + swap_cores(values)
    if lax.axis_size("dp") != CHIPS:
        return lax.psum_scatter(values, "dp", scatter_dimension=0, tiled=True)[0]
    for bit in (8, 4, 2, 1):
        half = values.shape[0] // 2
        at_zero = bit_of(bit) == 0
        kept = jnp.where(at_zero, values[:half], values[half:])
        sent = jnp.where(at_zero, values[half:], values[:half])
        values = kept + send(sent, bit)
    return values[0]


def sum_all(value):
    if lax.axis_size("dp") != CHIPS:
        return lax.psum(value, ("dp", "mp"))
    value = value.reshape(1, 1)
    value = value + swap_cores(value)
    for bit in (1, 2, 4, 8):
        value = value + send(value, bit)
    return value[0, 0]


def dot_nn(left, right):
    return lax.dot_general(left, right, (((1,), (0,)), ((), ())), preferred_element_type=jnp.float32)


def dot_nt(left, right):
    return lax.dot_general(left, right, (((1,), (1,)), ((), ())), preferred_element_type=jnp.float32)


def dot_tn(left, right):
    return lax.dot_general(left, right, (((0,), (0,)), ((), ())), preferred_element_type=jnp.float32)


def fold_rows(values):
    return jnp.sum(values.reshape(values.shape[0] // 8, 8, values.shape[1]), axis=0)


def close_rows(values):
    return jnp.sum(values, axis=0, keepdims=True)


def norm_rows(summed, gain, shift):
    average = jnp.mean(summed, axis=-1, keepdims=True)
    centered = summed - average
    inverse = lax.rsqrt(jnp.mean(centered * centered, axis=-1, keepdims=True) + norm_eps)
    normed = centered * inverse
    return normed * gain + shift, normed, inverse


def norm_rows_back(grad_out, normed, inverse, gain):
    scaled = grad_out * gain
    return inverse * (
        scaled
        - jnp.mean(scaled, axis=-1, keepdims=True)
        - normed * jnp.mean(scaled * normed, axis=-1, keepdims=True)
    )


def stack_heads(block):
    first = lax.broadcasted_iota(jnp.int32, block.shape, 1) < HEAD_DIM
    nothing = jnp.zeros_like(block)
    return jnp.concatenate(
        [jnp.where(first, block, nothing), jnp.where(first, nothing, block)], axis=0
    )


def merge_heads(double):
    rows = double.shape[0] // 2
    first = lax.broadcasted_iota(jnp.int32, (rows, double.shape[1]), 1) < HEAD_DIM
    return jnp.where(first, double[:rows], double[rows:])


def pair_forward(queries, keys, values, bias):
    count = keys.shape[0]
    scores = dot_nt(stack_heads(keys), queries * HEAD_SCALE)
    weights, totals = [], []
    for part in (scores[:count] + bias, scores[count:] + bias):
        top = jnp.max(part, axis=0, keepdims=True)
        powers = jnp.exp(part - top)
        total = jnp.sum(powers, axis=0, keepdims=True)
        weights.append((powers * (1.0 / total)).astype(low))
        totals.append(top + jnp.log(total))
    context = dot_tn(jnp.concatenate(weights, axis=0), stack_heads(values))
    return context.astype(low), totals


def pair_backward(queries, keys, values, grad, bias, totals):
    count = keys.shape[0]
    both_keys = stack_heads(keys)
    queries = queries * HEAD_SCALE
    scores = dot_nt(both_keys, queries)
    sensed = dot_nt(stack_heads(values), grad)
    weights, slopes = [], []
    for part, sense, total in (
        (scores[:count], sensed[:count], totals[0]),
        (scores[count:], sensed[count:], totals[1]),
    ):
        weight = jnp.exp(part + bias - total)
        inner = jnp.sum(sense * weight, axis=0, keepdims=True)
        weights.append(weight.astype(low))
        slopes.append((weight * (sense - inner)).astype(low))
    weights = jnp.concatenate(weights, axis=0)
    slopes = jnp.concatenate(slopes, axis=0)
    grad_queries = (dot_tn(slopes, both_keys) * HEAD_DIM ** (-0.5)).astype(low)
    grad_keys = merge_heads(dot_nn(slopes, queries)).astype(low)
    grad_values = merge_heads(dot_nn(weights, grad)).astype(low)
    return grad_queries, grad_keys, grad_values


def tiles_of(width):
    return [(at, min(TILE, width - at)) for at in range(0, width, TILE)]


def row_block(start, size, step):
    return pl.ds(pl.multiple_of(start + step * size, 16), size)


def attend_front(plan, *refs):
    streams, relations, cross = plan["streams"], plan["relations"], plan["cross"]
    refs = list(refs)

    def take(count):
        taken = refs[:count]
        del refs[:count]
        return taken

    (x_ref,) = take(1)
    before = [] if cross else take(1)
    mats = take(plan["mats"])
    gain_ref, bias_ref, key_ref = take(3)
    same = take(len(relations))
    q_ref, k_ref, v_ref, ctx_ref = take(4)
    logs = take(len(relations))
    normed = take(len(streams))
    inverse = take(len(streams))
    lowered = take(len(streams))
    (acc_ref,) = take(1)
    width = x_ref.shape[1]
    weights = [mats[i // (4 // len(mats))].at[i % (4 // len(mats))] for i in range(4)]
    rows = x_ref[...]
    for target, weight, row in ((q_ref, 0, 0), (k_ref, 1, None), (v_ref, 2, 1)):
        for at, size in tiles_of(width):
            part = dot_nn(rows, weights[weight][:, at : at + size])
            if row is not None:
                line = plan["rows"][row]
                part = part + bias_ref[line : line + 1, at : at + size]
            target[:, at : at + size] = part.astype(low)
    pairs = width // PAIR
    groups = plan["groups"]

    def one_group(group, carry):
        for which, (asking, asked) in enumerate(relations):
            ask = row_block(*streams[asking], group)
            key = row_block(*streams[asked], group)
            bias = same[which][...] + key_ref[key, :]
            for pair in range(pairs):
                lanes = slice(pair * PAIR, (pair + 1) * PAIR)
                context, totals = pair_forward(
                    q_ref[ask, lanes], k_ref[key, lanes], v_ref[key, lanes], bias
                )
                ctx_ref[ask, lanes] = context
                for side in range(2):
                    logs[which][group * (2 * pairs) + 2 * pair + side] = totals[side]
        return carry

    lax.fori_loop(0, groups, one_group, 0)
    context = ctx_ref[...]
    for at, size in tiles_of(width):
        acc_ref[:, at : at + size] = dot_nt(context, weights[3][at : at + size, :])
    gain = gain_ref[plan["gain"] : plan["gain"] + 1, :]
    shift = bias_ref[plan["shift"] : plan["shift"] + 1, :]
    out_bias = bias_ref[plan["rows"][2] : plan["rows"][2] + 1, :]
    for index, (start, size) in enumerate(streams):

        def one_chunk(step, carry, start=start, index=index):
            here = row_block(start, CHUNK, step)
            there = row_block(0, CHUNK, step)
            if cross:
                base = widen(x_ref[here, :])
            else:
                last_gain, last_shift = plan["before"]
                base = (
                    before[0][here, :] * gain_ref[last_gain : last_gain + 1, :]
                    + bias_ref[last_shift : last_shift + 1, :]
                )
            value, unit, scale = norm_rows(base + acc_ref[here, :] + out_bias, gain, shift)
            normed[index][there, :] = unit
            inverse[index][there, :] = scale
            lowered[index][there, :] = value.astype(low)
            return carry

        lax.fori_loop(0, size * groups // CHUNK, one_chunk, 0)


def add_inputs(streams, groups, weights, grads, grad_in):
    dq_ref, dk_ref, dv_ref = grads
    for index, (start, size) in enumerate(streams):
        span = slice(start, start + size * groups)
        for at, wide in tiles_of(dq_ref.shape[1]):
            grad_in[index][:, at : at + wide] += (
                dot_nt(dq_ref[span, :], weights[0][at : at + wide, :])
                + dot_nt(dk_ref[span, :], weights[1][at : at + wide, :])
                + dot_nt(dv_ref[span, :], weights[2][at : at + wide, :])
            )


def cross_inputs(plan, dq_ref, dk_ref, dv_ref, mat_ref, *refs):
    streams = plan["streams"]
    grads, outs = refs[: len(streams)], refs[len(streams) :]
    for grad, out in zip(grads, outs):
        out[...] = grad[...]
    weights = [mat_ref.at[i] for i in range(3)]
    add_inputs(streams, plan["groups"], weights, (dq_ref, dk_ref, dv_ref), outs)


def attend_back(plan, *refs):
    streams, relations = plan["streams"], plan["relations"]
    refs = list(refs)

    def take(count):
        taken = refs[:count]
        del refs[:count]
        return taken

    (core_ref,) = take(1)
    carried = [take(plan["carried"]) for _ in streams]
    normed = take(len(streams))
    inverse = take(len(streams))
    (x_ref,) = take(1)
    mats = take(plan["mats"])
    gain_ref, key_ref = take(2)
    same = take(len(relations))
    q_ref, k_ref, v_ref, ctx_ref = take(4)
    logs = take(len(relations))
    grad_in = take(len(streams))
    mine = take(plan["mats"])
    other = take(plan["mats"])
    (small_ref,) = take(1)
    dq_ref, dk_ref, dv_ref = take(3)
    do_ref, dctx_ref = take(2)
    width = x_ref.shape[1]
    half = width // 2
    each = 4 // plan["mats"]
    weights = [mats[i // each].at[i % each] for i in range(4)]
    gain = gain_ref[plan["gain"] : plan["gain"] + 1, :]
    groups = plan["groups"]
    nothing = jnp.zeros((8, width), jnp.float32)
    sums = (nothing, nothing, nothing)
    for index, (start, size) in enumerate(streams):

        def one_chunk(step, sums, start=start, index=index):
            here = row_block(start, CHUNK, step)
            there = row_block(0, CHUNK, step)
            grad = carried[index][0][there, :]
            for more in carried[index][1:]:
                grad = grad + more[there, :]
            unit = normed[index][there, :]
            down = norm_rows_back(grad, unit, inverse[index][there, :], gain)
            sent = down.astype(low)
            grad_in[index][there, :] = down
            do_ref[here, :] = sent
            return (
                sums[0] + fold_rows(grad * unit),
                sums[1] + fold_rows(grad),
                sums[2] + fold_rows(widen(sent)),
            )

        sums = lax.fori_loop(0, size * groups // CHUNK, one_chunk, sums)
    sent = do_ref[...]
    for at, size in tiles_of(width):
        dctx_ref[:, at : at + size] = dot_nn(sent, weights[3][:, at : at + size]).astype(low)
    pairs = width // PAIR

    def one_group(group, carry):
        for which, (asking, asked) in enumerate(relations):
            ask = row_block(*streams[asking], group)
            key = row_block(*streams[asked], group)
            bias = same[which][...] + key_ref[key, :]
            for pair in range(pairs):
                lanes = slice(pair * PAIR, (pair + 1) * PAIR)
                base = group * (2 * pairs) + 2 * pair
                grads = pair_backward(
                    q_ref[ask, lanes],
                    k_ref[key, lanes],
                    v_ref[key, lanes],
                    dctx_ref[ask, lanes],
                    bias,
                    [logs[which][base], logs[which][base + 1]],
                )
                dq_ref[ask, lanes], dk_ref[key, lanes], dv_ref[key, lanes] = grads
        return carry

    lax.fori_loop(0, groups, one_group, 0)
    at_zero = core_ref[0] == 0
    rows = x_ref[...]
    last = None
    for number, (left, right) in enumerate(
        ((rows, dq_ref), (rows, dk_ref), (rows, dv_ref), (sent, ctx_ref))
    ):
        wide = right[...]
        if left is not last:
            flipped, last = left.T, left
        for at, size in tiles_of(width):
            whole = dot_nn(flipped[at : at + size, :], wide).astype(low)
            former, latter = whole[:, :half], whole[:, half:]
            mine[number // each][number % each, at : at + size, :] = jnp.where(
                at_zero, former, latter
            )
            other[number // each][number % each, at : at + size, :] = jnp.where(
                at_zero, latter, former
            )
    if not plan["cross"]:
        add_inputs(streams, groups, weights, (dq_ref, dk_ref, dv_ref), grad_in)

    def add_chunk(step, sums):
        here = row_block(0, CHUNK, step)
        return (
            sums[0] + fold_rows(widen(dq_ref[here, :])),
            sums[1] + fold_rows(widen(dv_ref[here, :])),
        )

    more = lax.fori_loop(0, x_ref.shape[0] // CHUNK, add_chunk, (nothing, nothing))
    small_ref[...] = jnp.concatenate(
        [close_rows(part) for part in sums + more] + [jnp.zeros((3, width), jnp.float32)], axis=0
    )


def vmem(count):
    return [pl.BlockSpec(memory_space=pltpu.VMEM)] * count


def shape_of(shape, kind):
    return jax.ShapeDtypeStruct(tuple(shape), kind)


def cost_of(micros):
    return pl.CostEstimate(flops=int(micros * COST_SCALE * 1.15e9), bytes_accessed=1 << 20, transcendentals=0)


def params_of(mib):
    return pltpu.CompilerParams(vmem_limit_bytes=mib << 20)


def layer_plan(layer, sizes, groups, mats):
    if layer == 0:
        starts = (0, sizes[0] * groups)
        streams = [(starts[i], sizes[i]) for i in range(2)]
        relations, gain, shift = [(0, 1), (1, 0)], 0, 11
    else:
        streams, relations = [(0, sizes[0])], [(0, 0)]
        gain, shift = layer, 11 + layer
    return {
        "streams": streams,
        "relations": relations,
        "cross": layer == 0,
        "mats": mats,
        "groups": groups,
        "gain": gain,
        "shift": shift,
        "rows": [3 * layer, 3 * layer + 1, 3 * layer + 2],
        "before": (0, 11),
        "carried": 1 if layer == 0 else 3,
    }


def run_front(plan, x, before, mats, gains, biases, key_bias, same):
    rows, width = x.shape
    groups = plan["groups"]
    outs = [shape_of((rows, width), low)] * 4
    for asking, _ in plan["relations"]:
        outs.append(
            shape_of((groups * width // HEAD_DIM, 1, plan["streams"][asking][1]), jnp.float32)
        )
    counts = [size * groups for _, size in plan["streams"]]
    outs += [shape_of((count, width), jnp.float32) for count in counts]
    outs += [shape_of((count, 1), jnp.float32) for count in counts]
    outs += [shape_of((count, width), low) for count in counts]
    args = [x] + ([] if before is None else [before]) + list(mats) + [gains, biases, key_bias]
    args += list(same)
    results = pl.pallas_call(
        functools.partial(attend_front, plan),
        out_shape=outs,
        in_specs=vmem(len(args)),
        out_specs=vmem(len(outs)),
        scratch_shapes=[pltpu.VMEM((rows, width), jnp.float32)],
        compiler_params=params_of(48),
        cost_estimate=cost_of(0.028 * rows),
        name="attend_front",
    )(*args)
    related, many = len(plan["relations"]), len(counts)
    kept = results[: 4 + related]
    rest = results[4 + related :]
    return kept, rest[:many], rest[many : 2 * many], rest[2 * many :]


def run_back(plan, core, carried, normed, inverse, x, mats, gains, key_bias, same, kept):
    rows, width = x.shape
    counts = [size * plan["groups"] for _, size in plan["streams"]]
    grads = [shape_of(mat.shape[:2] + (width // 2,), low) for mat in mats]
    outs = [shape_of((count, width), jnp.float32) for count in counts] + grads + grads
    outs.append(shape_of((8, width), jnp.float32))
    pieces = [shape_of((rows, width), low)] * 3
    cross = plan["cross"]
    args = [part for parts in carried for part in parts] + list(normed) + list(inverse) + [x]
    args += list(mats) + [gains, key_bias] + list(same) + list(kept)
    results = pl.pallas_call(
        functools.partial(attend_back, plan),
        out_shape=outs + (pieces if cross else []),
        in_specs=[pl.BlockSpec(memory_space=pltpu.SMEM)] + vmem(len(args)),
        out_specs=vmem(len(outs) + (3 if cross else 0)),
        scratch_shapes=[pltpu.VMEM((rows, width), low)] * (2 if cross else 5),
        compiler_params=params_of(56),
        name="attend_back",
    )(core, *args)
    many, count = len(counts), len(mats)
    return (
        results[:many],
        results[many : many + count],
        results[many + count : many + 2 * count],
        results[len(outs) - 1],
        results[len(outs) :],
    )


def run_cross_inputs(plan, pieces, mat, grads):
    outs = [shape_of(grad.shape, jnp.float32) for grad in grads]
    return pl.pallas_call(
        functools.partial(cross_inputs, plan),
        out_shape=outs,
        in_specs=vmem(4 + len(grads)),
        out_specs=vmem(len(grads)),
        compiler_params=params_of(48),
        cost_estimate=cost_of(10),
        name="cross_inputs",
    )(*pieces, mat, *grads)


def feed_up(line, x_ref, mat_ref, bias_ref, h_ref, slope_ref, hidden_ref):
    bias = bias_ref[line : line + 1, :]
    hidden_ref[...] = dot_nn(x_ref[...], mat_ref[0])

    def one_chunk(step, carry):
        here = row_block(0, FEED_ROWS, step)
        hidden = hidden_ref[here, :] + bias
        share = 0.5 + 0.5 * lax.erf(hidden * SQRT_HALF)
        h_ref[here, :] = (hidden * share).astype(low)
        slope_ref[here, :] = (share + hidden * (jnp.exp(hidden * hidden * -0.5) * BELL)).astype(low)
        return carry

    lax.fori_loop(0, x_ref.shape[0] // FEED_ROWS, one_chunk, 0)


def feed_down(plan, h_ref, mat_ref, gain_ref, bias_ref, unit_ref, cot_ref, live_ref, *refs):
    out_ref, du_ref, do_ref, small_ref, acc_ref = refs
    step = pl.program_id(0)
    width = out_ref.shape[1]

    @pl.when(step == 0)
    def _():
        acc_ref[...] = jnp.zeros_like(acc_ref)

    rows = h_ref[...]
    for at, size in tiles_of(width):
        acc_ref[:, at : at + size] += dot_nt(rows, mat_ref[0, at : at + size, :])

    @pl.when(step == pl.num_programs(0) - 1)
    def _():
        def line(ref, row):
            return ref[row : row + 1, :]

        stream = plan
        last_gain, last_shift = line(gain_ref, 1 + stream), line(bias_ref, 12 + stream)
        gain, shift = line(gain_ref, 3 + stream), line(bias_ref, 14 + stream)
        out_bias = line(bias_ref, 9 + stream)
        nothing = jnp.zeros((8, width), jnp.float32)

        def one_chunk(chunk, sums):
            here = row_block(0, CHUNK, chunk)
            live = live_ref[here, :]
            base = unit_ref[here, :] * last_gain + last_shift
            value, unit, scale = norm_rows(base + acc_ref[here, :] + out_bias, gain, shift)
            out_ref[here, :] = value * live
            grad = widen(cot_ref[here, :]) * live
            down = norm_rows_back(grad, unit, scale, gain)
            sent = down.astype(low)
            du_ref[here, :] = down
            do_ref[here, :] = sent
            return (
                sums[0] + fold_rows(grad * unit),
                sums[1] + fold_rows(grad),
                sums[2] + fold_rows(widen(sent)),
            )

        sums = lax.fori_loop(0, out_ref.shape[0] // CHUNK, one_chunk, (nothing,) * 3)
        small_ref[...] = jnp.concatenate(
            [close_rows(part) for part in sums] + [jnp.zeros((5, width), jnp.float32)], axis=0
        )


def feed_back(core_ref, do_ref, x_ref, h_ref, slope_ref, up_ref, down_ref, *refs):
    dx_ref, grad_ref, line_ref, sent_flip, rows_flip = refs
    step = pl.program_id(0)
    sent = do_ref[...]

    @pl.when(step == 0)
    def _():
        sent_flip[...] = sent.T
        rows_flip[...] = x_ref[...].T

    slope = (dot_nn(sent, down_ref[0]) * widen(slope_ref[...])).astype(low)
    line_ref[...] = jnp.broadcast_to(close_rows(fold_rows(widen(slope))), line_ref.shape)
    grad_ref[0] = dot_nn(rows_flip[...], slope).astype(low)
    grad_ref[1] = dot_nn(sent_flip[...], h_ref[...]).astype(low)
    part = dot_nt(slope, up_ref[0])

    @pl.when(step == 0)
    def _():
        dx_ref[...] = part

    @pl.when(step > 0)
    def _():
        dx_ref[...] += part


def run_up(stream, x, mat, biases):
    rows, width = x.shape
    hidden = mat.shape[2]
    wide = lambda step: (0, step)
    return pl.pallas_call(
        functools.partial(feed_up, stream),
        grid=(hidden // FEED,),
        out_shape=[shape_of((rows, hidden), low)] * 2,
        in_specs=[
            pl.BlockSpec((rows, width), lambda step: (0, 0)),
            pl.BlockSpec((1, width, FEED), lambda step: (0, 0, step)),
            pl.BlockSpec((2, FEED), wide),
        ],
        out_specs=[pl.BlockSpec((rows, FEED), wide)] * 2,
        scratch_shapes=[pltpu.VMEM((rows, FEED), jnp.float32)],
        compiler_params=params_of(32),
        cost_estimate=cost_of(0.033 * rows),
        name="feed_up",
    )(x, mat, biases)


def run_down(stream, h, mat, gains, biases, unit, cot, live):
    rows, hidden = h.shape
    width = unit.shape[1]
    fixed = lambda step: (0, 0)

    def whole(array):
        return pl.BlockSpec(array.shape, fixed)

    outs = [
        shape_of((rows, width), jnp.float32),
        shape_of((rows, width), jnp.float32),
        shape_of((rows, width), low),
        shape_of((8, width), jnp.float32),
    ]
    return pl.pallas_call(
        functools.partial(feed_down, stream),
        grid=(hidden // FEED,),
        out_shape=outs,
        in_specs=[
            pl.BlockSpec((rows, FEED), lambda step: (0, step)),
            pl.BlockSpec((1, width, FEED), lambda step: (0, 0, step)),
            whole(gains),
            whole(biases),
            whole(unit),
            whole(cot),
            whole(live),
        ],
        out_specs=[whole(out) for out in outs],
        scratch_shapes=[pltpu.VMEM((rows, width), jnp.float32)],
        compiler_params=params_of(40),
        cost_estimate=cost_of(0.022 * rows),
        name="feed_down",
    )(h, mat, gains, biases, unit, cot, live)


def run_feed_back(core, flip, sent, x, h, slope, up, down):
    rows, hidden = h.shape
    width = x.shape[1]
    steps = hidden // FEED // 2

    def chunk(step, core_ref):
        side = core_ref[0]
        return step + steps * (1 - side if flip else side)

    def wide(step, core_ref):
        return (0, chunk(step, core_ref))

    def deep(step, core_ref):
        return (0, 0, chunk(step, core_ref))

    fixed = lambda step, core_ref: (0, 0)
    return pl.pallas_call(
        feed_back,
        grid_spec=pltpu.PrefetchScalarGridSpec(
            num_scalar_prefetch=1,
            grid=(steps,),
            in_specs=[
                pl.BlockSpec((rows, width), fixed),
                pl.BlockSpec((rows, width), fixed),
                pl.BlockSpec((rows, FEED), wide),
                pl.BlockSpec((rows, FEED), wide),
                pl.BlockSpec((1, width, FEED), deep),
                pl.BlockSpec((1, width, FEED), deep),
            ],
            out_specs=[
                pl.BlockSpec((rows, width), fixed),
                pl.BlockSpec((2, width, FEED), lambda step, core_ref: (0, 0, step)),
                pl.BlockSpec((8, FEED), lambda step, core_ref: (0, step)),
            ],
            scratch_shapes=[pltpu.VMEM((width, rows), low)] * 2,
        ),
        out_shape=[
            shape_of((rows, width), jnp.float32),
            shape_of((2, width, hidden // 2), low),
            shape_of((8, hidden // 2), jnp.float32),
        ],
        compiler_params=params_of(40),
        cost_estimate=cost_of(0.02 * rows),
        name="feed_back",
    )(core, sent, x, h, slope, up, down)


def adam_update(weight, moment_one, moment_two, average, grad, clip, rate):
    clipped = grad * clip
    new_one = beta_one * moment_one + (1.0 - beta_one) * clipped
    new_two = beta_two * moment_two + (1.0 - beta_two) * clipped * clipped
    direction = (
        new_one / (1.0 - beta_one**STEP) / (jnp.sqrt(new_two / (1.0 - beta_two**STEP)) + adam_eps)
    )
    new_weight = weight - rate * (direction + weight_decay * weight)
    new_average = ema_decay * average + (1.0 - ema_decay) * new_weight
    return (new_weight, new_one, new_two, new_average)


def local(
    lang,
    vis,
    word_mask,
    region_count,
    cot_lang,
    cot_vis,
    attn_w,
    attn_m,
    attn_v,
    attn_ema,
    ffn_w,
    ffn_m,
    ffn_v,
    ffn_ema,
    gains,
    gains_m,
    gains_v,
    gains_ema,
    biases,
    biases_m,
    biases_v,
    biases_ema,
    bias_up,
    bias_up_m,
    bias_up_v,
    bias_up_ema,
):
    core_index = lax.axis_index("mp")
    items, words, regions = lang.shape[0], lang.shape[1], vis.shape[1]
    width = lang.shape[2]
    model_share = gains.shape[1]
    hidden_share = bias_up.shape[1]
    small_own = jnp.concatenate([gains.reshape(-1), biases.reshape(-1), bias_up.reshape(-1)])
    small_size = small_own.shape[0]
    padded = -(-small_size // 1024) * 1024
    staged = lax.axis_size("dp") == CHIPS
    cuts = (5 * model_share, 21 * model_share)

    def spread(columns, count):
        parts = columns.reshape(columns.shape[0], count, -1)
        return parts.transpose(1, 0, 2).reshape(count, -1)

    attn_low = attn_w.astype(low)
    ffn_low = ffn_w.astype(low)
    share, columns = attn_w.shape[2:]
    if staged:
        terms = three_terms(small_own).reshape(-1)
        tall = -(-terms.shape[0] // (16 * columns)) * 16
        terms = jnp.pad(terms, (0, tall * columns - terms.shape[0])).reshape(tall, columns)
        own = jnp.concatenate([attn_low[0].reshape(-1, columns), terms])[None]
    else:
        own = attn_low[0]
    first, second, third, fourth = [
        Gather(own),
        Gather(attn_low[1:].reshape((-1,) + attn_low.shape[2:])),
        Gather(ffn_low[0]),
        Gather(ffn_low[1]),
    ]
    first.near()
    second.near(first.last)
    first.inner()
    third.near(first.last)
    second.inner(first.last)
    first.outer()
    fourth.near(first.last)
    first.sides()
    second.outer(first.four)
    third.inner(second.last)
    third.outer(second.last)
    fourth.inner(third.mid)
    first.corner()
    second.sides(first.last)
    first.most()
    first.rest()
    cross_mats = first.finish([(0, 4)], share)
    if staged:
        arrived = widen(first.below).reshape(CHIPS, -1)
        arrived = arrived[:, : 3 * small_size].reshape(CHIPS, 3, small_size)
        small_all = arrived[:, 0] + arrived[:, 1] + arrived[:, 2]
    else:
        small_all = lax.all_gather(small_own, "dp", axis=0, tiled=False)
    gain_all = spread(small_all[:, : cuts[0]], 5)
    bias_all = spread(small_all[:, cuts[0] : cuts[1]], 16)
    up_all = spread(small_all[:, cuts[1] : small_size], 2)

    core = core_index.astype(jnp.int32).reshape(1)
    slots = (words, regions)
    groups = items // GROUP
    sizes = (words * GROUP, regions * GROUP)
    counts = (words * items, regions * items)
    word_live = word_mask.astype(jnp.float32)
    region_live = (jnp.arange(regions)[None, :] < region_count[:, None]).astype(jnp.float32)
    live = [word_live.reshape(-1, 1), region_live.reshape(-1, 1)]
    key_bias = [(part - 1.0) * -mask_fill for part in live]
    key_all = jnp.concatenate(key_bias)
    x_all = jnp.concatenate([lang.reshape(-1, width), vis.reshape(-1, width)])
    cots = [cot_lang.reshape(-1, width), cot_vis.reshape(-1, width)]

    def same_item(asked, asking):
        rows = jnp.arange(sizes[asked])[:, None] // slots[asked]
        columns = jnp.arange(sizes[asking])[None, :] // slots[asking]
        return jnp.where(rows == columns, 0.0, mask_fill).astype(jnp.float32)

    cross_plan = layer_plan(0, sizes, groups, 1)
    cross_same = [same_item(1, 0), same_item(0, 1)]
    gains_first = after(gain_all, second.last, third.four, fourth.mid)
    cross_kept, unit_one, scale_one, low_one = run_front(
        cross_plan, x_all, None, cross_mats, gains_first, bias_all, key_all, cross_same
    )
    second.corner()
    third.sides(second.by_x if staged else second.last)
    fourth.outer()
    window = (scale_one, second.last, third.last, fourth.last)
    second.most(*window)
    second.rest(*window)
    self_mats = second.finish([(0, 4), (4, 4)], share)
    third.corner(*window)
    fourth.sides(*window)
    fronts_gate = (fourth.four,) if staged else ()
    self_plans = [layer_plan(1 + stream, (sizes[stream],), groups, 1) for stream in range(2)]
    self_same = [[same_item(stream, stream)] for stream in range(2)]
    yx, xy = (2, 1, 8, 4), (1, 2, 8, 4)

    def go_up(stream):
        kept, unit, scale, lowered = run_front(
            self_plans[stream],
            low_one[stream],
            unit_one[stream],
            [self_mats[stream]],
            after(gain_all, *fronts_gate),
            bias_all,
            key_bias[stream],
            self_same[stream],
        )
        return kept, unit[0], scale[0], lowered[0]

    def go_feed(stream, made, gate):
        return run_up(stream, made[3], mats_of[stream][0], after(up_all, *gate))

    def go_down(stream, made, up):
        out, grad, sent, small = run_down(
            stream,
            up[0],
            mats_of[stream][1],
            gain_all,
            bias_all,
            made[1],
            cots[stream],
            live[stream],
        )
        return out.reshape(items, slots[stream], width), grad, sent, small

    def go_feed_back(flip, stream, made, up, down, gate):
        return run_feed_back(
            after(core, *gate), flip, down[2], made[3], *up, *mats_of[stream]
        )

    def go_back(stream, made, down, feed, gate):
        return run_back(
            self_plans[stream],
            after(core, *gate),
            [[down[1], feed[0], feed[1]]],
            [made[1]],
            [made[2]],
            low_one[stream],
            [self_mats[stream]],
            gain_all,
            key_bias[stream],
            self_same[stream],
            made[0],
        )

    region_made = go_up(1)
    word_made = go_up(0)
    window = (word_made[2], region_made[2], third.last, fourth.last)
    third.most(*window)
    third.rest(*window)
    fourth.corner(*window)
    word_mats = third.finish([(0, 1), (1, 1)], share)
    mats_of = [word_mats]
    word_up = go_feed(0, word_made, ())
    word_down = go_down(0, word_made, word_up)
    corners = fourth.last
    word_far = go_feed_back(True, 0, word_made, word_up, word_down, (corners,))
    word_ring = Scatter(word_far[1])
    word_own = go_feed_back(False, 0, word_made, word_up, word_down, (word_far[2],))
    word_ring.add(word_own[1], True)
    fourth.most(word_own[2])
    fourth.rest(word_own[2])
    mats_of.append(fourth.finish([(0, 1), (1, 1)], share))
    word_back = go_back(
        0, word_made, word_down, (word_far[0], word_own[0]), (word_ring.last, corners)
    )
    word_ring.side(1)
    word_self_ring = Scatter(word_back[2][0])
    region_up = go_feed(1, region_made, (word_self_ring.last,))
    word_self_ring.add(word_back[1][0], True)
    region_down = go_down(1, region_made, region_up)
    window = (region_down[3], word_ring.raw)
    region_far = go_feed_back(True, 1, region_made, region_up, region_down, (word_ring.raw,))
    word_ring.side(2, *window)
    word_self_ring.side(1, *window)
    region_ring = Scatter(region_far[1])
    region_own = go_feed_back(
        False, 1, region_made, region_up, region_down, (region_far[2],)
    )
    region_ring.add(region_own[1], True)
    region_back = go_back(
        1, region_made, region_down, (region_far[0], region_own[0]), (region_ring.last,)
    )
    window = (region_own[2], word_ring.raw, word_self_ring.raw)
    region_ring.side(1, *window)
    word_self_ring.side(2, *window)
    word_ring.join(word_self_ring)
    word_ring.outer(region_back[3])
    region_self_ring = Scatter(region_back[2][0], region_ring.raw + word_self_ring.raw)
    swapped = region_self_ring.arrived
    region_self_ring.add(region_back[1][0], True)
    units, mine, other, cross_small, pieces = run_back(
        cross_plan,
        after(core, region_self_ring.last),
        [[word_back[0][0]], [region_back[0][0]]],
        unit_one,
        scale_one,
        x_all,
        cross_mats,
        gain_all,
        key_all,
        cross_same,
        cross_kept,
    )
    region_ring.side(2, swapped)
    region_self_ring.side(1)
    cross_ring = Scatter(other[0], region_ring.raw + region_self_ring.raw)
    region_self_ring.side(2, cross_small)
    region_ring.outer(cross_small)
    word_ring.inner(cross_small)
    cross_ring.add(mine[0], True)
    grads_in = run_cross_inputs(
        cross_plan, pieces, cross_mats[0], after(units, cross_ring.last)
    )
    cross_ring.side(1)
    small_gate = (cross_ring.raw, grads_in[0])
    word_shard = word_ring.near(*small_gate)
    region_ring.inner(*small_gate)
    region_self_ring.outer(*small_gate)
    cross_ring.side(2, *small_gate)
    region_self_ring.inner()
    cross_ring.outer()
    cross_ring.inner()
    if staged:
        wide = ffn_w.shape[3] // columns * 2
        parts = [word_shard[at : at + 2] for at in range(0, wide, 2)]
        word_shard, word_self_shard = jnp.concatenate(parts, axis=-1), word_shard[wide:]
    else:
        word_self_shard = word_self_ring.near()
    attn_shard = jnp.stack([cross_ring.near(), word_self_shard, region_self_ring.near()])
    ffn_shard = jnp.stack([word_shard, region_ring.near()])
    outputs = [word_down[0], region_down[0]]
    downs = [word_down[1:], region_down[1:]]
    feeds = [(word_far, word_own), (region_far, region_own)]
    self_small = [word_back[3], region_back[3]]
    grad_lang = grads_in[0].reshape(lang.shape)
    grad_vis = grads_in[1].reshape(vis.shape)

    layers = [after(part, small_gate) for part in (cross_small, self_small[0], self_small[1])]
    gain_rows = [part[0:1] for part in layers] + [part[2][0:1] for part in downs]
    bias_rows = []
    for part in layers:
        bias_rows += [part[3:5], part[2:3]]
    bias_rows += [part[2][2:3] for part in downs]
    bias_rows += [part[1:2] for part in layers] + [part[2][1:2] for part in downs]
    up_rows = []
    for far, own in feeds:
        lines = far[2][0:1], own[2][0:1]
        up_rows.append(
            jnp.where(
                core_index == 0,
                jnp.concatenate([lines[1], lines[0]], axis=1),
                jnp.concatenate([lines[0], lines[1]], axis=1),
            )
        )

    def split(rows, share):
        rows = jnp.concatenate(rows)
        count = rows.shape[0]
        return rows.reshape(count, -1, share).transpose(1, 0, 2).reshape(-1, count * share)

    small_grad = jnp.concatenate(
        [split(gain_rows, model_share), split(bias_rows, model_share), split(up_rows, hidden_share)],
        axis=1,
    )
    small_grad = jnp.pad(small_grad, ((0, 0), (0, padded - small_size)))
    small_sum = scatter_small(small_grad.reshape(small_grad.shape[0], -1, 128)).reshape(-1)
    gains_shard = small_sum[: cuts[0]].reshape(5, model_share)
    biases_shard = small_sum[cuts[0] : cuts[1]].reshape(16, model_share)
    up_shard = small_sum[cuts[1] : small_size].reshape(2, hidden_share)
    squares = jnp.sum(attn_shard * attn_shard) + jnp.sum(ffn_shard * ffn_shard)
    squares = squares + jnp.where(core_index == 0, jnp.sum(small_sum * small_sum), 0.0)
    grad_norm = jnp.sqrt(sum_all(squares))
    clip = jnp.minimum(1.0, clip_norm / (grad_norm + 1e-06))
    attn_new = adam_update(attn_w, attn_m, attn_v, attn_ema, attn_shard, clip, rate_mats)
    ffn_new = adam_update(ffn_w, ffn_m, ffn_v, ffn_ema, ffn_shard, clip, rate_mats)
    gains_new = adam_update(gains, gains_m, gains_v, gains_ema, gains_shard, clip, rate_small)
    biases_new = adam_update(biases, biases_m, biases_v, biases_ema, biases_shard, clip, rate_small)
    up_new = adam_update(bias_up, bias_up_m, bias_up_v, bias_up_ema, up_shard, clip, rate_small)
    return (
        outputs[0],
        outputs[1],
        grad_lang,
        grad_vis,
        grad_norm,
        attn_new[0],
        attn_new[1],
        attn_new[2],
        attn_new[3],
        ffn_new[0],
        ffn_new[1],
        ffn_new[2],
        ffn_new[3],
        gains_new[0],
        gains_new[1],
        gains_new[2],
        gains_new[3],
        biases_new[0],
        biases_new[1],
        biases_new[2],
        biases_new[3],
        up_new[0],
        up_new[1],
        up_new[2],
        up_new[3],
    )


def solution(mesh):
    return jax.shard_map(
        local,
        mesh=mesh,
        in_specs=(
            P(("dp", "mp"), None, None),
            P(("dp", "mp"), None, None),
            P(("dp", "mp"), None),
            P(("dp", "mp")),
            P(("dp", "mp"), None, None),
            P(("dp", "mp"), None, None),
            P(None, None, "dp", "mp"),
            P(None, None, "dp", "mp"),
            P(None, None, "dp", "mp"),
            P(None, None, "dp", "mp"),
            P(None, None, "dp", "mp"),
            P(None, None, "dp", "mp"),
            P(None, None, "dp", "mp"),
            P(None, None, "dp", "mp"),
            P(None, "dp"),
            P(None, "dp"),
            P(None, "dp"),
            P(None, "dp"),
            P(None, "dp"),
            P(None, "dp"),
            P(None, "dp"),
            P(None, "dp"),
            P(None, "dp"),
            P(None, "dp"),
            P(None, "dp"),
            P(None, "dp"),
        ),
        out_specs=(
            P(("dp", "mp"), None, None),
            P(("dp", "mp"), None, None),
            P(("dp", "mp"), None, None),
            P(("dp", "mp"), None, None),
            P(),
            P(None, None, "dp", "mp"),
            P(None, None, "dp", "mp"),
            P(None, None, "dp", "mp"),
            P(None, None, "dp", "mp"),
            P(None, None, "dp", "mp"),
            P(None, None, "dp", "mp"),
            P(None, None, "dp", "mp"),
            P(None, None, "dp", "mp"),
            P(None, "dp"),
            P(None, "dp"),
            P(None, "dp"),
            P(None, "dp"),
            P(None, "dp"),
            P(None, "dp"),
            P(None, "dp"),
            P(None, "dp"),
            P(None, "dp"),
            P(None, "dp"),
            P(None, "dp"),
            P(None, "dp"),
        ),
        check_vma=False,
    )
```

```python
import functools
import math
import jax
import jax.numpy as jnp
from jax import lax
from jax.experimental import pallas as pl
from jax.experimental.pallas import tpu as pltpu
from jax.sharding import PartitionSpec as P

HEAD_DIM = 64
STEP = 7


norm_eps = 1e-12
mask_fill = -1000000000.0
beta_one = 0.5
beta_two = 0.6
ema_decay = 0.5
adam_eps = 1e-08
weight_decay = 0.01
rate_mats = 0.02
rate_small = 0.2
clip_norm = 1.0

GROUP = 4
low = jnp.bfloat16
LINE = 4
CHIPS = 16
PAIR = 2 * HEAD_DIM
TILE = 256
CHUNK = 64
FEED = 1536
FEED_ROWS = 64
BELL = (2.0 * math.pi) ** -0.5
COST_SCALE = 0.05
HEAD_SCALE = HEAD_DIM ** (-0.5)
SQRT_HALF = 0.5**0.5


def moves(target):
    pairs = []
    for z in range(LINE):
        for y in range(2):
            for x in range(2):
                there = target(z, y, x)
                if there is not None:
                    pairs.append((z * 4 + y * 2 + x, there[0] * 4 + there[1] * 2 + there[2]))
    return pairs


routes = {
    1: moves(lambda z, y, x: (z, y, 1 - x)),
    2: moves(lambda z, y, x: (z, 1 - y, x)),
    4: moves(lambda z, y, x: (z ^ 1, y, x)),
    8: moves(lambda z, y, x: (z ^ 2, y, x)),
}
middle = moves(lambda z, y, x: (3 - z, y, x) if z in (1, 2) else None)
inwards = moves(lambda z, y, x: (z ^ 1, y, x) if z in (0, 3) else None)
outwards = moves(lambda z, y, x: (z ^ 1, y, x) if z in (1, 2) else None)


def send(values, bit):
    return lax.ppermute(values, "dp", routes[bit])


def swap_cores(values):
    return lax.ppermute(values, "mp", [(0, 1), (1, 0)])


def widen(values):
    return values.astype(jnp.float32)


def pick(values, axis, index):
    return lax.dynamic_index_in_dim(values, index, axis, keepdims=False)


def bit_of(bit):
    return (lax.axis_index("dp") // bit) % 2


def after(values, *others):
    return lax.optimization_barrier((values,) + others)[0]


def assemble_kernel(places, spans, rows, place_ref, *refs):
    pieces, wholes, sem = refs[: len(places)], refs[len(places) : -1], refs[-1]
    columns = pieces[0].shape[3]
    below = wholes[len(spans)] if len(wholes) > len(spans) else None
    copies = []
    for piece, (first, other) in zip(pieces, places):
        for number in range(piece.shape[0]):
            row = pl.ds(pl.multiple_of(place_ref[first + number] * rows, 16), rows)
            column = pl.ds(pl.multiple_of((place_ref[CHIPS] ^ other) * columns, 128), columns)
            for whole, (start, count) in zip(wholes, spans):
                if piece.shape[2] == rows:
                    pairs = [(piece.at[number, pl.ds(start, count)], whole.at[:, row, column])]
                else:
                    pairs = [
                        (piece.at[number, 0, pl.ds(at * rows, rows)], whole.at[at, row, column])
                        for at in range(start, start + count)
                    ]
                copies += [pltpu.make_async_copy(here, there, sem) for here, there in pairs]
            if below is not None and not other:
                rest = pl.ds(piece.shape[2] - below.shape[1], below.shape[1])
                copies.append(
                    pltpu.make_async_copy(
                        piece.at[number, 0, rest], below.at[place_ref[first + number]], sem
                    )
                )
    for copy in copies:
        copy.start()
    for copy in copies:
        copy.wait()


def assemble(pieces, places, spans, rows, place):
    columns = pieces[0].shape[3]
    outs = [shape_of((count, rows * CHIPS, columns * 2), low) for _, count in spans]
    below = pieces[0].shape[2] - rows * sum(count for _, count in spans)
    if pieces[0].shape[2] != rows:
        outs.append(shape_of((CHIPS, below, columns), low))
    return pl.pallas_call(
        functools.partial(assemble_kernel, places, spans, rows),
        out_shape=outs,
        in_specs=[pl.BlockSpec(memory_space=pltpu.SMEM)]
        + [pl.BlockSpec(memory_space=pl.ANY)] * len(pieces),
        out_specs=vmem(len(outs)),
        scratch_shapes=[pltpu.SemaphoreType.DMA],
        compiler_params=params_of(24),
        cost_estimate=cost_of(3),
        name="assemble",
    )(place, *pieces)


class Gather:
    def __init__(self, own):
        self.staged = lax.axis_size("dp") == CHIPS
        self.own = own[None]
        self.last = self.pair = self.mid = self.four = self.own

    def near(self, *gate):
        if self.staged:
            own = after(self.own, *gate) if gate else self.own
            self.pair = self.last = jnp.concatenate([self.own, send(own, 4)])

    def inner(self, *gate):
        if self.staged:
            self.mid = self.last = lax.ppermute(after(self.pair, *gate), "dp", middle)

    def outer(self, *gate):
        if self.staged:
            out = lax.ppermute(after(self.mid, *gate), "dp", outwards)
            self.four = self.last = jnp.concatenate([self.pair, self.mid + out])

    def sides(self, *gate):
        if self.staged:
            four = after(self.four, *gate)
            self.by_x, self.by_y = send(four, 1), send(four, 2)
            self.last = (self.by_x, self.by_y)

    def corner(self, *gate):
        if self.staged:
            by_x, by_y = after((self.by_x[:2], self.by_y[2:]), *gate)
            self.corners = send(by_x, 2), send(by_y, 1)
            self.last = self.corners

    def most(self, *gate):
        if self.staged:
            parts = jnp.concatenate([self.four, self.by_x, self.by_y])
            self.major = (parts, swap_cores(after(parts, *gate)))
            self.last = self.major[1]

    def rest(self, *gate):
        if self.staged:
            parts = jnp.concatenate(self.corners)
            self.minor = (parts, swap_cores(after(parts, *gate)))
            self.last = self.minor[1]

    def place(self):
        chip = lax.axis_index("dp")
        z = chip // 4
        far = jnp.where((z == 1) | (z == 2), 12, 8)
        four = jnp.stack([chip, chip ^ 4, chip ^ far, chip ^ far ^ 4])
        return jnp.concatenate(
            [four, four ^ 1, four ^ 2, four ^ 3, lax.axis_index("mp").reshape(1)]
        ).astype(jnp.int32)

    def finish(self, spans, rows):
        if not self.staged:
            whole = lax.all_gather(self.own[0], "dp", axis=1, tiled=True)
            whole = lax.all_gather(whole, "mp", axis=2, tiled=True)
            return [whole[start : start + count] for start, count in spans]
        pieces, places = [], []
        for pair, first in zip((self.major, self.minor), (0, 12)):
            pieces += pair
            places += [(first, 0), (first, 1)]
        made = assemble(pieces, places, spans, rows, self.place())
        self.below = made[-1]
        return made[: len(spans)]


class Scatter:
    def __init__(self, other, gate=()):
        self.staged = lax.axis_size("dp") == CHIPS
        self.raw = []
        self.arrived = self.last = swap_cores(after(other, *gate))

    def add(self, mine, split):
        self.total = widen(mine) + widen(self.arrived)
        if self.staged:
            total = self.total.astype(low)
            total = total.reshape((-1, 4, 2, 2, total.shape[1] // CHIPS, total.shape[2]))
            count = total.shape[0]
            self.parts = [total[: count // 2], total[count // 2 :]] if split else [total]
            self.last = self.parts

    def side(self, bit, *gate):
        if not self.staged:
            return
        parts, self.raw = [], []
        for part, way in zip(self.parts, (bit, 3 - bit)):
            axis = 2 if way == 2 or part.ndim == 5 else 3
            kept = pick(part, axis, bit_of(way))
            arrived = send(after(pick(part, axis, 1 - bit_of(way)), *gate), way)
            self.raw.append(arrived)
            parts.append((widen(kept) + widen(arrived)).astype(low))
        if parts[0].ndim == 4:
            whole = parts[0] if len(parts) == 1 else jnp.concatenate(parts)
            whole = whole.reshape((whole.shape[0], 2, 2) + whole.shape[2:])
            self.own = pick(whole, 1, bit_of(8))
            self.far = pick(whole, 1, 1 - bit_of(8))
            self.last = (self.own, self.far)
        else:
            self.parts = self.last = parts

    def join(self, narrow):
        if self.staged:
            columns = narrow.own.shape[-1]

            def cut(values):
                return [values[..., at : at + columns] for at in range(0, values.shape[-1], columns)]

            self.own = jnp.concatenate(cut(self.own) + [narrow.own])
            self.far = jnp.concatenate(cut(self.far) + [narrow.far])
            self.last = (self.own, self.far)

    def outer(self, *gate):
        if self.staged:
            arrived = lax.ppermute(after(self.far, *gate), "dp", inwards)
            self.far = self.last = (widen(self.far) + widen(arrived)).astype(low)

    def inner(self, *gate):
        if self.staged:
            arrived = lax.ppermute(after(self.far, *gate), "dp", middle)
            self.own = self.last = (widen(self.own) + widen(arrived)).astype(low)

    def near(self, *gate):
        if not self.staged:
            return lax.psum_scatter(self.total, "dp", scatter_dimension=1, tiled=True)
        arrived = send(after(pick(self.own, 1, 1 - bit_of(4)), *gate), 4)
        return widen(pick(self.own, 1, bit_of(4))) + widen(arrived)


def three_terms(values):
    terms = []
    for _ in range(3):
        terms.append(values.astype(low))
        values = values - lax.reduce_precision(values, 8, 7)
    return jnp.stack(terms)


def scatter_small(values):
    values = values + swap_cores(values)
    if lax.axis_size("dp") != CHIPS:
        return lax.psum_scatter(values, "dp", scatter_dimension=0, tiled=True)[0]
    for bit in (8, 4, 2, 1):
        half = values.shape[0] // 2
        at_zero = bit_of(bit) == 0
        kept = jnp.where(at_zero, values[:half], values[half:])
        sent = jnp.where(at_zero, values[half:], values[:half])
        values = kept + send(sent, bit)
    return values[0]


def sum_all(value):
    if lax.axis_size("dp") != CHIPS:
        return lax.psum(value, ("dp", "mp"))
    value = value.reshape(1, 1)
    value = value + swap_cores(value)
    for bit in (1, 2, 4, 8):
        value = value + send(value, bit)
    return value[0, 0]


def dot_nn(left, right):
    return lax.dot_general(left, right, (((1,), (0,)), ((), ())), preferred_element_type=jnp.float32)


def dot_nt(left, right):
    return lax.dot_general(left, right, (((1,), (1,)), ((), ())), preferred_element_type=jnp.float32)


def dot_tn(left, right):
    return lax.dot_general(left, right, (((0,), (0,)), ((), ())), preferred_element_type=jnp.float32)


def fold_rows(values):
    return jnp.sum(values.reshape(values.shape[0] // 8, 8, values.shape[1]), axis=0)


def close_rows(values):
    return jnp.sum(values, axis=0, keepdims=True)


def norm_rows(summed, gain, shift):
    average = jnp.mean(summed, axis=-1, keepdims=True)
    centered = summed - average
    inverse = lax.rsqrt(jnp.mean(centered * centered, axis=-1, keepdims=True) + norm_eps)
    normed = centered * inverse
    return normed * gain + shift, normed, inverse


def norm_rows_back(grad_out, normed, inverse, gain):
    scaled = grad_out * gain
    return inverse * (
        scaled
        - jnp.mean(scaled, axis=-1, keepdims=True)
        - normed * jnp.mean(scaled * normed, axis=-1, keepdims=True)
    )


def stack_heads(block):
    first = lax.broadcasted_iota(jnp.int32, block.shape, 1) < HEAD_DIM
    nothing = jnp.zeros_like(block)
    return jnp.concatenate(
        [jnp.where(first, block, nothing), jnp.where(first, nothing, block)], axis=0
    )


def merge_heads(double):
    rows = double.shape[0] // 2
    first = lax.broadcasted_iota(jnp.int32, (rows, double.shape[1]), 1) < HEAD_DIM
    return jnp.where(first, double[:rows], double[rows:])


def pair_forward(queries, keys, values, bias):
    count = keys.shape[0]
    scores = dot_nt(stack_heads(keys), queries * HEAD_SCALE)
    weights, totals = [], []
    for part in (scores[:count] + bias, scores[count:] + bias):
        top = jnp.max(part, axis=0, keepdims=True)
        powers = jnp.exp(part - top)
        total = jnp.sum(powers, axis=0, keepdims=True)
        weights.append((powers * (1.0 / total)).astype(low))
        totals.append(top + jnp.log(total))
    context = dot_tn(jnp.concatenate(weights, axis=0), stack_heads(values))
    return context.astype(low), totals


def pair_backward(queries, keys, values, grad, bias, totals):
    count = keys.shape[0]
    both_keys = stack_heads(keys)
    queries = queries * HEAD_SCALE
    scores = dot_nt(both_keys, queries)
    sensed = dot_nt(stack_heads(values), grad)
    weights, slopes = [], []
    for part, sense, total in (
        (scores[:count], sensed[:count], totals[0]),
        (scores[count:], sensed[count:], totals[1]),
    ):
        weight = jnp.exp(part + bias - total)
        inner = jnp.sum(sense * weight, axis=0, keepdims=True)
        weights.append(weight.astype(low))
        slopes.append((weight * (sense - inner)).astype(low))
    weights = jnp.concatenate(weights, axis=0)
    slopes = jnp.concatenate(slopes, axis=0)
    grad_queries = (dot_tn(slopes, both_keys) * HEAD_DIM ** (-0.5)).astype(low)
    grad_keys = merge_heads(dot_nn(slopes, queries)).astype(low)
    grad_values = merge_heads(dot_nn(weights, grad)).astype(low)
    return grad_queries, grad_keys, grad_values


def tiles_of(width):
    return [(at, min(TILE, width - at)) for at in range(0, width, TILE)]


def row_block(start, size, step):
    return pl.ds(pl.multiple_of(start + step * size, 16), size)


def attend_front(plan, *refs):
    streams, relations, cross = plan["streams"], plan["relations"], plan["cross"]
    refs = list(refs)

    def take(count):
        taken = refs[:count]
        del refs[:count]
        return taken

    (x_ref,) = take(1)
    before = [] if cross else take(1)
    mats = take(plan["mats"])
    gain_ref, bias_ref, key_ref = take(3)
    same = take(len(relations))
    q_ref, k_ref, v_ref, ctx_ref = take(4)
    logs = take(len(relations))
    normed = take(len(streams))
    inverse = take(len(streams))
    lowered = take(len(streams))
    (acc_ref,) = take(1)
    width = x_ref.shape[1]
    weights = [mats[i // (4 // len(mats))].at[i % (4 // len(mats))] for i in range(4)]
    rows = x_ref[...]
    for target, weight, row in ((q_ref, 0, 0), (k_ref, 1, None), (v_ref, 2, 1)):
        for at, size in tiles_of(width):
            part = dot_nn(rows, weights[weight][:, at : at + size])
            if row is not None:
                line = plan["rows"][row]
                part = part + bias_ref[line : line + 1, at : at + size]
            target[:, at : at + size] = part.astype(low)
    pairs = width // PAIR
    groups = plan["groups"]

    def one_group(group, carry):
        for which, (asking, asked) in enumerate(relations):
            ask = row_block(*streams[asking], group)
            key = row_block(*streams[asked], group)
            bias = same[which][...] + key_ref[key, :]
            for pair in range(pairs):
                lanes = slice(pair * PAIR, (pair + 1) * PAIR)
                context, totals = pair_forward(
                    q_ref[ask, lanes], k_ref[key, lanes], v_ref[key, lanes], bias
                )
                ctx_ref[ask, lanes] = context
                for side in range(2):
                    logs[which][group * (2 * pairs) + 2 * pair + side] = totals[side]
        return carry

    lax.fori_loop(0, groups, one_group, 0)
    context = ctx_ref[...]
    for at, size in tiles_of(width):
        acc_ref[:, at : at + size] = dot_nt(context, weights[3][at : at + size, :])
    gain = gain_ref[plan["gain"] : plan["gain"] + 1, :]
    shift = bias_ref[plan["shift"] : plan["shift"] + 1, :]
    out_bias = bias_ref[plan["rows"][2] : plan["rows"][2] + 1, :]
    for index, (start, size) in enumerate(streams):

        def one_chunk(step, carry, start=start, index=index):
            here = row_block(start, CHUNK, step)
            there = row_block(0, CHUNK, step)
            if cross:
                base = widen(x_ref[here, :])
            else:
                last_gain, last_shift = plan["before"]
                base = (
                    before[0][here, :] * gain_ref[last_gain : last_gain + 1, :]
                    + bias_ref[last_shift : last_shift + 1, :]
                )
            value, unit, scale = norm_rows(base + acc_ref[here, :] + out_bias, gain, shift)
            normed[index][there, :] = unit
            inverse[index][there, :] = scale
            lowered[index][there, :] = value.astype(low)
            return carry

        lax.fori_loop(0, size * groups // CHUNK, one_chunk, 0)


def add_inputs(streams, groups, weights, grads, grad_in):
    dq_ref, dk_ref, dv_ref = grads
    for index, (start, size) in enumerate(streams):
        span = slice(start, start + size * groups)
        for at, wide in tiles_of(dq_ref.shape[1]):
            grad_in[index][:, at : at + wide] += (
                dot_nt(dq_ref[span, :], weights[0][at : at + wide, :])
                + dot_nt(dk_ref[span, :], weights[1][at : at + wide, :])
                + dot_nt(dv_ref[span, :], weights[2][at : at + wide, :])
            )


def cross_inputs(plan, dq_ref, dk_ref, dv_ref, mat_ref, *refs):
    streams = plan["streams"]
    grads, outs = refs[: len(streams)], refs[len(streams) :]
    for grad, out in zip(grads, outs):
        out[...] = grad[...]
    weights = [mat_ref.at[i] for i in range(3)]
    add_inputs(streams, plan["groups"], weights, (dq_ref, dk_ref, dv_ref), outs)


def attend_back(plan, *refs):
    streams, relations = plan["streams"], plan["relations"]
    refs = list(refs)

    def take(count):
        taken = refs[:count]
        del refs[:count]
        return taken

    (core_ref,) = take(1)
    carried = [take(plan["carried"]) for _ in streams]
    normed = take(len(streams))
    inverse = take(len(streams))
    (x_ref,) = take(1)
    mats = take(plan["mats"])
    gain_ref, key_ref = take(2)
    same = take(len(relations))
    q_ref, k_ref, v_ref, ctx_ref = take(4)
    logs = take(len(relations))
    grad_in = take(len(streams))
    mine = take(plan["mats"])
    other = take(plan["mats"])
    (small_ref,) = take(1)
    dq_ref, dk_ref, dv_ref = take(3)
    do_ref, dctx_ref = take(2)
    fetched = take(5 + plan["mats"])
    sems = refs[0]
    copies = [
        pltpu.make_async_copy(source, target, sems.at[number])
        for number, (source, target) in enumerate(
            zip(mats + [q_ref, k_ref, v_ref, ctx_ref, x_ref], fetched)
        )
    ]
    for copy in copies:
        copy.start()
    mats = fetched[: plan["mats"]]
    q_ref, k_ref, v_ref, ctx_ref, x_ref = fetched[plan["mats"] :]
    width = x_ref.shape[1]
    half = width // 2
    each = 4 // plan["mats"]
    weights = [mats[i // each].at[i % each] for i in range(4)]
    gain = gain_ref[plan["gain"] : plan["gain"] + 1, :]
    groups = plan["groups"]
    nothing = jnp.zeros((8, width), jnp.float32)
    sums = (nothing, nothing, nothing)
    for index, (start, size) in enumerate(streams):

        def one_chunk(step, sums, start=start, index=index):
            here = row_block(start, CHUNK, step)
            there = row_block(0, CHUNK, step)
            grad = carried[index][0][there, :]
            for more in carried[index][1:]:
                grad = grad + more[there, :]
            unit = normed[index][there, :]
            down = norm_rows_back(grad, unit, inverse[index][there, :], gain)
            sent = down.astype(low)
            grad_in[index][there, :] = down
            do_ref[here, :] = sent
            return (
                sums[0] + fold_rows(grad * unit),
                sums[1] + fold_rows(grad),
                sums[2] + fold_rows(widen(sent)),
            )

        sums = lax.fori_loop(0, size * groups // CHUNK, one_chunk, sums)
    for copy in copies:
        copy.wait()
    sent = do_ref[...]
    for at, size in tiles_of(width):
        dctx_ref[:, at : at + size] = dot_nn(sent, weights[3][:, at : at + size]).astype(low)
    pairs = width // PAIR

    def one_group(group, carry):
        for which, (asking, asked) in enumerate(relations):
            ask = row_block(*streams[asking], group)
            key = row_block(*streams[asked], group)
            bias = same[which][...] + key_ref[key, :]
            for pair in range(pairs):
                lanes = slice(pair * PAIR, (pair + 1) * PAIR)
                base = group * (2 * pairs) + 2 * pair
                grads = pair_backward(
                    q_ref[ask, lanes],
                    k_ref[key, lanes],
                    v_ref[key, lanes],
                    dctx_ref[ask, lanes],
                    bias,
                    [logs[which][base], logs[which][base + 1]],
                )
                dq_ref[ask, lanes], dk_ref[key, lanes], dv_ref[key, lanes] = grads
        return carry

    lax.fori_loop(0, groups, one_group, 0)
    at_zero = core_ref[0] == 0
    rows = x_ref[...]
    last = None
    for number, (left, right) in enumerate(
        ((rows, dq_ref), (rows, dk_ref), (rows, dv_ref), (sent, ctx_ref))
    ):
        wide = right[...]
        if left is not last:
            flipped, last = left.T, left
        for at, size in tiles_of(width):
            whole = dot_nn(flipped[at : at + size, :], wide).astype(low)
            former, latter = whole[:, :half], whole[:, half:]
            mine[number // each][number % each, at : at + size, :] = jnp.where(
                at_zero, former, latter
            )
            other[number // each][number % each, at : at + size, :] = jnp.where(
                at_zero, latter, former
            )
    if not plan["cross"]:
        add_inputs(streams, groups, weights, (dq_ref, dk_ref, dv_ref), grad_in)

    def add_chunk(step, sums):
        here = row_block(0, CHUNK, step)
        return (
            sums[0] + fold_rows(widen(dq_ref[here, :])),
            sums[1] + fold_rows(widen(dv_ref[here, :])),
        )

    more = lax.fori_loop(0, x_ref.shape[0] // CHUNK, add_chunk, (nothing, nothing))
    small_ref[...] = jnp.concatenate(
        [close_rows(part) for part in sums + more] + [jnp.zeros((3, width), jnp.float32)], axis=0
    )


def vmem(count):
    return [pl.BlockSpec(memory_space=pltpu.VMEM)] * count


def shape_of(shape, kind):
    return jax.ShapeDtypeStruct(tuple(shape), kind)


def cost_of(micros):
    return pl.CostEstimate(flops=int(micros * COST_SCALE * 1.15e9), bytes_accessed=1 << 20, transcendentals=0)


def params_of(mib):
    return pltpu.CompilerParams(vmem_limit_bytes=mib << 20)


def layer_plan(layer, sizes, groups, mats):
    if layer == 0:
        starts = (0, sizes[0] * groups)
        streams = [(starts[i], sizes[i]) for i in range(2)]
        relations, gain, shift = [(0, 1), (1, 0)], 0, 11
    else:
        streams, relations = [(0, sizes[0])], [(0, 0)]
        gain, shift = layer, 11 + layer
    return {
        "streams": streams,
        "relations": relations,
        "cross": layer == 0,
        "mats": mats,
        "groups": groups,
        "gain": gain,
        "shift": shift,
        "rows": [3 * layer, 3 * layer + 1, 3 * layer + 2],
        "before": (0, 11),
        "carried": 1 if layer == 0 else 3,
    }


def run_front(plan, x, before, mats, gains, biases, key_bias, same):
    rows, width = x.shape
    groups = plan["groups"]
    outs = [shape_of((rows, width), low)] * 4
    for asking, _ in plan["relations"]:
        outs.append(
            shape_of((groups * width // HEAD_DIM, 1, plan["streams"][asking][1]), jnp.float32)
        )
    counts = [size * groups for _, size in plan["streams"]]
    outs += [shape_of((count, width), jnp.float32) for count in counts]
    outs += [shape_of((count, 1), jnp.float32) for count in counts]
    outs += [shape_of((count, width), low) for count in counts]
    args = [x] + ([] if before is None else [before]) + list(mats) + [gains, biases, key_bias]
    args += list(same)
    results = pl.pallas_call(
        functools.partial(attend_front, plan),
        out_shape=outs,
        in_specs=vmem(len(args)),
        out_specs=vmem(len(outs)),
        scratch_shapes=[pltpu.VMEM((rows, width), jnp.float32)],
        compiler_params=params_of(48),
        cost_estimate=cost_of(0.028 * rows),
        name="attend_front",
    )(*args)
    related, many = len(plan["relations"]), len(counts)
    kept = results[: 4 + related]
    rest = results[4 + related :]
    return kept, rest[:many], rest[many : 2 * many], rest[2 * many :]


def run_back(plan, core, carried, normed, inverse, x, mats, gains, key_bias, same, kept):
    rows, width = x.shape
    counts = [size * plan["groups"] for _, size in plan["streams"]]
    grads = [shape_of(mat.shape[:2] + (width // 2,), low) for mat in mats]
    outs = [shape_of((count, width), jnp.float32) for count in counts] + grads + grads
    outs.append(shape_of((8, width), jnp.float32))
    pieces = [shape_of((rows, width), low)] * 3
    cross = plan["cross"]
    args = [part for parts in carried for part in parts] + list(normed) + list(inverse) + [x]
    args += list(mats) + [gains, key_bias] + list(same) + list(kept)
    far = [x] + list(mats) + list(kept[:4])
    specs = [pl.BlockSpec(memory_space=pltpu.SMEM)] + [
        pl.BlockSpec(memory_space=pl.ANY if any(arg is part for part in far) else pltpu.VMEM)
        for arg in args
    ]
    results = pl.pallas_call(
        functools.partial(attend_back, plan),
        out_shape=outs + (pieces if cross else []),
        in_specs=specs,
        out_specs=vmem(len(outs) + (3 if cross else 0)),
        scratch_shapes=[pltpu.VMEM((rows, width), low)] * (2 if cross else 5)
        + [pltpu.VMEM(mat.shape, low) for mat in mats]
        + [pltpu.VMEM((rows, width), low)] * 5
        + [pltpu.SemaphoreType.DMA((5 + len(mats),))],
        compiler_params=params_of(58),
        name="attend_back",
    )(core, *args)
    many, count = len(counts), len(mats)
    return (
        results[:many],
        results[many : many + count],
        results[many + count : many + 2 * count],
        results[len(outs) - 1],
        results[len(outs) :],
    )


def run_cross_inputs(plan, pieces, mat, grads):
    outs = [shape_of(grad.shape, jnp.float32) for grad in grads]
    return pl.pallas_call(
        functools.partial(cross_inputs, plan),
        out_shape=outs,
        in_specs=vmem(4 + len(grads)),
        out_specs=vmem(len(grads)),
        compiler_params=params_of(48),
        cost_estimate=cost_of(10),
        name="cross_inputs",
    )(*pieces, mat, *grads)


def feed_up(line, x_ref, mat_ref, bias_ref, h_ref, slope_ref, hidden_ref):
    bias = bias_ref[line : line + 1, :]
    hidden_ref[...] = dot_nn(x_ref[...], mat_ref[0])

    def one_chunk(step, carry):
        here = row_block(0, FEED_ROWS, step)
        hidden = hidden_ref[here, :] + bias
        share = 0.5 + 0.5 * lax.erf(hidden * SQRT_HALF)
        h_ref[here, :] = (hidden * share).astype(low)
        slope_ref[here, :] = (share + hidden * (jnp.exp(hidden * hidden * -0.5) * BELL)).astype(low)
        return carry

    lax.fori_loop(0, x_ref.shape[0] // FEED_ROWS, one_chunk, 0)


def feed_down(plan, h_ref, mat_ref, gain_ref, bias_ref, unit_ref, cot_ref, live_ref, *refs):
    out_ref, du_ref, do_ref, small_ref, acc_ref, cots_ref = refs
    step = pl.program_id(0)
    items, slots, width = out_ref.shape

    @pl.when(step == 0)
    def _():
        acc_ref[...] = jnp.zeros_like(acc_ref)
        for item in range(items):
            cots_ref[item * slots : (item + 1) * slots, :] = widen(cot_ref[item])

    rows = h_ref[...]
    for at, size in tiles_of(width):
        acc_ref[:, at : at + size] += dot_nt(rows, mat_ref[0, at : at + size, :])

    @pl.when(step == pl.num_programs(0) - 1)
    def _():
        def line(ref, row):
            return ref[row : row + 1, :]

        stream = plan
        last_gain, last_shift = line(gain_ref, 1 + stream), line(bias_ref, 12 + stream)
        gain, shift = line(gain_ref, 3 + stream), line(bias_ref, 14 + stream)
        out_bias = line(bias_ref, 9 + stream)
        nothing = jnp.zeros((8, width), jnp.float32)

        def one_chunk(chunk, sums):
            here = row_block(0, CHUNK, chunk)
            live = live_ref[here, :]
            base = unit_ref[here, :] * last_gain + last_shift
            value, unit, scale = norm_rows(base + acc_ref[here, :] + out_bias, gain, shift)
            grad = cots_ref[here, :] * live
            cots_ref[here, :] = value * live
            down = norm_rows_back(grad, unit, scale, gain)
            sent = down.astype(low)
            du_ref[here, :] = down
            do_ref[here, :] = sent
            return (
                sums[0] + fold_rows(grad * unit),
                sums[1] + fold_rows(grad),
                sums[2] + fold_rows(widen(sent)),
            )

        sums = lax.fori_loop(0, items * slots // CHUNK, one_chunk, (nothing,) * 3)
        for item in range(items):
            out_ref[item] = cots_ref[item * slots : (item + 1) * slots, :]
        small_ref[...] = jnp.concatenate(
            [close_rows(part) for part in sums] + [jnp.zeros((5, width), jnp.float32)], axis=0
        )


def feed_back(core_ref, do_ref, x_ref, h_ref, slope_ref, up_ref, down_ref, *refs):
    dx_ref, grad_ref, line_ref, sent_flip, rows_flip = refs
    step = pl.program_id(0)
    sent = do_ref[...]

    @pl.when(step == 0)
    def _():
        sent_flip[...] = sent.T
        rows_flip[...] = x_ref[...].T

    slope = (dot_nn(sent, down_ref[0]) * widen(slope_ref[...])).astype(low)
    line_ref[...] = jnp.broadcast_to(close_rows(fold_rows(widen(slope))), line_ref.shape)
    grad_ref[0] = dot_nn(rows_flip[...], slope).astype(low)
    grad_ref[1] = dot_nn(sent_flip[...], h_ref[...]).astype(low)
    part = dot_nt(slope, up_ref[0])

    @pl.when(step == 0)
    def _():
        dx_ref[...] = part

    @pl.when(step > 0)
    def _():
        dx_ref[...] += part


def run_up(stream, x, mat, biases):
    rows, width = x.shape
    hidden = mat.shape[2]
    wide = lambda step: (0, step)
    return pl.pallas_call(
        functools.partial(feed_up, stream),
        grid=(hidden // FEED,),
        out_shape=[shape_of((rows, hidden), low)] * 2,
        in_specs=[
            pl.BlockSpec((rows, width), lambda step: (0, 0)),
            pl.BlockSpec((1, width, FEED), lambda step: (0, 0, step)),
            pl.BlockSpec((2, FEED), wide),
        ],
        out_specs=[pl.BlockSpec((rows, FEED), wide)] * 2,
        scratch_shapes=[pltpu.VMEM((rows, FEED), jnp.float32)],
        compiler_params=params_of(32),
        cost_estimate=cost_of(0.033 * rows),
        name="feed_up",
    )(x, mat, biases)


def run_down(stream, h, mat, gains, biases, unit, cot, live):
    rows, hidden = h.shape
    width = unit.shape[1]
    def whole(array):
        return pl.BlockSpec(array.shape, lambda step: (0,) * len(array.shape))

    outs = [
        shape_of(cot.shape, jnp.float32),
        shape_of((rows, width), jnp.float32),
        shape_of((rows, width), low),
        shape_of((8, width), jnp.float32),
    ]
    return pl.pallas_call(
        functools.partial(feed_down, stream),
        grid=(hidden // FEED,),
        out_shape=outs,
        in_specs=[
            pl.BlockSpec((rows, FEED), lambda step: (0, step)),
            pl.BlockSpec((1, width, FEED), lambda step: (0, 0, step)),
            whole(gains),
            whole(biases),
            whole(unit),
            whole(cot),
            whole(live),
        ],
        out_specs=[whole(out) for out in outs],
        scratch_shapes=[pltpu.VMEM((rows, width), jnp.float32)] * 2,
        compiler_params=params_of(40),
        cost_estimate=cost_of(0.022 * rows),
        name="feed_down",
    )(h, mat, gains, biases, unit, cot, live)


def run_feed_back(core, flip, sent, x, h, slope, up, down):
    rows, hidden = h.shape
    width = x.shape[1]
    steps = hidden // FEED // 2

    def chunk(step, core_ref):
        side = core_ref[0]
        return step + steps * (1 - side if flip else side)

    def wide(step, core_ref):
        return (0, chunk(step, core_ref))

    def deep(step, core_ref):
        return (0, 0, chunk(step, core_ref))

    fixed = lambda step, core_ref: (0, 0)
    return pl.pallas_call(
        feed_back,
        grid_spec=pltpu.PrefetchScalarGridSpec(
            num_scalar_prefetch=1,
            grid=(steps,),
            in_specs=[
                pl.BlockSpec((rows, width), fixed),
                pl.BlockSpec((rows, width), fixed),
                pl.BlockSpec((rows, FEED), wide),
                pl.BlockSpec((rows, FEED), wide),
                pl.BlockSpec((1, width, FEED), deep),
                pl.BlockSpec((1, width, FEED), deep),
            ],
            out_specs=[
                pl.BlockSpec((rows, width), fixed),
                pl.BlockSpec((2, width, FEED), lambda step, core_ref: (0, 0, step)),
                pl.BlockSpec((8, FEED), lambda step, core_ref: (0, step)),
            ],
            scratch_shapes=[pltpu.VMEM((width, rows), low)] * 2,
        ),
        out_shape=[
            shape_of((rows, width), jnp.float32),
            shape_of((2, width, hidden // 2), low),
            shape_of((8, hidden // 2), jnp.float32),
        ],
        compiler_params=params_of(40),
        cost_estimate=cost_of(0.02 * rows),
        name="feed_back",
    )(core, sent, x, h, slope, up, down)


def adam_update(weight, moment_one, moment_two, average, grad, clip, rate):
    clipped = grad * clip
    new_one = beta_one * moment_one + (1.0 - beta_one) * clipped
    new_two = beta_two * moment_two + (1.0 - beta_two) * clipped * clipped
    direction = (
        new_one / (1.0 - beta_one**STEP) / (jnp.sqrt(new_two / (1.0 - beta_two**STEP)) + adam_eps)
    )
    new_weight = weight - rate * (direction + weight_decay * weight)
    new_average = ema_decay * average + (1.0 - ema_decay) * new_weight
    return (new_weight, new_one, new_two, new_average)


def local(
    lang,
    vis,
    word_mask,
    region_count,
    cot_lang,
    cot_vis,
    attn_w,
    attn_m,
    attn_v,
    attn_ema,
    ffn_w,
    ffn_m,
    ffn_v,
    ffn_ema,
    gains,
    gains_m,
    gains_v,
    gains_ema,
    biases,
    biases_m,
    biases_v,
    biases_ema,
    bias_up,
    bias_up_m,
    bias_up_v,
    bias_up_ema,
):
    core_index = lax.axis_index("mp")
    items, words, regions = lang.shape[0], lang.shape[1], vis.shape[1]
    width = lang.shape[2]
    model_share = gains.shape[1]
    hidden_share = bias_up.shape[1]
    small_own = jnp.concatenate([gains.reshape(-1), biases.reshape(-1), bias_up.reshape(-1)])
    small_size = small_own.shape[0]
    padded = -(-small_size // 1024) * 1024
    staged = lax.axis_size("dp") == CHIPS
    cuts = (5 * model_share, 21 * model_share)

    def spread(columns, count):
        parts = columns.reshape(columns.shape[0], count, -1)
        return parts.transpose(1, 0, 2).reshape(count, -1)

    attn_low = attn_w.astype(low)
    ffn_low = ffn_w.astype(low)
    share, columns = attn_w.shape[2:]
    if staged:
        terms = three_terms(small_own).reshape(-1)
        tall = -(-terms.shape[0] // (16 * columns)) * 16
        terms = jnp.pad(terms, (0, tall * columns - terms.shape[0])).reshape(tall, columns)
        own = jnp.concatenate([attn_low[0].reshape(-1, columns), terms])[None]
    else:
        own = attn_low[0]
    first, second, third, fourth = [
        Gather(own),
        Gather(attn_low[1:].reshape((-1,) + attn_low.shape[2:])),
        Gather(ffn_low[0]),
        Gather(ffn_low[1]),
    ]
    first.near()
    second.near(first.last)
    first.inner()
    third.near(first.last)
    second.inner(first.last)
    first.outer()
    fourth.near(first.last)
    first.sides()
    second.outer(first.four)
    third.inner(second.last)
    third.outer(second.last)
    fourth.inner(third.mid)
    first.corner()
    second.sides(first.last)
    first.most()
    first.rest()
    cross_mats = first.finish([(0, 4)], share)
    if staged:
        arrived = widen(first.below).reshape(CHIPS, -1)
        arrived = arrived[:, : 3 * small_size].reshape(CHIPS, 3, small_size)
        small_all = arrived[:, 0] + arrived[:, 1] + arrived[:, 2]
    else:
        small_all = lax.all_gather(small_own, "dp", axis=0, tiled=False)
    gain_all = spread(small_all[:, : cuts[0]], 5)
    bias_all = spread(small_all[:, cuts[0] : cuts[1]], 16)
    up_all = spread(small_all[:, cuts[1] : small_size], 2)

    core = core_index.astype(jnp.int32).reshape(1)
    slots = (words, regions)
    groups = items // GROUP
    sizes = (words * GROUP, regions * GROUP)
    counts = (words * items, regions * items)
    word_live = word_mask.astype(jnp.float32)
    region_live = (jnp.arange(regions)[None, :] < region_count[:, None]).astype(jnp.float32)
    live = [word_live.reshape(-1, 1), region_live.reshape(-1, 1)]
    key_bias = [(part - 1.0) * -mask_fill for part in live]
    key_all = jnp.concatenate(key_bias)
    x_all = jnp.concatenate([lang.reshape(-1, width), vis.reshape(-1, width)])
    cots = [cot_lang, cot_vis]

    def same_item(asked, asking):
        rows = jnp.arange(sizes[asked])[:, None] // slots[asked]
        columns = jnp.arange(sizes[asking])[None, :] // slots[asking]
        return jnp.where(rows == columns, 0.0, mask_fill).astype(jnp.float32)

    cross_plan = layer_plan(0, sizes, groups, 1)
    cross_same = [same_item(1, 0), same_item(0, 1)]
    gains_first = after(gain_all, second.last, third.four, fourth.mid)
    cross_kept, unit_one, scale_one, low_one = run_front(
        cross_plan, x_all, None, cross_mats, gains_first, bias_all, key_all, cross_same
    )
    second.corner()
    third.sides(second.by_x if staged else second.last)
    fourth.outer()
    window = (scale_one, second.last, third.last, fourth.last)
    second.most(*window)
    second.rest(*window)
    self_mats = second.finish([(0, 4), (4, 4)], share)
    third.corner(*window)
    fourth.sides(*window)
    fronts_gate = (fourth.four,) if staged else ()
    self_plans = [layer_plan(1 + stream, (sizes[stream],), groups, 1) for stream in range(2)]
    self_same = [[same_item(stream, stream)] for stream in range(2)]
    yx, xy = (2, 1, 8, 4), (1, 2, 8, 4)

    def go_up(stream):
        kept, unit, scale, lowered = run_front(
            self_plans[stream],
            low_one[stream],
            unit_one[stream],
            [self_mats[stream]],
            after(gain_all, *fronts_gate),
            bias_all,
            key_bias[stream],
            self_same[stream],
        )
        return kept, unit[0], scale[0], lowered[0]

    def go_feed(stream, made, gate):
        return run_up(stream, made[3], mats_of[stream][0], after(up_all, *gate))

    def go_down(stream, made, up):
        out, grad, sent, small = run_down(
            stream,
            up[0],
            mats_of[stream][1],
            gain_all,
            bias_all,
            made[1],
            cots[stream],
            live[stream],
        )
        return out, grad, sent, small

    def go_feed_back(flip, stream, made, up, down, gate):
        return run_feed_back(
            after(core, *gate), flip, down[2], made[3], *up, *mats_of[stream]
        )

    def go_back(stream, made, down, feed, gate):
        return run_back(
            self_plans[stream],
            after(core, *gate),
            [[down[1], feed[0], feed[1]]],
            [made[1]],
            [made[2]],
            low_one[stream],
            [self_mats[stream]],
            gain_all,
            key_bias[stream],
            self_same[stream],
            made[0],
        )

    region_made = go_up(1)
    word_made = go_up(0)
    window = (word_made[2], region_made[2], third.last, fourth.last)
    third.most(*window)
    third.rest(*window)
    fourth.corner(*window)
    word_mats = third.finish([(0, 1), (1, 1)], share)
    mats_of = [word_mats]
    word_up = go_feed(0, word_made, ())
    word_down = go_down(0, word_made, word_up)
    corners = fourth.last
    word_far = go_feed_back(True, 0, word_made, word_up, word_down, (corners,))
    word_ring = Scatter(word_far[1])
    word_own = go_feed_back(False, 0, word_made, word_up, word_down, (word_far[2],))
    word_ring.add(word_own[1], True)
    fourth.most(word_own[2])
    fourth.rest(word_own[2])
    mats_of.append(fourth.finish([(0, 1), (1, 1)], share))
    word_back = go_back(
        0, word_made, word_down, (word_far[0], word_own[0]), (word_ring.last, corners)
    )
    word_ring.side(1)
    word_self_ring = Scatter(word_back[2][0])
    region_up = go_feed(1, region_made, (word_self_ring.last,))
    word_self_ring.add(word_back[1][0], True)
    region_down = go_down(1, region_made, region_up)
    window = (region_down[3], word_ring.raw)
    region_far = go_feed_back(True, 1, region_made, region_up, region_down, (word_ring.raw,))
    word_ring.side(2, *window)
    word_self_ring.side(1, *window)
    region_ring = Scatter(region_far[1])
    region_own = go_feed_back(
        False, 1, region_made, region_up, region_down, (region_far[2],)
    )
    region_ring.add(region_own[1], True)
    region_back = go_back(
        1, region_made, region_down, (region_far[0], region_own[0]), (region_ring.last,)
    )
    window = (region_own[2], word_ring.raw, word_self_ring.raw)
    region_ring.side(1, *window)
    word_self_ring.side(2, *window)
    word_ring.join(word_self_ring)
    word_ring.outer(region_back[3])
    region_self_ring = Scatter(region_back[2][0], region_ring.raw + word_self_ring.raw)
    swapped = region_self_ring.arrived
    region_self_ring.add(region_back[1][0], True)
    units, mine, other, cross_small, pieces = run_back(
        cross_plan,
        after(core, region_self_ring.last),
        [[word_back[0][0]], [region_back[0][0]]],
        unit_one,
        scale_one,
        x_all,
        cross_mats,
        gain_all,
        key_all,
        cross_same,
        cross_kept,
    )
    region_ring.side(2, swapped)
    region_self_ring.side(1)
    cross_ring = Scatter(other[0], region_ring.raw + region_self_ring.raw)
    region_self_ring.side(2, cross_small)
    region_ring.outer(cross_small)
    word_ring.inner(cross_small)
    cross_ring.add(mine[0], True)
    grads_in = run_cross_inputs(
        cross_plan, pieces, cross_mats[0], after(units, cross_ring.last)
    )
    cross_ring.side(1)
    small_gate = (cross_ring.raw, grads_in[0])
    word_shard = word_ring.near(*small_gate)
    region_ring.inner(*small_gate)
    region_self_ring.outer(*small_gate)
    cross_ring.side(2, *small_gate)
    region_self_ring.inner()
    cross_ring.outer()
    cross_ring.inner()
    if staged:
        wide = ffn_w.shape[3] // columns * 2
        parts = [word_shard[at : at + 2] for at in range(0, wide, 2)]
        word_shard, word_self_shard = jnp.concatenate(parts, axis=-1), word_shard[wide:]
    else:
        word_self_shard = word_self_ring.near()
    attn_shard = jnp.stack([cross_ring.near(), word_self_shard, region_self_ring.near()])
    ffn_shard = jnp.stack([word_shard, region_ring.near()])
    outputs = [word_down[0], region_down[0]]
    downs = [word_down[1:], region_down[1:]]
    feeds = [(word_far, word_own), (region_far, region_own)]
    self_small = [word_back[3], region_back[3]]
    grad_lang = grads_in[0].reshape(lang.shape)
    grad_vis = grads_in[1].reshape(vis.shape)

    layers = [after(part, small_gate) for part in (cross_small, self_small[0], self_small[1])]
    gain_rows = [part[0:1] for part in layers] + [part[2][0:1] for part in downs]
    bias_rows = []
    for part in layers:
        bias_rows += [part[3:5], part[2:3]]
    bias_rows += [part[2][2:3] for part in downs]
    bias_rows += [part[1:2] for part in layers] + [part[2][1:2] for part in downs]
    up_rows = []
    for far, own in feeds:
        lines = far[2][0:1], own[2][0:1]
        up_rows.append(
            jnp.where(
                core_index == 0,
                jnp.concatenate([lines[1], lines[0]], axis=1),
                jnp.concatenate([lines[0], lines[1]], axis=1),
            )
        )

    def split(rows, share):
        rows = jnp.concatenate(rows)
        count = rows.shape[0]
        return rows.reshape(count, -1, share).transpose(1, 0, 2).reshape(-1, count * share)

    small_grad = jnp.concatenate(
        [split(gain_rows, model_share), split(bias_rows, model_share), split(up_rows, hidden_share)],
        axis=1,
    )
    small_grad = jnp.pad(small_grad, ((0, 0), (0, padded - small_size)))
    small_sum = scatter_small(small_grad.reshape(small_grad.shape[0], -1, 128)).reshape(-1)
    gains_shard = small_sum[: cuts[0]].reshape(5, model_share)
    biases_shard = small_sum[cuts[0] : cuts[1]].reshape(16, model_share)
    up_shard = small_sum[cuts[1] : small_size].reshape(2, hidden_share)
    squares = jnp.sum(attn_shard * attn_shard) + jnp.sum(ffn_shard * ffn_shard)
    squares = squares + jnp.where(core_index == 0, jnp.sum(small_sum * small_sum), 0.0)
    grad_norm = jnp.sqrt(sum_all(squares))
    clip = jnp.minimum(1.0, clip_norm / (grad_norm + 1e-06))
    attn_new = adam_update(attn_w, attn_m, attn_v, attn_ema, attn_shard, clip, rate_mats)
    ffn_new = adam_update(ffn_w, ffn_m, ffn_v, ffn_ema, ffn_shard, clip, rate_mats)
    gains_new = adam_update(gains, gains_m, gains_v, gains_ema, gains_shard, clip, rate_small)
    biases_new = adam_update(biases, biases_m, biases_v, biases_ema, biases_shard, clip, rate_small)
    up_new = adam_update(bias_up, bias_up_m, bias_up_v, bias_up_ema, up_shard, clip, rate_small)
    return (
        outputs[0],
        outputs[1],
        grad_lang,
        grad_vis,
        grad_norm,
        attn_new[0],
        attn_new[1],
        attn_new[2],
        attn_new[3],
        ffn_new[0],
        ffn_new[1],
        ffn_new[2],
        ffn_new[3],
        gains_new[0],
        gains_new[1],
        gains_new[2],
        gains_new[3],
        biases_new[0],
        biases_new[1],
        biases_new[2],
        biases_new[3],
        up_new[0],
        up_new[1],
        up_new[2],
        up_new[3],
    )


def solution(mesh):
    return jax.shard_map(
        local,
        mesh=mesh,
        in_specs=(
            P(("dp", "mp"), None, None),
            P(("dp", "mp"), None, None),
            P(("dp", "mp"), None),
            P(("dp", "mp")),
            P(("dp", "mp"), None, None),
            P(("dp", "mp"), None, None),
            P(None, None, "dp", "mp"),
            P(None, None, "dp", "mp"),
            P(None, None, "dp", "mp"),
            P(None, None, "dp", "mp"),
            P(None, None, "dp", "mp"),
            P(None, None, "dp", "mp"),
            P(None, None, "dp", "mp"),
            P(None, None, "dp", "mp"),
            P(None, "dp"),
            P(None, "dp"),
            P(None, "dp"),
            P(None, "dp"),
            P(None, "dp"),
            P(None, "dp"),
            P(None, "dp"),
            P(None, "dp"),
            P(None, "dp"),
            P(None, "dp"),
            P(None, "dp"),
            P(None, "dp"),
        ),
        out_specs=(
            P(("dp", "mp"), None, None),
            P(("dp", "mp"), None, None),
            P(("dp", "mp"), None, None),
            P(("dp", "mp"), None, None),
            P(),
            P(None, None, "dp", "mp"),
            P(None, None, "dp", "mp"),
            P(None, None, "dp", "mp"),
            P(None, None, "dp", "mp"),
            P(None, None, "dp", "mp"),
            P(None, None, "dp", "mp"),
            P(None, None, "dp", "mp"),
            P(None, None, "dp", "mp"),
            P(None, "dp"),
            P(None, "dp"),
            P(None, "dp"),
            P(None, "dp"),
            P(None, "dp"),
            P(None, "dp"),
            P(None, "dp"),
            P(None, "dp"),
            P(None, "dp"),
            P(None, "dp"),
            P(None, "dp"),
            P(None, "dp"),
        ),
        check_vma=False,
    )
```

```python
import functools
import math
import jax
import jax.numpy as jnp
from jax import lax
from jax.experimental import pallas as pl
from jax.experimental.pallas import tpu as pltpu
from jax.sharding import PartitionSpec as P

HEAD_DIM = 64
STEP = 7


norm_eps = 1e-12
mask_fill = -1000000000.0
beta_one = 0.5
beta_two = 0.6
ema_decay = 0.5
adam_eps = 1e-08
weight_decay = 0.01
rate_mats = 0.02
rate_small = 0.2
clip_norm = 1.0

GROUP = 4
low = jnp.bfloat16
LINE = 4
CHIPS = 16
PAIR = 2 * HEAD_DIM
TILE = 256
CHUNK = 64
FEED = 1536
FEED_ROWS = 64
BELL = (2.0 * math.pi) ** -0.5
COST_SCALE = 0.05
HEAD_SCALE = HEAD_DIM ** (-0.5)
SQRT_HALF = 0.5**0.5


def moves(target):
    pairs = []
    for z in range(LINE):
        for y in range(2):
            for x in range(2):
                there = target(z, y, x)
                if there is not None:
                    pairs.append((z * 4 + y * 2 + x, there[0] * 4 + there[1] * 2 + there[2]))
    return pairs


routes = {
    1: moves(lambda z, y, x: (z, y, 1 - x)),
    2: moves(lambda z, y, x: (z, 1 - y, x)),
    4: moves(lambda z, y, x: (z ^ 1, y, x)),
    8: moves(lambda z, y, x: (z ^ 2, y, x)),
}
middle = moves(lambda z, y, x: (3 - z, y, x) if z in (1, 2) else None)
inwards = moves(lambda z, y, x: (z ^ 1, y, x) if z in (0, 3) else None)
outwards = moves(lambda z, y, x: (z ^ 1, y, x) if z in (1, 2) else None)


def send(values, bit):
    return lax.ppermute(values, "dp", routes[bit])


def swap_cores(values):
    return lax.ppermute(values, "mp", [(0, 1), (1, 0)])


def widen(values):
    return values.astype(jnp.float32)


def pick(values, axis, index):
    return lax.dynamic_index_in_dim(values, index, axis, keepdims=False)


def bit_of(bit):
    return (lax.axis_index("dp") // bit) % 2


def after(values, *others):
    return lax.optimization_barrier((values,) + others)[0]


def assemble_kernel(places, spans, rows, place_ref, *refs):
    pieces, wholes, sem = refs[: len(places)], refs[len(places) : -1], refs[-1]
    columns = pieces[0].shape[3]
    below = wholes[len(spans)] if len(wholes) > len(spans) else None
    copies = []
    for piece, (first, other) in zip(pieces, places):
        for number in range(piece.shape[0]):
            row = pl.ds(pl.multiple_of(place_ref[first + number] * rows, 16), rows)
            column = pl.ds(pl.multiple_of((place_ref[CHIPS] ^ other) * columns, 128), columns)
            for whole, (start, count) in zip(wholes, spans):
                if piece.shape[2] == rows:
                    pairs = [(piece.at[number, pl.ds(start, count)], whole.at[:, row, column])]
                else:
                    pairs = [
                        (piece.at[number, 0, pl.ds(at * rows, rows)], whole.at[at, row, column])
                        for at in range(start, start + count)
                    ]
                copies += [pltpu.make_async_copy(here, there, sem) for here, there in pairs]
            if below is not None and not other:
                rest = pl.ds(piece.shape[2] - below.shape[1], below.shape[1])
                copies.append(
                    pltpu.make_async_copy(
                        piece.at[number, 0, rest], below.at[place_ref[first + number]], sem
                    )
                )
    for copy in copies:
        copy.start()
    for copy in copies:
        copy.wait()


def assemble(pieces, places, spans, rows, place):
    columns = pieces[0].shape[3]
    outs = [shape_of((count, rows * CHIPS, columns * 2), low) for _, count in spans]
    below = pieces[0].shape[2] - rows * sum(count for _, count in spans)
    if pieces[0].shape[2] != rows:
        outs.append(shape_of((CHIPS, below, columns), low))
    return pl.pallas_call(
        functools.partial(assemble_kernel, places, spans, rows),
        out_shape=outs,
        in_specs=[pl.BlockSpec(memory_space=pltpu.SMEM)]
        + [pl.BlockSpec(memory_space=pl.ANY)] * len(pieces),
        out_specs=vmem(len(outs)),
        scratch_shapes=[pltpu.SemaphoreType.DMA],
        compiler_params=params_of(24),
        cost_estimate=cost_of(3),
        name="assemble",
    )(place, *pieces)


class Gather:
    def __init__(self, own):
        self.staged = lax.axis_size("dp") == CHIPS
        self.own = own[None]
        self.last = self.pair = self.mid = self.four = self.own

    def near(self, *gate):
        if self.staged:
            own = after(self.own, *gate) if gate else self.own
            self.pair = self.last = jnp.concatenate([self.own, send(own, 4)])

    def inner(self, *gate):
        if self.staged:
            self.mid = self.last = lax.ppermute(after(self.pair, *gate), "dp", middle)

    def outer(self, *gate):
        if self.staged:
            out = lax.ppermute(after(self.mid, *gate), "dp", outwards)
            self.four = self.last = jnp.concatenate([self.pair, self.mid + out])

    def sides(self, *gate):
        if self.staged:
            four = after(self.four, *gate)
            self.by_x, self.by_y = send(four, 1), send(four, 2)
            self.last = (self.by_x, self.by_y)

    def corner(self, *gate):
        if self.staged:
            by_x, by_y = after((self.by_x[:2], self.by_y[2:]), *gate)
            self.corners = send(by_x, 2), send(by_y, 1)
            self.last = self.corners

    def most(self, *gate):
        if self.staged:
            parts = jnp.concatenate([self.four, self.by_x, self.by_y])
            self.major = (parts, swap_cores(after(parts, *gate)))
            self.last = self.major[1]

    def rest(self, *gate):
        if self.staged:
            parts = jnp.concatenate(self.corners)
            self.minor = (parts, swap_cores(after(parts, *gate)))
            self.last = self.minor[1]

    def place(self):
        chip = lax.axis_index("dp")
        z = chip // 4
        far = jnp.where((z == 1) | (z == 2), 12, 8)
        four = jnp.stack([chip, chip ^ 4, chip ^ far, chip ^ far ^ 4])
        return jnp.concatenate(
            [four, four ^ 1, four ^ 2, four ^ 3, lax.axis_index("mp").reshape(1)]
        ).astype(jnp.int32)

    def finish(self, spans, rows):
        if not self.staged:
            whole = lax.all_gather(self.own[0], "dp", axis=1, tiled=True)
            whole = lax.all_gather(whole, "mp", axis=2, tiled=True)
            return [whole[start : start + count] for start, count in spans]
        pieces, places = [], []
        for pair, first in zip((self.major, self.minor), (0, 12)):
            pieces += pair
            places += [(first, 0), (first, 1)]
        made = assemble(pieces, places, spans, rows, self.place())
        self.below = made[-1]
        return made[: len(spans)]


class Scatter:
    def __init__(self, other, gate=()):
        self.staged = lax.axis_size("dp") == CHIPS
        self.raw = []
        self.arrived = self.last = swap_cores(after(other, *gate))

    def add(self, mine, split):
        self.total = widen(mine) + widen(self.arrived)
        if self.staged:
            total = self.total.astype(low)
            total = total.reshape((-1, 4, 2, 2, total.shape[1] // CHIPS, total.shape[2]))
            count = total.shape[0]
            self.parts = [total[: count // 2], total[count // 2 :]] if split else [total]
            self.last = self.parts

    def side(self, bit, *gate):
        if not self.staged:
            return
        parts, self.raw = [], []
        for part, way in zip(self.parts, (bit, 3 - bit)):
            axis = 2 if way == 2 or part.ndim == 5 else 3
            kept = pick(part, axis, bit_of(way))
            arrived = send(after(pick(part, axis, 1 - bit_of(way)), *gate), way)
            self.raw.append(arrived)
            parts.append((widen(kept) + widen(arrived)).astype(low))
        if parts[0].ndim == 4:
            whole = parts[0] if len(parts) == 1 else jnp.concatenate(parts)
            whole = whole.reshape((whole.shape[0], 2, 2) + whole.shape[2:])
            self.own = pick(whole, 1, bit_of(8))
            self.far = pick(whole, 1, 1 - bit_of(8))
            self.last = (self.own, self.far)
        else:
            self.parts = self.last = parts

    def join(self, narrow):
        if self.staged:
            columns = narrow.own.shape[-1]

            def cut(values):
                return [values[..., at : at + columns] for at in range(0, values.shape[-1], columns)]

            self.own = jnp.concatenate(cut(self.own) + [narrow.own])
            self.far = jnp.concatenate(cut(self.far) + [narrow.far])
            self.last = (self.own, self.far)

    def outer(self, *gate):
        if self.staged:
            arrived = lax.ppermute(after(self.far, *gate), "dp", inwards)
            self.far = self.last = (widen(self.far) + widen(arrived)).astype(low)

    def inner(self, *gate):
        if self.staged:
            arrived = lax.ppermute(after(self.far, *gate), "dp", middle)
            self.own = self.last = (widen(self.own) + widen(arrived)).astype(low)

    def near(self, *gate):
        if not self.staged:
            return lax.psum_scatter(self.total, "dp", scatter_dimension=1, tiled=True)
        arrived = send(after(pick(self.own, 1, 1 - bit_of(4)), *gate), 4)
        return widen(pick(self.own, 1, bit_of(4))) + widen(arrived)


def three_terms(values):
    terms = []
    for _ in range(3):
        terms.append(values.astype(low))
        values = values - lax.reduce_precision(values, 8, 7)
    return jnp.stack(terms)


def scatter_small(values):
    values = values + swap_cores(values)
    if lax.axis_size("dp") != CHIPS:
        return lax.psum_scatter(values, "dp", scatter_dimension=0, tiled=True)[0]
    for bit in (8, 4, 2, 1):
        half = values.shape[0] // 2
        at_zero = bit_of(bit) == 0
        kept = jnp.where(at_zero, values[:half], values[half:])
        sent = jnp.where(at_zero, values[half:], values[:half])
        values = kept + send(sent, bit)
    return values[0]


def sum_all(value):
    if lax.axis_size("dp") != CHIPS:
        return lax.psum(value, ("dp", "mp"))
    value = value.reshape(1, 1)
    value = value + swap_cores(value)
    for bit in (1, 2, 4, 8):
        value = value + send(value, bit)
    return value[0, 0]


def dot_nn(left, right):
    return lax.dot_general(left, right, (((1,), (0,)), ((), ())), preferred_element_type=jnp.float32)


def dot_nt(left, right):
    return lax.dot_general(left, right, (((1,), (1,)), ((), ())), preferred_element_type=jnp.float32)


def dot_tn(left, right):
    return lax.dot_general(left, right, (((0,), (0,)), ((), ())), preferred_element_type=jnp.float32)


def fold_rows(values):
    return jnp.sum(values.reshape(values.shape[0] // 8, 8, values.shape[1]), axis=0)


def close_rows(values):
    return jnp.sum(values, axis=0, keepdims=True)


def norm_rows(summed, gain, shift):
    average = jnp.mean(summed, axis=-1, keepdims=True)
    centered = summed - average
    inverse = lax.rsqrt(jnp.mean(centered * centered, axis=-1, keepdims=True) + norm_eps)
    normed = centered * inverse
    return normed * gain + shift, normed, inverse


def norm_rows_back(grad_out, normed, inverse, gain):
    scaled = grad_out * gain
    return inverse * (
        scaled
        - jnp.mean(scaled, axis=-1, keepdims=True)
        - normed * jnp.mean(scaled * normed, axis=-1, keepdims=True)
    )


def stack_heads(block):
    first = lax.broadcasted_iota(jnp.int32, block.shape, 1) < HEAD_DIM
    nothing = jnp.zeros_like(block)
    return jnp.concatenate(
        [jnp.where(first, block, nothing), jnp.where(first, nothing, block)], axis=0
    )


def merge_heads(double):
    rows = double.shape[0] // 2
    first = lax.broadcasted_iota(jnp.int32, (rows, double.shape[1]), 1) < HEAD_DIM
    return jnp.where(first, double[:rows], double[rows:])


def pair_forward(queries, keys, values, bias):
    count = keys.shape[0]
    scores = dot_nt(stack_heads(keys), queries * HEAD_SCALE)
    weights, totals = [], []
    for part in (scores[:count] + bias, scores[count:] + bias):
        top = jnp.max(part, axis=0, keepdims=True)
        powers = jnp.exp(part - top)
        total = jnp.sum(powers, axis=0, keepdims=True)
        weights.append((powers * (1.0 / total)).astype(low))
        totals.append(top + jnp.log(total))
    context = dot_tn(jnp.concatenate(weights, axis=0), stack_heads(values))
    return context.astype(low), totals


def pair_backward(queries, keys, values, grad, bias, totals):
    count = keys.shape[0]
    both_keys = stack_heads(keys)
    queries = queries * HEAD_SCALE
    scores = dot_nt(both_keys, queries)
    sensed = dot_nt(stack_heads(values), grad)
    weights, slopes = [], []
    for part, sense, total in (
        (scores[:count], sensed[:count], totals[0]),
        (scores[count:], sensed[count:], totals[1]),
    ):
        weight = jnp.exp(part + bias - total)
        inner = jnp.sum(sense * weight, axis=0, keepdims=True)
        weights.append(weight.astype(low))
        slopes.append((weight * (sense - inner)).astype(low))
    weights = jnp.concatenate(weights, axis=0)
    slopes = jnp.concatenate(slopes, axis=0)
    grad_queries = (dot_tn(slopes, both_keys) * HEAD_DIM ** (-0.5)).astype(low)
    grad_keys = merge_heads(dot_nn(slopes, queries)).astype(low)
    grad_values = merge_heads(dot_nn(weights, grad)).astype(low)
    return grad_queries, grad_keys, grad_values


def tiles_of(width):
    return [(at, min(TILE, width - at)) for at in range(0, width, TILE)]


def row_block(start, size, step):
    return pl.ds(pl.multiple_of(start + step * size, 16), size)


def attend_front(plan, *refs):
    streams, relations, cross = plan["streams"], plan["relations"], plan["cross"]
    refs = list(refs)

    def take(count):
        taken = refs[:count]
        del refs[:count]
        return taken

    (x_ref,) = take(1)
    before = [] if cross else take(1)
    mats = take(plan["mats"])
    gain_ref, bias_ref, key_ref = take(3)
    same = take(len(relations))
    q_ref, k_ref, v_ref, ctx_ref = take(4)
    logs = take(len(relations))
    normed = take(len(streams))
    inverse = take(len(streams))
    lowered = take(len(streams))
    (acc_ref,) = take(1)
    width = x_ref.shape[1]
    weights = [mats[i // (4 // len(mats))].at[i % (4 // len(mats))] for i in range(4)]
    rows = x_ref[...]
    for target, weight, row in ((q_ref, 0, 0), (k_ref, 1, None), (v_ref, 2, 1)):
        for at, size in tiles_of(width):
            part = dot_nn(rows, weights[weight][:, at : at + size])
            if row is not None:
                line = plan["rows"][row]
                part = part + bias_ref[line : line + 1, at : at + size]
            target[:, at : at + size] = part.astype(low)
    pairs = width // PAIR
    groups = plan["groups"]

    def one_group(group, carry):
        for which, (asking, asked) in enumerate(relations):
            ask = row_block(*streams[asking], group)
            key = row_block(*streams[asked], group)
            bias = same[which][...] + key_ref[key, :]
            for pair in range(pairs):
                lanes = slice(pair * PAIR, (pair + 1) * PAIR)
                context, totals = pair_forward(
                    q_ref[ask, lanes], k_ref[key, lanes], v_ref[key, lanes], bias
                )
                ctx_ref[ask, lanes] = context
                for side in range(2):
                    logs[which][group * (2 * pairs) + 2 * pair + side] = totals[side]
        return carry

    lax.fori_loop(0, groups, one_group, 0)
    context = ctx_ref[...]
    for at, size in tiles_of(width):
        acc_ref[:, at : at + size] = dot_nt(context, weights[3][at : at + size, :])
    gain = gain_ref[plan["gain"] : plan["gain"] + 1, :]
    shift = bias_ref[plan["shift"] : plan["shift"] + 1, :]
    out_bias = bias_ref[plan["rows"][2] : plan["rows"][2] + 1, :]
    for index, (start, size) in enumerate(streams):

        def one_chunk(step, carry, start=start, index=index):
            here = row_block(start, CHUNK, step)
            there = row_block(0, CHUNK, step)
            if cross:
                base = widen(x_ref[here, :])
            else:
                last_gain, last_shift = plan["before"]
                base = (
                    before[0][here, :] * gain_ref[last_gain : last_gain + 1, :]
                    + bias_ref[last_shift : last_shift + 1, :]
                )
            value, unit, scale = norm_rows(base + acc_ref[here, :] + out_bias, gain, shift)
            normed[index][there, :] = unit
            inverse[index][there, :] = scale
            lowered[index][there, :] = value.astype(low)
            return carry

        lax.fori_loop(0, size * groups // CHUNK, one_chunk, 0)


def add_inputs(streams, groups, weights, grads, grad_in):
    dq_ref, dk_ref, dv_ref = grads
    for index, (start, size) in enumerate(streams):
        span = slice(start, start + size * groups)
        for at, wide in tiles_of(dq_ref.shape[1]):
            grad_in[index][:, at : at + wide] += (
                dot_nt(dq_ref[span, :], weights[0][at : at + wide, :])
                + dot_nt(dk_ref[span, :], weights[1][at : at + wide, :])
                + dot_nt(dv_ref[span, :], weights[2][at : at + wide, :])
            )


def cross_inputs(plan, dq_ref, dk_ref, dv_ref, mat_ref, *refs):
    streams = plan["streams"]
    grads, outs = refs[: len(streams)], refs[len(streams) :]
    for grad, out in zip(grads, outs):
        out[...] = grad[...]
    weights = [mat_ref.at[i] for i in range(3)]
    add_inputs(streams, plan["groups"], weights, (dq_ref, dk_ref, dv_ref), outs)


def attend_back(plan, *refs):
    streams, relations = plan["streams"], plan["relations"]
    refs = list(refs)

    def take(count):
        taken = refs[:count]
        del refs[:count]
        return taken

    (core_ref,) = take(1)
    carried = [take(plan["carried"]) for _ in streams]
    normed = take(len(streams))
    inverse = take(len(streams))
    (x_ref,) = take(1)
    mats = take(plan["mats"])
    gain_ref, key_ref = take(2)
    same = take(len(relations))
    q_ref, k_ref, v_ref, ctx_ref = take(4)
    logs = take(len(relations))
    grad_in = take(len(streams))
    mine = take(plan["mats"])
    other = take(plan["mats"])
    (small_ref,) = take(1)
    dq_ref, dk_ref, dv_ref = take(3)
    do_ref, dctx_ref = take(2)
    fetched = take(5 + plan["mats"])
    sems = refs[0]
    copies = [
        pltpu.make_async_copy(source, target, sems.at[number])
        for number, (source, target) in enumerate(
            zip(mats + [q_ref, k_ref, v_ref, ctx_ref, x_ref], fetched)
        )
    ]
    for copy in copies:
        copy.start()
    mats = fetched[: plan["mats"]]
    q_ref, k_ref, v_ref, ctx_ref, x_ref = fetched[plan["mats"] :]
    width = x_ref.shape[1]
    half = width // 2
    each = 4 // plan["mats"]
    weights = [mats[i // each].at[i % each] for i in range(4)]
    gain = gain_ref[plan["gain"] : plan["gain"] + 1, :]
    groups = plan["groups"]
    nothing = jnp.zeros((8, width), jnp.float32)
    sums = (nothing, nothing, nothing)
    for index, (start, size) in enumerate(streams):

        def one_chunk(step, sums, start=start, index=index):
            here = row_block(start, CHUNK, step)
            there = row_block(0, CHUNK, step)
            grad = carried[index][0][there, :]
            for more in carried[index][1:]:
                grad = grad + more[there, :]
            unit = normed[index][there, :]
            down = norm_rows_back(grad, unit, inverse[index][there, :], gain)
            sent = down.astype(low)
            grad_in[index][there, :] = down
            do_ref[here, :] = sent
            return (
                sums[0] + fold_rows(grad * unit),
                sums[1] + fold_rows(grad),
                sums[2] + fold_rows(widen(sent)),
            )

        sums = lax.fori_loop(0, size * groups // CHUNK, one_chunk, sums)
    for copy in copies:
        copy.wait()
    sent = do_ref[...]
    for at, size in tiles_of(width):
        dctx_ref[:, at : at + size] = dot_nn(sent, weights[3][:, at : at + size]).astype(low)
    pairs = width // PAIR

    def one_group(group, carry):
        for which, (asking, asked) in enumerate(relations):
            ask = row_block(*streams[asking], group)
            key = row_block(*streams[asked], group)
            bias = same[which][...] + key_ref[key, :]
            for pair in range(pairs):
                lanes = slice(pair * PAIR, (pair + 1) * PAIR)
                base = group * (2 * pairs) + 2 * pair
                grads = pair_backward(
                    q_ref[ask, lanes],
                    k_ref[key, lanes],
                    v_ref[key, lanes],
                    dctx_ref[ask, lanes],
                    bias,
                    [logs[which][base], logs[which][base + 1]],
                )
                dq_ref[ask, lanes], dk_ref[key, lanes], dv_ref[key, lanes] = grads
        return carry

    lax.fori_loop(0, groups, one_group, 0)
    at_zero = core_ref[0] == 0
    rows = x_ref[...]
    last = None
    for number, (left, right) in enumerate(
        ((rows, dq_ref), (rows, dk_ref), (rows, dv_ref), (sent, ctx_ref))
    ):
        wide = right[...]
        if left is not last:
            flipped, last = left.T, left
        for at, size in tiles_of(width):
            whole = dot_nn(flipped[at : at + size, :], wide).astype(low)
            former, latter = whole[:, :half], whole[:, half:]
            mine[number // each][number % each, at : at + size, :] = jnp.where(
                at_zero, former, latter
            )
            other[number // each][number % each, at : at + size, :] = jnp.where(
                at_zero, latter, former
            )
    if not plan["cross"]:
        add_inputs(streams, groups, weights, (dq_ref, dk_ref, dv_ref), grad_in)

    def add_chunk(step, sums):
        here = row_block(0, CHUNK, step)
        return (
            sums[0] + fold_rows(widen(dq_ref[here, :])),
            sums[1] + fold_rows(widen(dv_ref[here, :])),
        )

    more = lax.fori_loop(0, x_ref.shape[0] // CHUNK, add_chunk, (nothing, nothing))
    small_ref[...] = jnp.concatenate(
        [close_rows(part) for part in sums + more] + [jnp.zeros((3, width), jnp.float32)], axis=0
    )


def vmem(count):
    return [pl.BlockSpec(memory_space=pltpu.VMEM)] * count


def shape_of(shape, kind):
    return jax.ShapeDtypeStruct(tuple(shape), kind)


def cost_of(micros):
    return pl.CostEstimate(flops=int(micros * COST_SCALE * 1.15e9), bytes_accessed=1 << 20, transcendentals=0)


def params_of(mib):
    return pltpu.CompilerParams(vmem_limit_bytes=mib << 20)


def layer_plan(layer, sizes, groups, mats):
    if layer == 0:
        starts = (0, sizes[0] * groups)
        streams = [(starts[i], sizes[i]) for i in range(2)]
        relations, gain, shift = [(0, 1), (1, 0)], 0, 11
    else:
        streams, relations = [(0, sizes[0])], [(0, 0)]
        gain, shift = layer, 11 + layer
    return {
        "streams": streams,
        "relations": relations,
        "cross": layer == 0,
        "mats": mats,
        "groups": groups,
        "gain": gain,
        "shift": shift,
        "rows": [3 * layer, 3 * layer + 1, 3 * layer + 2],
        "before": (0, 11),
        "carried": 1 if layer == 0 else 3,
    }


def run_front(plan, x, before, mats, gains, biases, key_bias, same):
    rows, width = x.shape
    groups = plan["groups"]
    outs = [shape_of((rows, width), low)] * 4
    for asking, _ in plan["relations"]:
        outs.append(
            shape_of((groups * width // HEAD_DIM, 1, plan["streams"][asking][1]), jnp.float32)
        )
    counts = [size * groups for _, size in plan["streams"]]
    outs += [shape_of((count, width), jnp.float32) for count in counts]
    outs += [shape_of((count, 1), jnp.float32) for count in counts]
    outs += [shape_of((count, width), low) for count in counts]
    args = [x] + ([] if before is None else [before]) + list(mats) + [gains, biases, key_bias]
    args += list(same)
    results = pl.pallas_call(
        functools.partial(attend_front, plan),
        out_shape=outs,
        in_specs=vmem(len(args)),
        out_specs=vmem(len(outs)),
        scratch_shapes=[pltpu.VMEM((rows, width), jnp.float32)],
        compiler_params=params_of(27),
        cost_estimate=cost_of(0.028 * rows),
        name="attend_front",
    )(*args)
    related, many = len(plan["relations"]), len(counts)
    kept = results[: 4 + related]
    rest = results[4 + related :]
    return kept, rest[:many], rest[many : 2 * many], rest[2 * many :]


def run_back(plan, core, carried, normed, inverse, x, mats, gains, key_bias, same, kept):
    rows, width = x.shape
    counts = [size * plan["groups"] for _, size in plan["streams"]]
    grads = [shape_of(mat.shape[:2] + (width // 2,), low) for mat in mats]
    outs = [shape_of((count, width), jnp.float32) for count in counts] + grads + grads
    outs.append(shape_of((8, width), jnp.float32))
    pieces = [shape_of((rows, width), low)] * 3
    cross = plan["cross"]
    args = [part for parts in carried for part in parts] + list(normed) + list(inverse) + [x]
    args += list(mats) + [gains, key_bias] + list(same) + list(kept)
    far = [x] + list(mats) + list(kept[:4])
    specs = [pl.BlockSpec(memory_space=pltpu.SMEM)] + [
        pl.BlockSpec(memory_space=pl.ANY if any(arg is part for part in far) else pltpu.VMEM)
        for arg in args
    ]
    results = pl.pallas_call(
        functools.partial(attend_back, plan),
        out_shape=outs + (pieces if cross else []),
        in_specs=specs,
        out_specs=vmem(len(outs) + (3 if cross else 0)),
        scratch_shapes=[pltpu.VMEM((rows, width), low)] * (2 if cross else 5)
        + [pltpu.VMEM(mat.shape, low) for mat in mats]
        + [pltpu.VMEM((rows, width), low)] * 5
        + [pltpu.SemaphoreType.DMA((5 + len(mats),))],
        compiler_params=params_of(40),
        name="attend_back",
    )(core, *args)
    many, count = len(counts), len(mats)
    return (
        results[:many],
        results[many : many + count],
        results[many + count : many + 2 * count],
        results[len(outs) - 1],
        results[len(outs) :],
    )


def run_cross_inputs(plan, pieces, mat, grads):
    outs = [shape_of(grad.shape, jnp.float32) for grad in grads]
    return pl.pallas_call(
        functools.partial(cross_inputs, plan),
        out_shape=outs,
        in_specs=vmem(4 + len(grads)),
        out_specs=vmem(len(grads)),
        compiler_params=params_of(28),
        cost_estimate=cost_of(10),
        name="cross_inputs",
    )(*pieces, mat, *grads)


def feed_up(line, x_ref, mat_ref, bias_ref, h_ref, slope_ref, hidden_ref):
    bias = bias_ref[line : line + 1, :]
    hidden_ref[...] = dot_nn(x_ref[...], mat_ref[0])

    def one_chunk(step, carry):
        here = row_block(0, FEED_ROWS, step)
        hidden = hidden_ref[here, :] + bias
        share = 0.5 + 0.5 * lax.erf(hidden * SQRT_HALF)
        h_ref[here, :] = (hidden * share).astype(low)
        slope_ref[here, :] = (share + hidden * (jnp.exp(hidden * hidden * -0.5) * BELL)).astype(low)
        return carry

    lax.fori_loop(0, x_ref.shape[0] // FEED_ROWS, one_chunk, 0)


def feed_down(plan, h_ref, mat_ref, gain_ref, bias_ref, unit_ref, cot_ref, live_ref, *refs):
    out_ref, du_ref, do_ref, small_ref, acc_ref, cots_ref = refs
    step = pl.program_id(0)
    items, slots, width = out_ref.shape

    @pl.when(step == 0)
    def _():
        acc_ref[...] = jnp.zeros_like(acc_ref)
        for item in range(items):
            cots_ref[item * slots : (item + 1) * slots, :] = widen(cot_ref[item])

    rows = h_ref[...]
    for at, size in tiles_of(width):
        acc_ref[:, at : at + size] += dot_nt(rows, mat_ref[0, at : at + size, :])

    @pl.when(step == pl.num_programs(0) - 1)
    def _():
        def line(ref, row):
            return ref[row : row + 1, :]

        stream = plan
        last_gain, last_shift = line(gain_ref, 1 + stream), line(bias_ref, 12 + stream)
        gain, shift = line(gain_ref, 3 + stream), line(bias_ref, 14 + stream)
        out_bias = line(bias_ref, 9 + stream)
        nothing = jnp.zeros((8, width), jnp.float32)

        def one_chunk(chunk, sums):
            here = row_block(0, CHUNK, chunk)
            live = live_ref[here, :]
            base = unit_ref[here, :] * last_gain + last_shift
            value, unit, scale = norm_rows(base + acc_ref[here, :] + out_bias, gain, shift)
            grad = cots_ref[here, :] * live
            cots_ref[here, :] = value * live
            down = norm_rows_back(grad, unit, scale, gain)
            sent = down.astype(low)
            du_ref[here, :] = down
            do_ref[here, :] = sent
            return (
                sums[0] + fold_rows(grad * unit),
                sums[1] + fold_rows(grad),
                sums[2] + fold_rows(widen(sent)),
            )

        sums = lax.fori_loop(0, items * slots // CHUNK, one_chunk, (nothing,) * 3)
        for item in range(items):
            out_ref[item] = cots_ref[item * slots : (item + 1) * slots, :]
        small_ref[...] = jnp.concatenate(
            [close_rows(part) for part in sums] + [jnp.zeros((5, width), jnp.float32)], axis=0
        )


def feed_back(core_ref, do_ref, x_ref, h_ref, slope_ref, up_ref, down_ref, *refs):
    dx_ref, grad_ref, line_ref, sent_flip, rows_flip = refs
    step = pl.program_id(0)
    sent = do_ref[...]

    @pl.when(step == 0)
    def _():
        sent_flip[...] = sent.T
        rows_flip[...] = x_ref[...].T

    slope = (dot_nn(sent, down_ref[0]) * widen(slope_ref[...])).astype(low)
    line_ref[...] = jnp.broadcast_to(close_rows(fold_rows(widen(slope))), line_ref.shape)
    grad_ref[0] = dot_nn(rows_flip[...], slope).astype(low)
    grad_ref[1] = dot_nn(sent_flip[...], h_ref[...]).astype(low)
    part = dot_nt(slope, up_ref[0])

    @pl.when(step == 0)
    def _():
        dx_ref[...] = part

    @pl.when(step > 0)
    def _():
        dx_ref[...] += part


def run_up(stream, x, mat, biases):
    rows, width = x.shape
    hidden = mat.shape[2]
    wide = lambda step: (0, step)
    return pl.pallas_call(
        functools.partial(feed_up, stream),
        grid=(hidden // FEED,),
        out_shape=[shape_of((rows, hidden), low)] * 2,
        in_specs=[
            pl.BlockSpec((rows, width), lambda step: (0, 0)),
            pl.BlockSpec((1, width, FEED), lambda step: (0, 0, step)),
            pl.BlockSpec((2, FEED), wide),
        ],
        out_specs=[pl.BlockSpec((rows, FEED), wide)] * 2,
        scratch_shapes=[pltpu.VMEM((rows, FEED), jnp.float32)],
        compiler_params=params_of(24),
        cost_estimate=cost_of(0.033 * rows),
        name="feed_up",
    )(x, mat, biases)


def run_down(stream, h, mat, gains, biases, unit, cot, live):
    rows, hidden = h.shape
    width = unit.shape[1]
    def whole(array):
        return pl.BlockSpec(array.shape, lambda step: (0,) * len(array.shape))

    outs = [
        shape_of(cot.shape, jnp.float32),
        shape_of((rows, width), jnp.float32),
        shape_of((rows, width), low),
        shape_of((8, width), jnp.float32),
    ]
    return pl.pallas_call(
        functools.partial(feed_down, stream),
        grid=(hidden // FEED,),
        out_shape=outs,
        in_specs=[
            pl.BlockSpec((rows, FEED), lambda step: (0, step)),
            pl.BlockSpec((1, width, FEED), lambda step: (0, 0, step)),
            whole(gains),
            whole(biases),
            whole(unit),
            whole(cot),
            whole(live),
        ],
        out_specs=[whole(out) for out in outs],
        scratch_shapes=[pltpu.VMEM((rows, width), jnp.float32)] * 2,
        compiler_params=params_of(31),
        cost_estimate=cost_of(0.022 * rows),
        name="feed_down",
    )(h, mat, gains, biases, unit, cot, live)


def run_feed_back(core, flip, sent, x, h, slope, up, down):
    rows, hidden = h.shape
    width = x.shape[1]
    steps = hidden // FEED // 2

    def chunk(step, core_ref):
        side = core_ref[0]
        return step + steps * (1 - side if flip else side)

    def wide(step, core_ref):
        return (0, chunk(step, core_ref))

    def deep(step, core_ref):
        return (0, 0, chunk(step, core_ref))

    fixed = lambda step, core_ref: (0, 0)
    return pl.pallas_call(
        feed_back,
        grid_spec=pltpu.PrefetchScalarGridSpec(
            num_scalar_prefetch=1,
            grid=(steps,),
            in_specs=[
                pl.BlockSpec((rows, width), fixed),
                pl.BlockSpec((rows, width), fixed),
                pl.BlockSpec((rows, FEED), wide),
                pl.BlockSpec((rows, FEED), wide),
                pl.BlockSpec((1, width, FEED), deep),
                pl.BlockSpec((1, width, FEED), deep),
            ],
            out_specs=[
                pl.BlockSpec((rows, width), fixed),
                pl.BlockSpec((2, width, FEED), lambda step, core_ref: (0, 0, step)),
                pl.BlockSpec((8, FEED), lambda step, core_ref: (0, step)),
            ],
            scratch_shapes=[pltpu.VMEM((width, rows), low)] * 2,
        ),
        out_shape=[
            shape_of((rows, width), jnp.float32),
            shape_of((2, width, hidden // 2), low),
            shape_of((8, hidden // 2), jnp.float32),
        ],
        compiler_params=params_of(40),
        cost_estimate=cost_of(0.02 * rows),
        name="feed_back",
    )(core, sent, x, h, slope, up, down)


def adam_update(weight, moment_one, moment_two, average, grad, clip, rate):
    clipped = grad * clip
    new_one = beta_one * moment_one + (1.0 - beta_one) * clipped
    new_two = beta_two * moment_two + (1.0 - beta_two) * clipped * clipped
    direction = (
        new_one / (1.0 - beta_one**STEP) / (jnp.sqrt(new_two / (1.0 - beta_two**STEP)) + adam_eps)
    )
    new_weight = weight - rate * (direction + weight_decay * weight)
    new_average = ema_decay * average + (1.0 - ema_decay) * new_weight
    return (new_weight, new_one, new_two, new_average)


def local(
    lang,
    vis,
    word_mask,
    region_count,
    cot_lang,
    cot_vis,
    attn_w,
    attn_m,
    attn_v,
    attn_ema,
    ffn_w,
    ffn_m,
    ffn_v,
    ffn_ema,
    gains,
    gains_m,
    gains_v,
    gains_ema,
    biases,
    biases_m,
    biases_v,
    biases_ema,
    bias_up,
    bias_up_m,
    bias_up_v,
    bias_up_ema,
):
    core_index = lax.axis_index("mp")
    items, words, regions = lang.shape[0], lang.shape[1], vis.shape[1]
    width = lang.shape[2]
    model_share = gains.shape[1]
    hidden_share = bias_up.shape[1]
    small_own = jnp.concatenate([gains.reshape(-1), biases.reshape(-1), bias_up.reshape(-1)])
    small_size = small_own.shape[0]
    padded = -(-small_size // 1024) * 1024
    staged = lax.axis_size("dp") == CHIPS
    cuts = (5 * model_share, 21 * model_share)

    def spread(columns, count):
        parts = columns.reshape(columns.shape[0], count, -1)
        return parts.transpose(1, 0, 2).reshape(count, -1)

    attn_low = attn_w.astype(low)
    ffn_low = ffn_w.astype(low)
    share, columns = attn_w.shape[2:]
    if staged:
        terms = three_terms(small_own).reshape(-1)
        tall = -(-terms.shape[0] // (16 * columns)) * 16
        terms = jnp.pad(terms, (0, tall * columns - terms.shape[0])).reshape(tall, columns)
        own = jnp.concatenate([attn_low[0].reshape(-1, columns), terms])[None]
    else:
        own = attn_low[0]
    first, second, third, fourth = [
        Gather(own),
        Gather(attn_low[1:].reshape((-1,) + attn_low.shape[2:])),
        Gather(ffn_low[0]),
        Gather(ffn_low[1]),
    ]
    first.near()
    second.near(first.last)
    first.inner()
    third.near(first.last)
    second.inner(first.last)
    first.outer()
    fourth.near(first.last)
    first.sides()
    second.outer(first.four)
    third.inner(second.last)
    third.outer(second.last)
    fourth.inner(third.mid)
    first.corner()
    second.sides(first.last)
    first.most()
    first.rest()
    cross_mats = first.finish([(0, 4)], share)
    if staged:
        arrived = widen(first.below).reshape(CHIPS, -1)
        arrived = arrived[:, : 3 * small_size].reshape(CHIPS, 3, small_size)
        small_all = arrived[:, 0] + arrived[:, 1] + arrived[:, 2]
    else:
        small_all = lax.all_gather(small_own, "dp", axis=0, tiled=False)
    gain_all = spread(small_all[:, : cuts[0]], 5)
    bias_all = spread(small_all[:, cuts[0] : cuts[1]], 16)
    up_all = spread(small_all[:, cuts[1] : small_size], 2)

    core = core_index.astype(jnp.int32).reshape(1)
    slots = (words, regions)
    groups = items // GROUP
    sizes = (words * GROUP, regions * GROUP)
    counts = (words * items, regions * items)
    word_live = word_mask.astype(jnp.float32)
    region_live = (jnp.arange(regions)[None, :] < region_count[:, None]).astype(jnp.float32)
    live = [word_live.reshape(-1, 1), region_live.reshape(-1, 1)]
    key_bias = [(part - 1.0) * -mask_fill for part in live]
    key_all = jnp.concatenate(key_bias)
    x_all = jnp.concatenate([lang.reshape(-1, width), vis.reshape(-1, width)])
    cots = [cot_lang, cot_vis]

    def same_item(asked, asking):
        rows = jnp.arange(sizes[asked])[:, None] // slots[asked]
        columns = jnp.arange(sizes[asking])[None, :] // slots[asking]
        return jnp.where(rows == columns, 0.0, mask_fill).astype(jnp.float32)

    cross_plan = layer_plan(0, sizes, groups, 1)
    cross_same = [same_item(1, 0), same_item(0, 1)]
    gains_first = after(gain_all, second.last, third.four, fourth.mid)
    cross_kept, unit_one, scale_one, low_one = run_front(
        cross_plan, x_all, None, cross_mats, gains_first, bias_all, key_all, cross_same
    )
    second.corner()
    third.sides(second.by_x if staged else second.last)
    fourth.outer()
    window = (scale_one, second.last, third.last, fourth.last)
    second.most(*window)
    second.rest(*window)
    self_mats = second.finish([(0, 4), (4, 4)], share)
    third.corner(*window)
    fourth.sides(*window)
    fronts_gate = (fourth.four,) if staged else ()
    self_plans = [layer_plan(1 + stream, (sizes[stream],), groups, 1) for stream in range(2)]
    self_same = [[same_item(stream, stream)] for stream in range(2)]
    yx, xy = (2, 1, 8, 4), (1, 2, 8, 4)

    def go_up(stream):
        kept, unit, scale, lowered = run_front(
            self_plans[stream],
            low_one[stream],
            unit_one[stream],
            [self_mats[stream]],
            after(gain_all, *fronts_gate),
            bias_all,
            key_bias[stream],
            self_same[stream],
        )
        return kept, unit[0], scale[0], lowered[0]

    def go_feed(stream, made, gate):
        return run_up(stream, made[3], mats_of[stream][0], after(up_all, *gate))

    def go_down(stream, made, up):
        out, grad, sent, small = run_down(
            stream,
            up[0],
            mats_of[stream][1],
            gain_all,
            bias_all,
            made[1],
            cots[stream],
            live[stream],
        )
        return out, grad, sent, small

    def go_feed_back(flip, stream, made, up, down, gate):
        return run_feed_back(
            after(core, *gate), flip, down[2], made[3], *up, *mats_of[stream]
        )

    def go_back(stream, made, down, feed, gate):
        return run_back(
            self_plans[stream],
            after(core, *gate),
            [[down[1], feed[0], feed[1]]],
            [made[1]],
            [made[2]],
            low_one[stream],
            [self_mats[stream]],
            gain_all,
            key_bias[stream],
            self_same[stream],
            made[0],
        )

    region_made = go_up(1)
    word_made = go_up(0)
    window = (word_made[2], region_made[2], third.last, fourth.last)
    third.most(*window)
    third.rest(*window)
    fourth.corner(*window)
    word_mats = third.finish([(0, 1), (1, 1)], share)
    mats_of = [word_mats]
    word_up = go_feed(0, word_made, ())
    word_down = go_down(0, word_made, word_up)
    corners = fourth.last
    word_far = go_feed_back(True, 0, word_made, word_up, word_down, (corners,))
    word_ring = Scatter(word_far[1])
    word_own = go_feed_back(False, 0, word_made, word_up, word_down, (word_far[2],))
    word_ring.add(word_own[1], True)
    fourth.most(word_own[2])
    fourth.rest(word_own[2])
    mats_of.append(fourth.finish([(0, 1), (1, 1)], share))
    word_back = go_back(
        0, word_made, word_down, (word_far[0], word_own[0]), (word_ring.last, corners)
    )
    word_ring.side(1)
    word_self_ring = Scatter(word_back[2][0])
    region_up = go_feed(1, region_made, (word_self_ring.last,))
    word_self_ring.add(word_back[1][0], True)
    region_down = go_down(1, region_made, region_up)
    window = (region_down[3], word_ring.raw)
    region_far = go_feed_back(True, 1, region_made, region_up, region_down, (word_ring.raw,))
    word_ring.side(2, *window)
    word_self_ring.side(1, *window)
    region_ring = Scatter(region_far[1])
    region_own = go_feed_back(
        False, 1, region_made, region_up, region_down, (region_far[2],)
    )
    region_ring.add(region_own[1], True)
    region_back = go_back(
        1, region_made, region_down, (region_far[0], region_own[0]), (region_ring.last,)
    )
    window = (region_own[2], word_ring.raw, word_self_ring.raw)
    region_ring.side(1, *window)
    word_self_ring.side(2, *window)
    word_ring.join(word_self_ring)
    word_ring.outer(region_back[3])
    region_self_ring = Scatter(region_back[2][0], region_ring.raw + word_self_ring.raw)
    swapped = region_self_ring.arrived
    region_self_ring.add(region_back[1][0], True)
    units, mine, other, cross_small, pieces = run_back(
        cross_plan,
        after(core, region_self_ring.last),
        [[word_back[0][0]], [region_back[0][0]]],
        unit_one,
        scale_one,
        x_all,
        cross_mats,
        gain_all,
        key_all,
        cross_same,
        cross_kept,
    )
    region_ring.side(2, swapped)
    region_self_ring.side(1)
    cross_ring = Scatter(other[0], region_ring.raw + region_self_ring.raw)
    region_self_ring.side(2, cross_small)
    region_ring.outer(cross_small)
    word_ring.inner(cross_small)
    cross_ring.add(mine[0], True)
    grads_in = run_cross_inputs(
        cross_plan, pieces, cross_mats[0], after(units, cross_ring.last)
    )
    cross_ring.side(1)
    small_gate = (cross_ring.raw, grads_in[0])
    word_shard = word_ring.near(*small_gate)
    region_ring.inner(*small_gate)
    region_self_ring.outer(*small_gate)
    cross_ring.side(2, *small_gate)
    region_self_ring.inner()
    cross_ring.outer()
    cross_ring.inner()
    if staged:
        wide = ffn_w.shape[3] // columns * 2
        parts = [word_shard[at : at + 2] for at in range(0, wide, 2)]
        word_shard, word_self_shard = jnp.concatenate(parts, axis=-1), word_shard[wide:]
    else:
        word_self_shard = word_self_ring.near()
    attn_shard = jnp.stack([cross_ring.near(), word_self_shard, region_self_ring.near()])
    ffn_shard = jnp.stack([word_shard, region_ring.near()])
    outputs = [word_down[0], region_down[0]]
    downs = [word_down[1:], region_down[1:]]
    feeds = [(word_far, word_own), (region_far, region_own)]
    self_small = [word_back[3], region_back[3]]
    grad_lang = grads_in[0].reshape(lang.shape)
    grad_vis = grads_in[1].reshape(vis.shape)

    layers = [after(part, small_gate) for part in (cross_small, self_small[0], self_small[1])]
    gain_rows = [part[0:1] for part in layers] + [part[2][0:1] for part in downs]
    bias_rows = []
    for part in layers:
        bias_rows += [part[3:5], part[2:3]]
    bias_rows += [part[2][2:3] for part in downs]
    bias_rows += [part[1:2] for part in layers] + [part[2][1:2] for part in downs]
    up_rows = []
    for far, own in feeds:
        lines = far[2][0:1], own[2][0:1]
        up_rows.append(
            jnp.where(
                core_index == 0,
                jnp.concatenate([lines[1], lines[0]], axis=1),
                jnp.concatenate([lines[0], lines[1]], axis=1),
            )
        )

    def split(rows, share):
        rows = jnp.concatenate(rows)
        count = rows.shape[0]
        return rows.reshape(count, -1, share).transpose(1, 0, 2).reshape(-1, count * share)

    small_grad = jnp.concatenate(
        [split(gain_rows, model_share), split(bias_rows, model_share), split(up_rows, hidden_share)],
        axis=1,
    )
    small_grad = jnp.pad(small_grad, ((0, 0), (0, padded - small_size)))
    small_sum = scatter_small(small_grad.reshape(small_grad.shape[0], -1, 128)).reshape(-1)
    gains_shard = small_sum[: cuts[0]].reshape(5, model_share)
    biases_shard = small_sum[cuts[0] : cuts[1]].reshape(16, model_share)
    up_shard = small_sum[cuts[1] : small_size].reshape(2, hidden_share)
    squares = jnp.sum(attn_shard * attn_shard) + jnp.sum(ffn_shard * ffn_shard)
    squares = squares + jnp.where(core_index == 0, jnp.sum(small_sum * small_sum), 0.0)
    grad_norm = jnp.sqrt(sum_all(squares))
    clip = jnp.minimum(1.0, clip_norm / (grad_norm + 1e-06))
    attn_new = adam_update(attn_w, attn_m, attn_v, attn_ema, attn_shard, clip, rate_mats)
    ffn_new = adam_update(ffn_w, ffn_m, ffn_v, ffn_ema, ffn_shard, clip, rate_mats)
    gains_new = adam_update(gains, gains_m, gains_v, gains_ema, gains_shard, clip, rate_small)
    biases_new = adam_update(biases, biases_m, biases_v, biases_ema, biases_shard, clip, rate_small)
    up_new = adam_update(bias_up, bias_up_m, bias_up_v, bias_up_ema, up_shard, clip, rate_small)
    return (
        outputs[0],
        outputs[1],
        grad_lang,
        grad_vis,
        grad_norm,
        attn_new[0],
        attn_new[1],
        attn_new[2],
        attn_new[3],
        ffn_new[0],
        ffn_new[1],
        ffn_new[2],
        ffn_new[3],
        gains_new[0],
        gains_new[1],
        gains_new[2],
        gains_new[3],
        biases_new[0],
        biases_new[1],
        biases_new[2],
        biases_new[3],
        up_new[0],
        up_new[1],
        up_new[2],
        up_new[3],
    )


def solution(mesh):
    return jax.shard_map(
        local,
        mesh=mesh,
        in_specs=(
            P(("dp", "mp"), None, None),
            P(("dp", "mp"), None, None),
            P(("dp", "mp"), None),
            P(("dp", "mp")),
            P(("dp", "mp"), None, None),
            P(("dp", "mp"), None, None),
            P(None, None, "dp", "mp"),
            P(None, None, "dp", "mp"),
            P(None, None, "dp", "mp"),
            P(None, None, "dp", "mp"),
            P(None, None, "dp", "mp"),
            P(None, None, "dp", "mp"),
            P(None, None, "dp", "mp"),
            P(None, None, "dp", "mp"),
            P(None, "dp"),
            P(None, "dp"),
            P(None, "dp"),
            P(None, "dp"),
            P(None, "dp"),
            P(None, "dp"),
            P(None, "dp"),
            P(None, "dp"),
            P(None, "dp"),
            P(None, "dp"),
            P(None, "dp"),
            P(None, "dp"),
        ),
        out_specs=(
            P(("dp", "mp"), None, None),
            P(("dp", "mp"), None, None),
            P(("dp", "mp"), None, None),
            P(("dp", "mp"), None, None),
            P(),
            P(None, None, "dp", "mp"),
            P(None, None, "dp", "mp"),
            P(None, None, "dp", "mp"),
            P(None, None, "dp", "mp"),
            P(None, None, "dp", "mp"),
            P(None, None, "dp", "mp"),
            P(None, None, "dp", "mp"),
            P(None, None, "dp", "mp"),
            P(None, "dp"),
            P(None, "dp"),
            P(None, "dp"),
            P(None, "dp"),
            P(None, "dp"),
            P(None, "dp"),
            P(None, "dp"),
            P(None, "dp"),
            P(None, "dp"),
            P(None, "dp"),
            P(None, "dp"),
            P(None, "dp"),
        ),
        check_vma=False,
    )
```
